32 devices in a mesh: tm: 8 (over z, x), mode: 4 (over y, core).
Axes of the slice: x: 2, y: 2, z: 4, core: 2. Of those that a mesh axis runs over, the one named last changes fastest.
Arguments:
- observations: bfloat16 [512, 2048], P('tm', 'mode'), may hold values from -6 to 6
- basis: bfloat16 [2048, 2048], P(None, 'mode'), may hold values from -0.125 to 0.125
- eigvals: float32 [2048], P('mode'), may hold values from 0.05 to 4
- lengths: float32 [2048], P('mode'), may hold values from 8 to 2048
- noise: float32 [1], replicated, may hold values from 0.3 to 1
Outputs:
- grad_obs: float32 [512, 2048], P('tm', 'mode')
The draws below stay inside these ranges and needn't reach their ends.
All inputs are finite; a program needn't handle non-finite values.
Results may differ from the reference program's by a relative error of at most 0.0024.
Values may be sent and summed in bfloat16 or wider, within the bound.
No kernel may reach another device: no remote copies, remote signals or barrier semaphores. Data moves between devices by JAX's collectives and lax.ppermute only.
A program may use at most 64 MiB of HBM per device.

```python
import math
import jax
import jax.numpy as jnp
from jax import lax

S = 2048
STEPS = 512
N_MODE = 4


def slow_signal(key, shortest, amplitude):
    subkeys = jax.random.split(key, 3)
    number = 6
    longest = max(shortest + 1, 2 * STEPS)
    periods = jax.random.randint(subkeys[0], (number,), shortest, longest)
    shifts = jax.random.randint(subkeys[1], (number,), 0, longest)
    loadings = jax.random.normal(subkeys[2], (number, S), jnp.float32) / math.sqrt(number)
    hour_rows = lax.broadcasted_iota(jnp.int32, (STEPS, 1), 0)
    signal = jnp.zeros((STEPS, S), jnp.float32)
    for member in range(number):
        phase_steps = (hour_rows + shifts[member]) % periods[member]
        angles = 2.0 * math.pi / periods[member].astype(jnp.float32) * phase_steps.astype(jnp.float32)
        signal = signal + jnp.sin(angles) * loadings[member][None, :]
    return amplitude * signal


def draw_observations(key, part):
    key = jax.random.fold_in(key, 11)
    subkeys = jax.random.split(key, 3)
    rough = jax.random.normal(subkeys[1], (STEPS, S), jnp.float32)
    offsets = jax.random.normal(subkeys[2], (1, S), jnp.float32)
    signal = slow_signal(jax.random.fold_in(key, 5), 30, 1.5)
    return jnp.clip(rough + offsets + signal, -6.0, 6.0).astype(jnp.bfloat16)


def shard_levels(key, extent, pieces, least, largest):
    level, own = 1.0, jax.random.fold_in(key, 6)
    for dim, blocks in pieces:
        heights = jnp.exp(jax.random.uniform(jax.random.fold_in(own, dim), (blocks,), jnp.float32, least / len(pieces), largest / len(pieces)))
        level = level * jnp.repeat(heights, extent[dim] // blocks).reshape([-1 if axis == dim else 1 for axis in range(len(extent))])
    return level


def normal_values(stream_key, dims, scale, most, pieces=(), kind=jnp.bfloat16):
    level = shard_levels(stream_key, dims, pieces, -0.22, 0.18) if pieces else 1.0
    result = jax.random.normal(stream_key, dims, jnp.float32) * scale * level
    return jnp.minimum(jnp.maximum(result, -most), most).astype(kind)


def setup_inputs(seed: int = 0) -> dict:
    splits = jax.random.split(jax.random.key(seed), 6)
    return {
        "observations": draw_observations(jax.random.fold_in(splits[5], 71), 0),
        "basis": normal_values(splits[1], (S, S), S ** -0.5, 0.125, ((1, 4),)),
        "eigvals": jnp.clip(jnp.exp(math.log(4.0) - 4.3820266 * jax.random.uniform(splits[2], (S,), jnp.float32) ** shard_levels(splits[2], (S,), ((0, 4),), -0.2, 0.2)), 0.05, 4.0),
        "lengths": jnp.clip(jnp.exp(math.log(2048.0) - 5.5451774 * jax.random.uniform(splits[3], (S,), jnp.float32) ** shard_levels(splits[3], (S,), ((0, 4),), -0.2, 0.2)), 8.0, 2048.0),
        "noise": jnp.clip(jax.random.uniform(splits[4], (1,), jnp.float32, 0.3, 1.0), 0.3, 1.0),
    }


def mat_mul(p, q):
    return (p[0] * q[0] + p[1] * q[2], p[0] * q[1] + p[1] * q[3], p[2] * q[0] + p[3] * q[2], p[2] * q[1] + p[3] * q[3])

def mat_trans(p):
    return (p[0], p[2], p[1], p[3])

def mat_add(p, q):
    return tuple((a + b for a, b in zip(p, q)))

def mat_vec(p, v):
    return (p[0] * v[0] + p[1] * v[1], p[2] * v[0] + p[3] * v[1])

def mat_inverse(p):
    determ = p[0] * p[3] - p[1] * p[2]
    return (p[3] / determ, -p[1] / determ, -p[2] / determ, p[0] / determ)

def lower_third(value, fall):
    series = 1.0 / 604800.0
    for factor in (60480.0, 6720.0, 840.0, 120.0, 20.0, 4.0, 1.0):
        series = series * value + 1.0 / factor
    return fall * value * value * value / 6.0 * series

def model_terms(scale2, length):
    lam = math.sqrt(3.0) / length
    decay = jnp.exp(-lam)
    trans = (decay * (1.0 + lam), decay, -decay * lam * lam, decay * (1.0 - lam))
    twice = 2.0 * lam
    fall = jnp.exp(-twice)
    lower = lower_third(twice, fall)
    cross = 2.0 * scale2 * lam * lam * lam * fall
    qnoise = (scale2 * lower, cross, cross, lam * lam * scale2 * (lower + twice * fall))
    return (trans, qnoise, lam * lam * scale2)

def smooth_block(values, scale2, length, noise_var):
    trans, qnoise, prior_dd = model_terms(scale2, length)
    zero = jnp.zeros_like(scale2)

    def update(mean_pred, cov_pred, obs):
        inn = cov_pred[0] + noise_var
        gain0 = cov_pred[0] / inn
        gain1 = cov_pred[2] / inn
        err = obs - mean_pred[0]
        mean = (mean_pred[0] + gain0 * err, mean_pred[1] + gain1 * err)
        cov = (cov_pred[0] - gain0 * gain0 * inn, cov_pred[1] - gain0 * gain1 * inn, cov_pred[2] - gain1 * gain0 * inn, cov_pred[3] - gain1 * gain1 * inn)
        return (mean, cov)
    start_mean, start_cov = update((zero, zero), (scale2, zero, zero, prior_dd), values[0])

    def forward(carry, obs):
        mean, cov = carry
        mean_pred = mat_vec(trans, mean)
        cov_pred = mat_add(mat_mul(mat_mul(trans, cov), mat_trans(trans)), qnoise)
        new = update(mean_pred, cov_pred, obs)
        return (new, new)
    last, (means, covs) = lax.scan(forward, (start_mean, start_cov), values[1:])
    means = tuple((jnp.concatenate([s[None], m], axis=0) for s, m in zip(start_mean, means)))
    covs = tuple((jnp.concatenate([s[None], c], axis=0) for s, c in zip(start_cov, covs)))

    def backward(carry, item):
        mean, cov = item
        pred = mat_add(mat_mul(mat_mul(trans, cov), mat_trans(trans)), qnoise)
        gain = mat_mul(mat_mul(cov, mat_trans(trans)), mat_inverse(pred))
        moved = mat_vec(trans, mean)
        delta = (carry[0] - moved[0], carry[1] - moved[1])
        corr = mat_vec(gain, delta)
        new = (mean[0] + corr[0], mean[1] + corr[1])
        return (new, new[0])
    ends = (means[0][-1], means[1][-1])
    early = (tuple((m[:-1] for m in means)), tuple((c[:-1] for c in covs)))
    final, firsts = lax.scan(backward, ends, early, reverse=True)
    smoothed = jnp.concatenate([firsts, ends[0][None]], axis=0)
    return -(values - smoothed) / noise_var

def reference(observations, basis, eigvals, lengths, noise):
    rotated = jnp.dot(observations.astype(jnp.float32), basis.astype(jnp.float32), precision=lax.Precision.HIGHEST, preferred_element_type=jnp.float32)
    width = S // N_MODE
    zblocks = rotated.reshape(STEPS, N_MODE, width).transpose(1, 0, 2)
    sblocks = eigvals.reshape(N_MODE, width)
    lblocks = lengths.reshape(N_MODE, width)
    noise_var = noise[0]
    rblocks = lax.map(lambda item: smooth_block(item[0], item[1], item[2], noise_var), (zblocks, sblocks, lblocks))
    residual = rblocks.transpose(1, 0, 2).reshape(STEPS, S).astype(jnp.bfloat16)
    return jnp.dot(residual.astype(jnp.float32), basis.astype(jnp.float32).T, precision=lax.Precision.HIGHEST, preferred_element_type=jnp.float32)
```

```python
import functools
import math

import jax
import jax.numpy as jnp
from jax import lax
from jax.experimental import pallas as pl
from jax.experimental.pallas import tpu as pltpu
from jax.sharding import PartitionSpec as P

F32 = jnp.float32
SUB = 8
VMEM_LIMIT = 24 * 1024 * 1024


def mat_mul(p, q):
    return (
        p[0] * q[0] + p[1] * q[2],
        p[0] * q[1] + p[1] * q[3],
        p[2] * q[0] + p[3] * q[2],
        p[2] * q[1] + p[3] * q[3],
    )


def mat_trans(p):
    return (p[0], p[2], p[1], p[3])


def mat_add(p, q):
    return tuple(a + b for a, b in zip(p, q))


def mat_sub(p, q):
    return tuple(a - b for a, b in zip(p, q))


def mat_pick(flag, p, q):
    return tuple(jnp.where(flag, a, b) for a, b in zip(p, q))


def full(s):
    return (s[0], s[1], s[1], s[2])


def congruence(s, f):
    t = (
        s[0] * f[0] + s[1] * f[2],
        s[0] * f[1] + s[1] * f[3],
        s[1] * f[0] + s[2] * f[2],
        s[1] * f[1] + s[2] * f[3],
    )
    return (f[0] * t[0] + f[2] * t[2], f[0] * t[1] + f[2] * t[3], f[1] * t[1] + f[3] * t[3])


def power(squares, exponent, like):
    one, zero = jnp.ones_like(like), jnp.zeros_like(like)
    out = None
    for bit, base in enumerate(squares):
        flag = (exponent & (1 << bit)) != 0
        if out is None:
            out = mat_pick(flag, base, (one, zero, zero, one))
        else:
            out = mat_pick(flag, mat_mul(out, base), out)
    return out


def gramian(squares, grams, count, like):
    zero = jnp.zeros_like(like)
    out = (zero, zero, zero)
    for bit, (base, gram) in enumerate(zip(squares, grams)):
        flag = (count & (1 << bit)) != 0
        out = mat_pick(flag, mat_add(gram, congruence(out, base)), out)
    return out


def steady_state(scale2, length, noise_var):
    lam = math.sqrt(3.0) / length
    decay = jnp.exp(-lam)
    twice = 2.0 * lam
    fall = jnp.exp(-twice)
    rho = scale2 / noise_var
    series = 1.0 / 604800.0
    for factor in (60480.0, 6720.0, 840.0, 120.0, 20.0, 4.0, 1.0):
        series = series * twice + 1.0 / factor
    lower = fall * twice * twice * twice * (1.0 / 6.0) * series
    loss = 1.0
    for order in (8, 7, 6, 5, 4, 3, 2):
        loss = 1.0 - lam * (1.0 / order) * loss
    loss = lam * loss
    q00 = rho * lower
    q01 = 2.0 * rho * lam * lam * fall
    q11 = rho * (lower + twice * fall)
    slope = decay * lam
    tilt = loss + slope
    g0 = q00 * tilt * tilt + 2.0 * slope * q01 * tilt + slope * slope * q11
    g1 = slope * q01 - decay * (1.0 - lam) * q00
    loss2 = loss * loss
    c2 = decay * decay
    u = (2.0 * decay * loss2 - g1) / c2
    v = (loss2 * loss2 + g0) / c2
    root = jnp.sqrt(v * (v + 4.0 * u + 16.0))
    product = 4.0 * v / (v + root + jnp.sqrt(2.0 * v * (v + 2.0 * u + root)))
    total = 0.5 * (jnp.sqrt(u * u + 4.0 * u - 2.0 * v + 2.0 * root) - u)
    gain0 = total - 2.0 * loss
    gain1 = (product - loss2 - gain0 * tilt) / slope
    inverse = (1.0 - total + product) / c2
    inn = c2 / (1.0 - total + product)
    closed = (1.0 + slope - loss - gain0, slope, -slope - gain1, decay * (1.0 - lam))
    p00 = inn * ((1.0 - lam) * gain0 - lam * gain1) / decay
    p01 = inn * (lam * gain0 + (1.0 + lam) * gain1) / decay
    p11 = (
        p01 * (loss * (1.0 + decay) + 2.0 * slope * slope)
        + slope * decay * (1.0 + lam) * p00
        - q01
        + gain0 * gain1 * inn
    ) / (slope * decay * (1.0 - lam))
    return closed, gain0, gain1, inverse, (rho - p00, -p01, rho - p11)


def coefficients_kernel(blocks, me_ref, noise_ref, scale_ref, length_ref, const_ref, w_ref, g_ref):
    steps = w_ref.shape[1]
    width = scale_ref.shape[1]
    tile = (SUB, width)
    me = me_ref[0]
    scale2 = jnp.broadcast_to(scale_ref[...], tile)
    length = jnp.broadcast_to(length_ref[...], tile)
    noise_var = jnp.full(tile, noise_ref[0], F32)
    closed, gain0, gain1, inverse, excess = steady_state(scale2, length, noise_var)
    zero = jnp.zeros(tile, F32)

    squares, grams = [closed], [(inverse, zero, zero)]
    doublings = (steps * blocks).bit_length() - 1
    for _ in range(doublings):
        base = squares[-1]
        grams.append(mat_add(grams[-1], congruence(grams[-1], base)))
        squares.append(mat_mul(base, base))
    local = steps.bit_length() - 1
    consts = closed + (gain0, gain1, inverse) + squares[3] + squares[4] + squares[5]
    for place, value in enumerate(consts):
        const_ref[place] = value
    const_ref[len(consts)] = -1.0 / noise_var

    row = lax.broadcasted_iota(jnp.int32, tile, 0)
    small, gram_small = squares[:3], grams[:3]
    behind = power(small, 7 - row, zero)
    gram = gramian(small, gram_small, 7 - row, zero)
    eight, gram_eight = squares[3], grams[3]
    parts = steps // SUB
    for part in range(parts - 1, -1, -1):
        rows = pl.ds(part * SUB, SUB)
        w_ref[0, rows, :] = behind[0] * gain0 + behind[1] * gain1
        w_ref[1, rows, :] = behind[2] * gain0 + behind[3] * gain1
        k0 = gain0 * gram[0] + gain1 * gram[1]
        k1 = gain0 * gram[1] + gain1 * gram[2]
        w_ref[2, rows, :] = inverse - (k0 * closed[0] + k1 * closed[2])
        w_ref[3, rows, :] = -(k0 * closed[1] + k1 * closed[3])
        if part:
            behind = mat_mul(behind, eight)
            gram = mat_add(gram_eight, congruence(gram, eight))
    ahead = power(small, row, zero)
    for part in range(parts):
        rows = pl.ds(part * SUB, SUB)
        u0, u1 = w_ref[2, rows, :], w_ref[3, rows, :]
        w_ref[2, rows, :] = u0 * ahead[0] + u1 * ahead[2]
        w_ref[3, rows, :] = u0 * ahead[1] + u1 * ahead[3]
        if part < parts - 1:
            ahead = mat_mul(ahead, eight)

    s = grams[-1]
    left = (
        1.0 + excess[0] * s[0] + excess[1] * s[1],
        excess[0] * s[1] + excess[1] * s[2],
        excess[1] * s[0] + excess[2] * s[1],
        1.0 + excess[1] * s[1] + excess[2] * s[2],
    )
    determ = 1.0 / (left[0] * left[3] - left[1] * left[2])
    start = mat_mul((left[3], -left[1], -left[2], left[0]), full(excess))
    start = tuple(x * determ for x in start)
    block_squares, block_grams = squares[local:-1], grams[local:-1]
    mine = jnp.full(tile, me, jnp.int32)
    to_me = power(block_squares, mine, zero)
    rest = full(gramian(block_squares, block_grams, blocks - 1 - mine, zero))
    to_state = mat_mul(to_me, start)
    to_adjoint = mat_mul(mat_mul(rest, mat_mul(to_me, block_squares[0])), start)
    for group in range(4 * blocks // SUB):
        rows = row + group * SUB
        kind = rows & 3
        other = (rows >> 2) ^ me
        gap = jnp.abs(other - me)
        near = power(block_squares, jnp.maximum(gap - 1, 0), zero)
        same = other == me
        one = jnp.ones_like(zero)
        far = mat_pick(same, (one, zero, zero, one), mat_mul(near, block_squares[0]))
        origin = mat_trans(power(block_squares, other, zero))
        left_over = full(gramian(block_squares, block_grams, blocks - 1 - other, zero))
        first = mat_mul(mat_mul(origin, mat_trans(block_squares[0])), left_over)
        before = other < me
        after = other > me
        state_b = mat_sub(mat_pick(before, near, (zero,) * 4), mat_mul(to_state, first))
        state_l = mat_mul(to_state, origin)
        cross = mat_pick(after, mat_mul(mat_trans(far), left_over), mat_mul(rest, far))
        adjoint_b = mat_sub(mat_mul(to_adjoint, first), cross)
        adjoint_l = mat_sub(
            mat_pick(after, mat_trans(near), (zero,) * 4), mat_mul(to_adjoint, origin)
        )
        place = pl.ds(group * SUB, SUB)
        for line, (from_b, from_l) in enumerate(
            ((adjoint_b[:2], adjoint_l[:2]), (adjoint_b[2:], adjoint_l[2:]),
             (state_b[:2], state_l[:2]), (state_b[2:], state_l[2:]))
        ):
            g_ref[line, place, :] = jnp.where(
                kind < 2,
                jnp.where(kind == 0, from_b[0], from_b[1]),
                jnp.where(kind == 2, from_l[0], from_l[1]),
            )


def rotate_kernel(pieces, place_ref, *refs):
    obs_refs = refs[:pieces]
    basis_ref, w_ref, z_ref, sum_ref = refs[pieces:]
    depth = obs_refs[0].shape[1]
    z = None
    for piece, obs_ref in enumerate(obs_refs):
        begin = pl.multiple_of((place_ref[0] ^ piece) * depth, depth)
        term = jnp.dot(
            obs_ref[...], basis_ref[pl.ds(begin, depth), :], preferred_element_type=F32
        )
        z = term if z is None else z + term
    z_ref[...] = z
    for line in range(4):
        sum_ref[line : line + 1, :] = jnp.sum(w_ref[line] * z, axis=0, keepdims=True)


def shift(value, by):
    rows = value.shape[0]
    row = lax.broadcasted_iota(jnp.int32, value.shape, 0)
    keep = row >= by if by > 0 else row < rows + by
    return jnp.where(keep, pltpu.roll(value, by % rows, 0), 0.0)


def local_kernel(z_ref, const_ref, r_ref, scratch):
    steps, width = z_ref.shape
    span = steps // SUB
    lanes = 128
    for chunk in range(width // lanes):
        cols = pl.ds(chunk * lanes, lanes)
        scratch[chunk] = z_ref[:, cols]
    for chunk in range(width // lanes):
        cols = pl.ds(chunk * lanes, lanes)
        const = [const_ref[k, :, cols] for k in range(19)]
        f, (k0, k1, inverse) = const[0:4], const[4:7]
        jumps = (const[7:11], const[11:15], const[15:19])
        zero = jnp.zeros((SUB, lanes), F32)
        x0, x1 = zero, zero
        vs = []
        for t in range(span):
            z = scratch[chunk, pl.ds(t, SUB, stride=span), :]
            vs.append(z - x0)
            x0, x1 = f[0] * x0 + f[1] * x1 + k0 * z, f[2] * x0 + f[3] * x1 + k1 * z
        for level, jump in enumerate(jumps):
            s0, s1 = shift(x0, 1 << level), shift(x1, 1 << level)
            x0, x1 = x0 + jump[0] * s0 + jump[1] * s1, x1 + jump[2] * s0 + jump[3] * s1
        x0, x1 = shift(x0, 1), shift(x1, 1)
        for t in range(span):
            vs[t] = (vs[t] - x0) * inverse
            x0, x1 = f[0] * x0 + f[1] * x1, f[2] * x0 + f[3] * x1
        a0, a1 = zero, zero
        for t in range(span - 1, -1, -1):
            a0, a1 = f[0] * a0 + f[2] * a1 + vs[t], f[1] * a0 + f[3] * a1
        for level, jump in enumerate(jumps):
            s0, s1 = shift(a0, -(1 << level)), shift(a1, -(1 << level))
            a0, a1 = a0 + jump[0] * s0 + jump[2] * s1, a1 + jump[1] * s0 + jump[3] * s1
        a0, a1 = shift(a0, -1), shift(a1, -1)
        for t in range(span - 1, -1, -1):
            r = vs[t] - k0 * a0 - k1 * a1
            a0, a1 = f[0] * a0 + f[2] * a1 + vs[t], f[1] * a0 + f[3] * a1
            scratch[chunk, pl.ds(t, SUB, stride=span), :] = r
        r_ref[:, cols] = scratch[chunk]


def finish_kernel(blocks, pieces, place_ref, r_ref, w_ref, g_ref, const_ref, basis_ref, *refs):
    sums = refs[:blocks]
    outs = refs[blocks:]
    depth = outs[0].shape[1]
    value = r_ref[...]
    for line in range(4):
        total = None
        for block in range(blocks):
            term = g_ref[line, pl.ds(4 * block, 4), :] * sums[block][...]
            total = term if total is None else total + term
        value = value - w_ref[line] * jnp.sum(total, axis=0, keepdims=True)
    scale = const_ref[19, 0:1, :]
    residual = (value * scale).astype(jnp.bfloat16)
    for piece in range(pieces - 1, -1, -1):
        begin = pl.multiple_of((place_ref[0] ^ piece) * depth, depth)
        outs[piece][...] = lax.dot_general(
            residual,
            basis_ref[pl.ds(begin, depth), :],
            (((1,), (1,)), ((), ())),
            preferred_element_type=F32,
        )


def exchange(value, axis, count):
    out = [value]
    for step in range(1, count):
        out.append(lax.ppermute(value, axis, [(a, a ^ step) for a in range(count)]))
    return out


def shards(observations, basis, eigvals, lengths, noise):
    steps, depth = observations.shape
    width = basis.shape[1]
    blocks, pieces = lax.axis_size("tm"), lax.axis_size("mode")
    me = lax.axis_index("tm").astype(jnp.int32).reshape(1)
    place = lax.axis_index("mode").astype(jnp.int32).reshape(1)
    vmem = pl.BlockSpec(memory_space=pltpu.VMEM)
    smem = pl.BlockSpec(memory_space=pltpu.SMEM)
    params = pltpu.CompilerParams(vmem_limit_bytes=VMEM_LIMIT)

    def shape(*dims, dtype=F32):
        return jax.ShapeDtypeStruct(dims, dtype)

    obs = exchange(observations, "mode", pieces)
    const, w, g = pl.pallas_call(
        functools.partial(coefficients_kernel, blocks),
        out_shape=(shape(20, SUB, width), shape(4, steps, width), shape(4, 4 * blocks, width)),
        in_specs=[smem, smem, vmem, vmem],
        out_specs=(vmem,) * 3,
        compiler_params=params,
        cost_estimate=pl.CostEstimate(flops=20000000, bytes_accessed=2000000, transcendentals=0),
        name="coefficients",
    )(me, noise, eigvals.reshape(1, width), lengths.reshape(1, width))
    z, summary = pl.pallas_call(
        functools.partial(rotate_kernel, pieces),
        out_shape=(shape(steps, width), shape(4, width)),
        in_specs=[smem] + [vmem] * (pieces + 2),
        out_specs=(vmem,) * 2,
        compiler_params=params,
        name="rotate",
    )(place, *obs, basis, w)
    if blocks <= 8:
        sums = exchange(summary, "tm", blocks)
    else:
        gathered = lax.all_gather(summary, "tm")
        sums = [gathered[me[0] ^ block] for block in range(blocks)]
    local = pl.pallas_call(
        local_kernel,
        out_shape=shape(steps, width),
        in_specs=[vmem] * 2,
        out_specs=vmem,
        scratch_shapes=[pltpu.VMEM((width // 128, steps, 128), F32)],
        compiler_params=params,
        cost_estimate=pl.CostEstimate(flops=10000000, bytes_accessed=1000000, transcendentals=0),
        name="local",
    )(z, const)
    parts = pl.pallas_call(
        functools.partial(finish_kernel, blocks, pieces),
        out_shape=(shape(steps, depth),) * pieces,
        in_specs=[smem] + [vmem] * (5 + blocks),
        out_specs=(vmem,) * pieces,
        compiler_params=params,
        name="finish",
    )(place, local, w, g, const, basis, *sums)
    grad_obs = parts[0]
    for step in range(1, pieces):
        grad_obs = grad_obs + lax.ppermute(
            parts[step], "mode", [(a, a ^ step) for a in range(pieces)]
        )
    return grad_obs


def solution(mesh):
    placed = (P("tm", "mode"), P(None, "mode"), P("mode"), P("mode"), P())
    return jax.shard_map(
        shards, mesh=mesh, in_specs=placed, out_specs=P("tm", "mode"), check_vma=False
    )
```

```python
import functools
import math

import jax
import jax.numpy as jnp
from jax import lax
from jax.experimental import pallas as pl
from jax.experimental.pallas import tpu as pltpu
from jax.sharding import PartitionSpec as P

F32 = jnp.float32
SUB = 8
VMEM_LIMIT = 24 * 1024 * 1024


def mat_mul(p, q):
    return (
        p[0] * q[0] + p[1] * q[2],
        p[0] * q[1] + p[1] * q[3],
        p[2] * q[0] + p[3] * q[2],
        p[2] * q[1] + p[3] * q[3],
    )


def mat_trans(p):
    return (p[0], p[2], p[1], p[3])


def mat_add(p, q):
    return tuple(a + b for a, b in zip(p, q))


def mat_sub(p, q):
    return tuple(a - b for a, b in zip(p, q))


def mat_pick(flag, p, q):
    return tuple(jnp.where(flag, a, b) for a, b in zip(p, q))


def full(s):
    return (s[0], s[1], s[1], s[2])


def congruence(s, f):
    t = (
        s[0] * f[0] + s[1] * f[2],
        s[0] * f[1] + s[1] * f[3],
        s[1] * f[0] + s[2] * f[2],
        s[1] * f[1] + s[2] * f[3],
    )
    return (f[0] * t[0] + f[2] * t[2], f[0] * t[1] + f[2] * t[3], f[1] * t[1] + f[3] * t[3])


def power(squares, exponent, like):
    one, zero = jnp.ones_like(like), jnp.zeros_like(like)
    out = None
    for bit, base in enumerate(squares):
        flag = (exponent & (1 << bit)) != 0
        if out is None:
            out = mat_pick(flag, base, (one, zero, zero, one))
        else:
            out = mat_pick(flag, mat_mul(out, base), out)
    return out


def gramian(squares, grams, count, like):
    zero = jnp.zeros_like(like)
    out = (zero, zero, zero)
    for bit, (base, gram) in enumerate(zip(squares, grams)):
        flag = (count & (1 << bit)) != 0
        out = mat_pick(flag, mat_add(gram, congruence(out, base)), out)
    return out


def steady_state(scale2, length, noise_var):
    lam = math.sqrt(3.0) / length
    decay = jnp.exp(-lam)
    twice = 2.0 * lam
    fall = jnp.exp(-twice)
    rho = scale2 / noise_var
    series = 1.0 / 604800.0
    for factor in (60480.0, 6720.0, 840.0, 120.0, 20.0, 4.0, 1.0):
        series = series * twice + 1.0 / factor
    lower = fall * twice * twice * twice * (1.0 / 6.0) * series
    loss = 1.0
    for order in (8, 7, 6, 5, 4, 3, 2):
        loss = 1.0 - lam * (1.0 / order) * loss
    loss = lam * loss
    q00 = rho * lower
    q01 = 2.0 * rho * lam * lam * fall
    q11 = rho * (lower + twice * fall)
    slope = decay * lam
    tilt = loss + slope
    g0 = q00 * tilt * tilt + 2.0 * slope * q01 * tilt + slope * slope * q11
    g1 = slope * q01 - decay * (1.0 - lam) * q00
    loss2 = loss * loss
    c2 = decay * decay
    u = (2.0 * decay * loss2 - g1) / c2
    v = (loss2 * loss2 + g0) / c2
    root = jnp.sqrt(v * (v + 4.0 * u + 16.0))
    product = 4.0 * v / (v + root + jnp.sqrt(2.0 * v * (v + 2.0 * u + root)))
    total = 0.5 * (jnp.sqrt(u * u + 4.0 * u - 2.0 * v + 2.0 * root) - u)
    gain0 = total - 2.0 * loss
    gain1 = (product - loss2 - gain0 * tilt) / slope
    inverse = (1.0 - total + product) / c2
    inn = c2 / (1.0 - total + product)
    closed = (1.0 + slope - loss - gain0, slope, -slope - gain1, decay * (1.0 - lam))
    p00 = inn * ((1.0 - lam) * gain0 - lam * gain1) / decay
    p01 = inn * (lam * gain0 + (1.0 + lam) * gain1) / decay
    p11 = (
        p01 * (loss * (1.0 + decay) + 2.0 * slope * slope)
        + slope * decay * (1.0 + lam) * p00
        - q01
        + gain0 * gain1 * inn
    ) / (slope * decay * (1.0 - lam))
    return closed, gain0, gain1, inverse, (rho - p00, -p01, rho - p11)


def coefficients_kernel(blocks, me_ref, *refs):
    arguments, (const_ref, w_ref, g_ref, basis_ref, obs_ref) = refs[:5], refs[5:10]
    noise_ref, scale_ref, length_ref, sems = refs[10:]
    copies = [
        pltpu.make_async_copy(source, target, sems.at[k])
        for k, (source, target) in enumerate(
            zip(arguments, (noise_ref, scale_ref, length_ref, obs_ref, basis_ref))
        )
    ]
    for copy in copies:
        copy.start()
    for copy in copies[:3]:
        copy.wait()
    steps = w_ref.shape[1]
    width = scale_ref.shape[1]
    tile = (SUB, width)
    me = me_ref[0]
    scale2 = jnp.broadcast_to(scale_ref[...], tile)
    length = jnp.broadcast_to(length_ref[...], tile)
    noise_var = jnp.full(tile, noise_ref[0], F32)
    closed, gain0, gain1, inverse, excess = steady_state(scale2, length, noise_var)
    zero = jnp.zeros(tile, F32)

    squares, grams = [closed], [(inverse, zero, zero)]
    doublings = (steps * blocks).bit_length() - 1
    for _ in range(doublings):
        base = squares[-1]
        grams.append(mat_add(grams[-1], congruence(grams[-1], base)))
        squares.append(mat_mul(base, base))
    local = steps.bit_length() - 1
    consts = closed + (gain0, gain1, inverse) + squares[3] + squares[4] + squares[5]
    for place, value in enumerate(consts):
        const_ref[place] = value
    const_ref[len(consts)] = -1.0 / noise_var

    row = lax.broadcasted_iota(jnp.int32, tile, 0)
    small, gram_small = squares[:3], grams[:3]
    behind = power(small, 7 - row, zero)
    gram = gramian(small, gram_small, 7 - row, zero)
    eight, gram_eight = squares[3], grams[3]
    parts = steps // SUB
    for part in range(parts - 1, -1, -1):
        rows = pl.ds(part * SUB, SUB)
        w_ref[0, rows, :] = behind[0] * gain0 + behind[1] * gain1
        w_ref[1, rows, :] = behind[2] * gain0 + behind[3] * gain1
        k0 = gain0 * gram[0] + gain1 * gram[1]
        k1 = gain0 * gram[1] + gain1 * gram[2]
        w_ref[2, rows, :] = inverse - (k0 * closed[0] + k1 * closed[2])
        w_ref[3, rows, :] = -(k0 * closed[1] + k1 * closed[3])
        if part:
            behind = mat_mul(behind, eight)
            gram = mat_add(gram_eight, congruence(gram, eight))
    ahead = power(small, row, zero)
    for part in range(parts):
        rows = pl.ds(part * SUB, SUB)
        u0, u1 = w_ref[2, rows, :], w_ref[3, rows, :]
        w_ref[2, rows, :] = u0 * ahead[0] + u1 * ahead[2]
        w_ref[3, rows, :] = u0 * ahead[1] + u1 * ahead[3]
        if part < parts - 1:
            ahead = mat_mul(ahead, eight)

    s = grams[-1]
    left = (
        1.0 + excess[0] * s[0] + excess[1] * s[1],
        excess[0] * s[1] + excess[1] * s[2],
        excess[1] * s[0] + excess[2] * s[1],
        1.0 + excess[1] * s[1] + excess[2] * s[2],
    )
    determ = 1.0 / (left[0] * left[3] - left[1] * left[2])
    start = mat_mul((left[3], -left[1], -left[2], left[0]), full(excess))
    start = tuple(x * determ for x in start)
    block_squares, block_grams = squares[local:-1], grams[local:-1]
    mine = jnp.full(tile, me, jnp.int32)
    to_me = power(block_squares, mine, zero)
    rest = full(gramian(block_squares, block_grams, blocks - 1 - mine, zero))
    to_state = mat_mul(to_me, start)
    to_adjoint = mat_mul(mat_mul(rest, mat_mul(to_me, block_squares[0])), start)
    for group in range(4 * blocks // SUB):
        rows = row + group * SUB
        kind = rows & 3
        other = rows >> 2
        gap = jnp.abs(other - me)
        near = power(block_squares, jnp.maximum(gap - 1, 0), zero)
        same = other == me
        one = jnp.ones_like(zero)
        far = mat_pick(same, (one, zero, zero, one), mat_mul(near, block_squares[0]))
        origin = mat_trans(power(block_squares, other, zero))
        left_over = full(gramian(block_squares, block_grams, blocks - 1 - other, zero))
        first = mat_mul(mat_mul(origin, mat_trans(block_squares[0])), left_over)
        before = other < me
        after = other > me
        state_b = mat_sub(mat_pick(before, near, (zero,) * 4), mat_mul(to_state, first))
        state_l = mat_mul(to_state, origin)
        cross = mat_pick(after, mat_mul(mat_trans(far), left_over), mat_mul(rest, far))
        adjoint_b = mat_sub(mat_mul(to_adjoint, first), cross)
        adjoint_l = mat_sub(
            mat_pick(after, mat_trans(near), (zero,) * 4), mat_mul(to_adjoint, origin)
        )
        place = pl.ds(group * SUB, SUB)
        for line, (from_b, from_l) in enumerate(
            ((adjoint_b[:2], adjoint_l[:2]), (adjoint_b[2:], adjoint_l[2:]),
             (state_b[:2], state_l[:2]), (state_b[2:], state_l[2:]))
        ):
            g_ref[line, place, :] = jnp.where(
                kind < 2,
                jnp.where(kind == 0, from_b[0], from_b[1]),
                jnp.where(kind == 2, from_l[0], from_l[1]),
            )
    for copy in copies[3:]:
        copy.wait()


def rotate_kernel(pieces, place_ref, *refs):
    obs_refs = refs[:pieces]
    basis_ref, w_ref, z_ref, sum_ref = refs[pieces:]
    depth = obs_refs[0].shape[1]
    z = None
    for piece, obs_ref in enumerate(obs_refs):
        begin = pl.multiple_of((place_ref[0] ^ piece) * depth, depth)
        term = jnp.dot(
            obs_ref[...], basis_ref[pl.ds(begin, depth), :], preferred_element_type=F32
        )
        z = term if z is None else z + term
    z_ref[...] = z
    for line in range(4):
        summary = jnp.sum(w_ref[line] * z, axis=0, keepdims=True)
        for block in range(sum_ref.shape[0]):
            sum_ref[block, line : line + 1, :] = summary


def shift(value, by):
    rows = value.shape[0]
    row = lax.broadcasted_iota(jnp.int32, value.shape, 0)
    keep = row >= by if by > 0 else row < rows + by
    return jnp.where(keep, pltpu.roll(value, by % rows, 0), 0.0)


def local_kernel(z_ref, const_ref, r_ref, scratch):
    steps, width = z_ref.shape
    span = steps // SUB
    lanes = 128
    for chunk in range(width // lanes):
        cols = pl.ds(chunk * lanes, lanes)
        scratch[chunk] = z_ref[:, cols]
    for chunk in range(width // lanes):
        cols = pl.ds(chunk * lanes, lanes)
        const = [const_ref[k, :, cols] for k in range(19)]
        f, (k0, k1, inverse) = const[0:4], const[4:7]
        jumps = (const[7:11], const[11:15], const[15:19])
        zero = jnp.zeros((SUB, lanes), F32)
        x0, x1 = zero, zero
        vs = []
        for t in range(span):
            z = scratch[chunk, pl.ds(t, SUB, stride=span), :]
            vs.append(z - x0)
            x0, x1 = f[0] * x0 + f[1] * x1 + k0 * z, f[2] * x0 + f[3] * x1 + k1 * z
        for level, jump in enumerate(jumps):
            s0, s1 = shift(x0, 1 << level), shift(x1, 1 << level)
            x0, x1 = x0 + jump[0] * s0 + jump[1] * s1, x1 + jump[2] * s0 + jump[3] * s1
        x0, x1 = shift(x0, 1), shift(x1, 1)
        for t in range(span):
            vs[t] = (vs[t] - x0) * inverse
            x0, x1 = f[0] * x0 + f[1] * x1, f[2] * x0 + f[3] * x1
        a0, a1 = zero, zero
        for t in range(span - 1, -1, -1):
            a0, a1 = f[0] * a0 + f[2] * a1 + vs[t], f[1] * a0 + f[3] * a1
        for level, jump in enumerate(jumps):
            s0, s1 = shift(a0, -(1 << level)), shift(a1, -(1 << level))
            a0, a1 = a0 + jump[0] * s0 + jump[2] * s1, a1 + jump[1] * s0 + jump[3] * s1
        a0, a1 = shift(a0, -1), shift(a1, -1)
        for t in range(span - 1, -1, -1):
            r = vs[t] - k0 * a0 - k1 * a1
            a0, a1 = f[0] * a0 + f[2] * a1 + vs[t], f[1] * a0 + f[3] * a1
            scratch[chunk, pl.ds(t, SUB, stride=span), :] = r
        r_ref[:, cols] = scratch[chunk]


def finish_kernel(place_ref, r_ref, w_ref, g_ref, const_ref, basis_ref, sums_ref, *outs):
    blocks, pieces = sums_ref.shape[0], len(outs)
    depth = outs[0].shape[1]
    value = r_ref[...]
    for line in range(4):
        total = None
        for block in range(blocks):
            term = g_ref[line, pl.ds(4 * block, 4), :] * sums_ref[block]
            total = term if total is None else total + term
        value = value - w_ref[line] * jnp.sum(total, axis=0, keepdims=True)
    scale = const_ref[19, 0:1, :]
    residual = (value * scale).astype(jnp.bfloat16)
    for piece in range(pieces - 1, -1, -1):
        begin = pl.multiple_of((place_ref[0] ^ piece) * depth, depth)
        outs[piece][...] = lax.dot_general(
            residual,
            basis_ref[pl.ds(begin, depth), :],
            (((1,), (1,)), ((), ())),
            preferred_element_type=F32,
        ).astype(outs[piece].dtype)


def exchange(value, axis, count):
    out = [value]
    for step in range(1, count):
        out.append(lax.ppermute(value, axis, [(a, a ^ step) for a in range(count)]))
    return out


def shards(observations, basis, eigvals, lengths, noise):
    steps, depth = observations.shape
    width = basis.shape[1]
    blocks, pieces = lax.axis_size("tm"), lax.axis_size("mode")
    me = lax.axis_index("tm").astype(jnp.int32).reshape(1)
    place = lax.axis_index("mode").astype(jnp.int32).reshape(1)
    vmem = pl.BlockSpec(memory_space=pltpu.VMEM)
    smem = pl.BlockSpec(memory_space=pltpu.SMEM)
    params = pltpu.CompilerParams(vmem_limit_bytes=VMEM_LIMIT)

    def shape(*dims, dtype=F32):
        return jax.ShapeDtypeStruct(dims, dtype)

    obs = exchange(observations, "mode", pieces)
    const, w, g, basis, obs[0] = pl.pallas_call(
        functools.partial(coefficients_kernel, blocks),
        out_shape=(
            shape(20, SUB, width),
            shape(4, steps, width),
            shape(4, 4 * blocks, width),
            shape(*basis.shape, dtype=basis.dtype),
            shape(steps, depth, dtype=observations.dtype),
        ),
        in_specs=[smem] + [pl.BlockSpec(memory_space=pltpu.HBM)] * 5,
        out_specs=(vmem,) * 5,
        scratch_shapes=[
            pltpu.SMEM((1,), F32),
            pltpu.VMEM((1, width), F32),
            pltpu.VMEM((1, width), F32),
            pltpu.SemaphoreType.DMA((5,)),
        ],
        compiler_params=params,
        cost_estimate=pl.CostEstimate(flops=20000000, bytes_accessed=2000000, transcendentals=0),
        name="coefficients",
    )(me, noise, eigvals.reshape(1, width), lengths.reshape(1, width), observations, basis)
    z, summary = pl.pallas_call(
        functools.partial(rotate_kernel, pieces),
        out_shape=(shape(steps, width), shape(blocks, 4, width)),
        in_specs=[smem] + [vmem] * (pieces + 2),
        out_specs=(vmem,) * 2,
        compiler_params=params,
        name="rotate",
    )(place, *obs, basis, w)
    sums = lax.all_to_all(summary, "tm", 0, 0)
    local = pl.pallas_call(
        local_kernel,
        out_shape=shape(steps, width),
        in_specs=[vmem] * 2,
        out_specs=vmem,
        scratch_shapes=[pltpu.VMEM((width // 128, steps, 128), F32)],
        compiler_params=params,
        cost_estimate=pl.CostEstimate(flops=10000000, bytes_accessed=1000000, transcendentals=0),
        name="local",
    )(z, const)
    parts = pl.pallas_call(
        finish_kernel,
        out_shape=(shape(steps, depth),)
        + (shape(steps, depth, dtype=jnp.bfloat16),) * (pieces - 1),
        in_specs=[smem] + [vmem] * 6,
        out_specs=(vmem,) * pieces,
        compiler_params=params,
        name="finish",
    )(place, local, w, g, const, basis, sums)
    grad_obs = parts[0]
    for step in range(1, pieces):
        grad_obs = grad_obs + lax.ppermute(
            parts[step], "mode", [(a, a ^ step) for a in range(pieces)]
        ).astype(F32)
    return grad_obs


def solution(mesh):
    placed = (P("tm", "mode"), P(None, "mode"), P("mode"), P("mode"), P())
    return jax.shard_map(
        shards, mesh=mesh, in_specs=placed, out_specs=P("tm", "mode"), check_vma=False
    )
```

```python
import functools
import math

import jax
import jax.numpy as jnp
from jax import lax
from jax.experimental import pallas as pl
from jax.experimental.pallas import tpu as pltpu
from jax.sharding import PartitionSpec as P

F32 = jnp.float32
SUB = 8
VMEM_LIMIT = 24 * 1024 * 1024


def mat_mul(p, q):
    return (
        p[0] * q[0] + p[1] * q[2],
        p[0] * q[1] + p[1] * q[3],
        p[2] * q[0] + p[3] * q[2],
        p[2] * q[1] + p[3] * q[3],
    )


def mat_trans(p):
    return (p[0], p[2], p[1], p[3])


def mat_add(p, q):
    return tuple(a + b for a, b in zip(p, q))


def mat_sub(p, q):
    return tuple(a - b for a, b in zip(p, q))


def mat_pick(flag, p, q):
    return tuple(jnp.where(flag, a, b) for a, b in zip(p, q))


def full(s):
    return (s[0], s[1], s[1], s[2])


def congruence(s, f):
    t = (
        s[0] * f[0] + s[1] * f[2],
        s[0] * f[1] + s[1] * f[3],
        s[1] * f[0] + s[2] * f[2],
        s[1] * f[1] + s[2] * f[3],
    )
    return (f[0] * t[0] + f[2] * t[2], f[0] * t[1] + f[2] * t[3], f[1] * t[1] + f[3] * t[3])


def power(squares, exponent, like):
    one, zero = jnp.ones_like(like), jnp.zeros_like(like)
    out = None
    for bit, base in enumerate(squares):
        flag = (exponent & (1 << bit)) != 0
        if out is None:
            out = mat_pick(flag, base, (one, zero, zero, one))
        else:
            out = mat_pick(flag, mat_mul(out, base), out)
    return out


def gramian(squares, grams, count, like):
    zero = jnp.zeros_like(like)
    out = (zero, zero, zero)
    for bit, (base, gram) in enumerate(zip(squares, grams)):
        flag = (count & (1 << bit)) != 0
        out = mat_pick(flag, mat_add(gram, congruence(out, base)), out)
    return out


def steady_state(scale2, length, noise_var):
    lam = math.sqrt(3.0) / length
    decay = jnp.exp(-lam)
    twice = 2.0 * lam
    fall = jnp.exp(-twice)
    rho = scale2 / noise_var
    series = 1.0 / 604800.0
    for factor in (60480.0, 6720.0, 840.0, 120.0, 20.0, 4.0, 1.0):
        series = series * twice + 1.0 / factor
    lower = fall * twice * twice * twice * (1.0 / 6.0) * series
    loss = 1.0
    for order in (8, 7, 6, 5, 4, 3, 2):
        loss = 1.0 - lam * (1.0 / order) * loss
    loss = lam * loss
    q00 = rho * lower
    q01 = 2.0 * rho * lam * lam * fall
    q11 = rho * (lower + twice * fall)
    slope = decay * lam
    tilt = loss + slope
    g0 = q00 * tilt * tilt + 2.0 * slope * q01 * tilt + slope * slope * q11
    g1 = slope * q01 - decay * (1.0 - lam) * q00
    loss2 = loss * loss
    c2 = decay * decay
    u = (2.0 * decay * loss2 - g1) / c2
    v = (loss2 * loss2 + g0) / c2
    root = jnp.sqrt(v * (v + 4.0 * u + 16.0))
    product = 4.0 * v / (v + root + jnp.sqrt(2.0 * v * (v + 2.0 * u + root)))
    total = 0.5 * (jnp.sqrt(u * u + 4.0 * u - 2.0 * v + 2.0 * root) - u)
    gain0 = total - 2.0 * loss
    gain1 = (product - loss2 - gain0 * tilt) / slope
    inverse = (1.0 - total + product) / c2
    inn = c2 / (1.0 - total + product)
    closed = (1.0 + slope - loss - gain0, slope, -slope - gain1, decay * (1.0 - lam))
    p00 = inn * ((1.0 - lam) * gain0 - lam * gain1) / decay
    p01 = inn * (lam * gain0 + (1.0 + lam) * gain1) / decay
    p11 = (
        p01 * (loss * (1.0 + decay) + 2.0 * slope * slope)
        + slope * decay * (1.0 + lam) * p00
        - q01
        + gain0 * gain1 * inn
    ) / (slope * decay * (1.0 - lam))
    return closed, gain0, gain1, inverse, (rho - p00, -p01, rho - p11)


def coefficients_kernel(blocks, me_ref, noise_ref, *refs):
    arguments, (const_ref, w_ref, g_ref, merge_ref, basis_ref, obs_ref) = (
        refs[:4],
        refs[4:10],
    )
    scale_ref, length_ref, sems = refs[10:]
    copies = [
        pltpu.make_async_copy(source, target, sems.at[k])
        for k, (source, target) in enumerate(
            zip(arguments, (scale_ref, length_ref, obs_ref, basis_ref))
        )
    ]
    for copy in copies:
        copy.start()
    for copy in copies[:2]:
        copy.wait()
    steps = w_ref.shape[1]
    width = scale_ref.shape[1]
    tile = (SUB, width)
    me = me_ref[0]
    scale2 = jnp.broadcast_to(scale_ref[...], tile)
    length = jnp.broadcast_to(length_ref[...], tile)
    noise_var = jnp.full(tile, noise_ref[0], F32)
    closed, gain0, gain1, inverse, excess = steady_state(scale2, length, noise_var)
    zero = jnp.zeros(tile, F32)

    squares, grams = [closed], [(inverse, zero, zero)]
    doublings = (steps * blocks).bit_length() - 1
    for _ in range(doublings):
        base = squares[-1]
        grams.append(mat_add(grams[-1], congruence(grams[-1], base)))
        squares.append(mat_mul(base, base))
    local = steps.bit_length() - 1
    consts = closed + (gain0, gain1, inverse) + squares[3] + squares[4] + squares[5]
    for place, value in enumerate(consts):
        const_ref[place] = value
    const_ref[len(consts)] = -1.0 / noise_var
    for level in range(blocks.bit_length() - 1):
        for place, value in enumerate(squares[local + level] + grams[local + level]):
            merge_ref[7 * level + place : 7 * level + place + 1, :] = value[0:1, :]

    row = lax.broadcasted_iota(jnp.int32, tile, 0)
    small, gram_small = squares[:3], grams[:3]
    behind = power(small, 7 - row, zero)
    gram = gramian(small, gram_small, 7 - row, zero)
    eight, gram_eight = squares[3], grams[3]
    parts = steps // SUB
    for part in range(parts - 1, -1, -1):
        rows = pl.ds(part * SUB, SUB)
        w_ref[0, rows, :] = behind[0] * gain0 + behind[1] * gain1
        w_ref[1, rows, :] = behind[2] * gain0 + behind[3] * gain1
        k0 = gain0 * gram[0] + gain1 * gram[1]
        k1 = gain0 * gram[1] + gain1 * gram[2]
        w_ref[2, rows, :] = inverse - (k0 * closed[0] + k1 * closed[2])
        w_ref[3, rows, :] = -(k0 * closed[1] + k1 * closed[3])
        if part:
            behind = mat_mul(behind, eight)
            gram = mat_add(gram_eight, congruence(gram, eight))
    ahead = power(small, row, zero)
    for part in range(parts):
        rows = pl.ds(part * SUB, SUB)
        u0, u1 = w_ref[2, rows, :], w_ref[3, rows, :]
        w_ref[2, rows, :] = u0 * ahead[0] + u1 * ahead[2]
        w_ref[3, rows, :] = u0 * ahead[1] + u1 * ahead[3]
        if part < parts - 1:
            ahead = mat_mul(ahead, eight)

    s = grams[-1]
    left = (
        1.0 + excess[0] * s[0] + excess[1] * s[1],
        excess[0] * s[1] + excess[1] * s[2],
        excess[1] * s[0] + excess[2] * s[1],
        1.0 + excess[1] * s[1] + excess[2] * s[2],
    )
    determ = 1.0 / (left[0] * left[3] - left[1] * left[2])
    start = mat_mul((left[3], -left[1], -left[2], left[0]), full(excess))
    start = tuple(x * determ for x in start)
    block_squares, block_grams = squares[local:-1], grams[local:-1]
    mine = jnp.full(tile, me, jnp.int32)
    to_me = power(block_squares, mine, zero)
    rest = full(gramian(block_squares, block_grams, blocks - 1 - mine, zero))
    to_state = mat_mul(to_me, start)
    to_adjoint = mat_mul(mat_mul(rest, mat_mul(to_me, block_squares[0])), start)
    for group in range(g_ref.shape[1] // SUB):
        rows = row + group * SUB
        kind = rows & 3
        line = rows >> 2
        span = jnp.where(line == 0, 1, jnp.left_shift(1, jnp.maximum(line - 1, 0)))
        near_me = jnp.where(line == 0, mine, mine ^ span)
        front = jnp.minimum((near_me // span) * span, blocks - 1)
        back = jnp.minimum(front + span - 1, blocks - 1)
        before, after = back < me, front > me
        gap = jnp.where(before, me - 1 - back, jnp.where(after, front - 1 - me, 0))
        reach = jnp.where(before, me - back, jnp.where(after, back - me, 0))
        near = power(block_squares, gap, zero)
        far = power(block_squares, reach, zero)
        origin = mat_trans(power(block_squares, front, zero))
        left_over = full(gramian(block_squares, block_grams, blocks - 1 - back, zero))
        end = mat_trans(mat_mul(power(block_squares, back, zero), block_squares[0]))
        first = mat_mul(end, left_over)
        state_b = mat_sub(mat_pick(before, near, (zero,) * 4), mat_mul(to_state, first))
        state_l = mat_mul(to_state, origin)
        cross = mat_pick(after, mat_mul(mat_trans(far), left_over), mat_mul(rest, far))
        adjoint_b = mat_sub(mat_mul(to_adjoint, first), cross)
        adjoint_l = mat_sub(
            mat_pick(after, mat_trans(near), (zero,) * 4), mat_mul(to_adjoint, origin)
        )
        place = pl.ds(group * SUB, SUB)
        for output, (from_b, from_l) in enumerate(
            ((adjoint_b[:2], adjoint_l[:2]), (adjoint_b[2:], adjoint_l[2:]),
             (state_b[:2], state_l[:2]), (state_b[2:], state_l[2:]))
        ):
            g_ref[output, place, :] = jnp.where(
                kind < 2,
                jnp.where(kind == 0, from_b[0], from_b[1]),
                jnp.where(kind == 2, from_l[0], from_l[1]),
            )
    for copy in copies[2:]:
        copy.wait()


def rotate_kernel(pieces, place_ref, *refs):
    obs_refs = refs[:pieces]
    basis_ref, w_ref, z_ref, sum_ref = refs[pieces:]
    depth = obs_refs[0].shape[1]
    z = None
    for piece, obs_ref in enumerate(obs_refs):
        begin = pl.multiple_of((place_ref[0] ^ piece) * depth, depth)
        term = jnp.dot(
            obs_ref[...], basis_ref[pl.ds(begin, depth), :], preferred_element_type=F32
        )
        z = term if z is None else z + term
    z_ref[...] = z
    for line in range(4):
        sum_ref[line : line + 1, :] = jnp.sum(w_ref[line] * z, axis=0, keepdims=True)


def merge_kernel(level, me_ref, own_ref, other_ref, merge_ref, out_ref):
    own, other = own_ref[...], other_ref[...]
    lower = jnp.full(own.shape, (me_ref[0] >> level) & 1, jnp.int32) == 0
    left, right = jnp.where(lower, own, other), jnp.where(lower, other, own)
    f00, f01, f10, f11, s00, s01, s11 = (
        merge_ref[7 * level + k : 7 * level + k + 1, :] for k in range(7)
    )
    b0, b1 = left[0:1, :], left[1:2, :]
    a0 = right[2:3, :] - s00 * b0 - s01 * b1
    a1 = right[3:4, :] - s01 * b0 - s11 * b1
    out_ref[0:1, :] = right[0:1, :] + f00 * b0 + f01 * b1
    out_ref[1:2, :] = right[1:2, :] + f10 * b0 + f11 * b1
    out_ref[2:3, :] = left[2:3, :] + f00 * a0 + f10 * a1
    out_ref[3:4, :] = left[3:4, :] + f01 * a0 + f11 * a1


def shift(value, by):
    rows = value.shape[0]
    row = lax.broadcasted_iota(jnp.int32, value.shape, 0)
    keep = row >= by if by > 0 else row < rows + by
    return jnp.where(keep, pltpu.roll(value, by % rows, 0), 0.0)


def local_kernel(z_ref, const_ref, r_ref, scratch):
    steps, width = z_ref.shape
    span = steps // SUB
    lanes = 128
    for chunk in range(width // lanes):
        cols = pl.ds(chunk * lanes, lanes)
        scratch[chunk] = z_ref[:, cols]
    for chunk in range(width // lanes):
        cols = pl.ds(chunk * lanes, lanes)
        const = [const_ref[k, :, cols] for k in range(19)]
        f, (k0, k1, inverse) = const[0:4], const[4:7]
        jumps = (const[7:11], const[11:15], const[15:19])
        zero = jnp.zeros((SUB, lanes), F32)
        x0, x1 = zero, zero
        vs = []
        for t in range(span):
            z = scratch[chunk, pl.ds(t, SUB, stride=span), :]
            vs.append(z - x0)
            x0, x1 = f[0] * x0 + f[1] * x1 + k0 * z, f[2] * x0 + f[3] * x1 + k1 * z
        for level, jump in enumerate(jumps):
            s0, s1 = shift(x0, 1 << level), shift(x1, 1 << level)
            x0, x1 = x0 + jump[0] * s0 + jump[1] * s1, x1 + jump[2] * s0 + jump[3] * s1
        x0, x1 = shift(x0, 1), shift(x1, 1)
        for t in range(span):
            vs[t] = (vs[t] - x0) * inverse
            x0, x1 = f[0] * x0 + f[1] * x1, f[2] * x0 + f[3] * x1
        a0, a1 = zero, zero
        for t in range(span - 1, -1, -1):
            a0, a1 = f[0] * a0 + f[2] * a1 + vs[t], f[1] * a0 + f[3] * a1
        for level, jump in enumerate(jumps):
            s0, s1 = shift(a0, -(1 << level)), shift(a1, -(1 << level))
            a0, a1 = a0 + jump[0] * s0 + jump[2] * s1, a1 + jump[1] * s0 + jump[3] * s1
        a0, a1 = shift(a0, -1), shift(a1, -1)
        for t in range(span - 1, -1, -1):
            r = vs[t] - k0 * a0 - k1 * a1
            a0, a1 = f[0] * a0 + f[2] * a1 + vs[t], f[1] * a0 + f[3] * a1
            scratch[chunk, pl.ds(t, SUB, stride=span), :] = r
        r_ref[:, cols] = scratch[chunk]


def finish_kernel(pieces, place_ref, r_ref, w_ref, g_ref, const_ref, basis_ref, *refs):
    sums, outs = refs[:-pieces], refs[-pieces:]
    depth = outs[0].shape[1]
    value = r_ref[...]
    for line in range(4):
        total = None
        for place, sum_ref in enumerate(sums):
            term = g_ref[line, pl.ds(4 * place, 4), :] * sum_ref[...]
            total = term if total is None else total + term
        value = value - w_ref[line] * jnp.sum(total, axis=0, keepdims=True)
    scale = const_ref[19, 0:1, :]
    residual = (value * scale).astype(jnp.bfloat16)
    for piece in range(pieces - 1, -1, -1):
        begin = pl.multiple_of((place_ref[0] ^ piece) * depth, depth)
        outs[piece][...] = lax.dot_general(
            residual,
            basis_ref[pl.ds(begin, depth), :],
            (((1,), (1,)), ((), ())),
            preferred_element_type=F32,
        ).astype(outs[piece].dtype)


def exchange(value, axis, count):
    out = [value]
    for step in range(1, count):
        out.append(lax.ppermute(value, axis, [(a, a ^ step) for a in range(count)]))
    return out


def shards(observations, basis, eigvals, lengths, noise):
    steps, depth = observations.shape
    width = basis.shape[1]
    blocks, pieces = lax.axis_size("tm"), lax.axis_size("mode")
    me = lax.axis_index("tm").astype(jnp.int32).reshape(1)
    place = lax.axis_index("mode").astype(jnp.int32).reshape(1)
    rounds = blocks.bit_length() - 1
    vmem = pl.BlockSpec(memory_space=pltpu.VMEM)
    smem = pl.BlockSpec(memory_space=pltpu.SMEM)
    params = pltpu.CompilerParams(vmem_limit_bytes=VMEM_LIMIT)

    def shape(*dims, dtype=F32):
        return jax.ShapeDtypeStruct(dims, dtype)

    obs = exchange(observations, "mode", pieces)
    const, w, g, merge, basis, obs[0] = pl.pallas_call(
        functools.partial(coefficients_kernel, blocks),
        out_shape=(
            shape(20, SUB, width),
            shape(4, steps, width),
            shape(4, -(-4 * (rounds + 1) // SUB) * SUB, width),
            shape(-(-7 * rounds // SUB) * SUB, width),
            shape(*basis.shape, dtype=basis.dtype),
            shape(steps, depth, dtype=observations.dtype),
        ),
        in_specs=[smem] * 2 + [pl.BlockSpec(memory_space=pltpu.HBM)] * 4,
        out_specs=(vmem,) * 6,
        scratch_shapes=[
            pltpu.VMEM((1, width), F32),
            pltpu.VMEM((1, width), F32),
            pltpu.SemaphoreType.DMA((4,)),
        ],
        compiler_params=params,
        cost_estimate=pl.CostEstimate(flops=20000000, bytes_accessed=2000000, transcendentals=0),
        name="coefficients",
    )(
        me,
        noise,
        *(
            pltpu.with_memory_space_constraint(x, pltpu.HBM)
            for x in (
                eigvals.reshape(1, width),
                lengths.reshape(1, width),
                observations,
                basis,
            )
        ),
    )
    z, summary = pl.pallas_call(
        functools.partial(rotate_kernel, pieces),
        out_shape=(shape(steps, width), shape(4, width)),
        in_specs=[smem] + [vmem] * (pieces + 2),
        out_specs=(vmem,) * 2,
        compiler_params=params,
        name="rotate",
    )(place, *obs, basis, w)
    sums = [summary]
    for level in range(rounds):
        step = 1 << level
        other = lax.ppermute(summary, "tm", [(a, a ^ step) for a in range(blocks)])
        sums.append(other)
        if level < rounds - 1:
            summary = pl.pallas_call(
                functools.partial(merge_kernel, level),
                out_shape=shape(4, width),
                in_specs=[smem] + [vmem] * 3,
                out_specs=vmem,
                compiler_params=params,
                name="merge",
            )(me, summary, other, merge)
    local = pl.pallas_call(
        local_kernel,
        out_shape=shape(steps, width),
        in_specs=[vmem] * 2,
        out_specs=vmem,
        scratch_shapes=[pltpu.VMEM((width // 128, steps, 128), F32)],
        compiler_params=params,
        cost_estimate=pl.CostEstimate(flops=10000000, bytes_accessed=1000000, transcendentals=0),
        name="local",
    )(z, const)
    parts = pl.pallas_call(
        functools.partial(finish_kernel, pieces),
        out_shape=(shape(steps, depth),)
        + (shape(steps, depth, dtype=jnp.bfloat16),) * (pieces - 1),
        in_specs=[smem] + [vmem] * (5 + len(sums)),
        out_specs=(vmem,) * pieces,
        compiler_params=params,
        name="finish",
    )(place, local, w, g, const, basis, *sums)
    grad_obs = parts[0]
    for step in range(1, pieces):
        grad_obs = grad_obs + lax.ppermute(
            parts[step], "mode", [(a, a ^ step) for a in range(pieces)]
        ).astype(F32)
    return grad_obs


def solution(mesh):
    placed = (P("tm", "mode"), P(None, "mode"), P("mode"), P("mode"), P())
    return jax.shard_map(
        shards, mesh=mesh, in_specs=placed, out_specs=P("tm", "mode"), check_vma=False
    )
```

```python
import functools
import math

import jax
import jax.numpy as jnp
from jax import lax
from jax.experimental import pallas as pl
from jax.experimental.pallas import tpu as pltpu
from jax.sharding import PartitionSpec as P

F32 = jnp.float32
SUB = 8
VMEM_LIMIT = 24 * 1024 * 1024


def mat_mul(p, q):
    return (
        p[0] * q[0] + p[1] * q[2],
        p[0] * q[1] + p[1] * q[3],
        p[2] * q[0] + p[3] * q[2],
        p[2] * q[1] + p[3] * q[3],
    )


def mat_trans(p):
    return (p[0], p[2], p[1], p[3])


def mat_add(p, q):
    return tuple(a + b for a, b in zip(p, q))


def mat_sub(p, q):
    return tuple(a - b for a, b in zip(p, q))


def mat_pick(flag, p, q):
    return tuple(jnp.where(flag, a, b) for a, b in zip(p, q))


def full(s):
    return (s[0], s[1], s[1], s[2])


def congruence(s, f):
    t = (
        s[0] * f[0] + s[1] * f[2],
        s[0] * f[1] + s[1] * f[3],
        s[1] * f[0] + s[2] * f[2],
        s[1] * f[1] + s[2] * f[3],
    )
    return (f[0] * t[0] + f[2] * t[2], f[0] * t[1] + f[2] * t[3], f[1] * t[1] + f[3] * t[3])


def power(squares, exponent, like):
    one, zero = jnp.ones_like(like), jnp.zeros_like(like)
    out = None
    for bit, base in enumerate(squares):
        flag = (exponent & (1 << bit)) != 0
        if out is None:
            out = mat_pick(flag, base, (one, zero, zero, one))
        else:
            out = mat_pick(flag, mat_mul(out, base), out)
    return out


def gramian(squares, grams, count, like):
    zero = jnp.zeros_like(like)
    out = (zero, zero, zero)
    for bit, (base, gram) in enumerate(zip(squares, grams)):
        flag = (count & (1 << bit)) != 0
        out = mat_pick(flag, mat_add(gram, congruence(out, base)), out)
    return out


def steady_state(scale2, length, noise_var):
    lam = math.sqrt(3.0) / length
    decay = jnp.exp(-lam)
    twice = 2.0 * lam
    fall = jnp.exp(-twice)
    rho = scale2 / noise_var
    series = 1.0 / 604800.0
    for factor in (60480.0, 6720.0, 840.0, 120.0, 20.0, 4.0, 1.0):
        series = series * twice + 1.0 / factor
    lower = fall * twice * twice * twice * (1.0 / 6.0) * series
    loss = 1.0
    for order in (8, 7, 6, 5, 4, 3, 2):
        loss = 1.0 - lam * (1.0 / order) * loss
    loss = lam * loss
    q00 = rho * lower
    q01 = 2.0 * rho * lam * lam * fall
    q11 = rho * (lower + twice * fall)
    slope = decay * lam
    tilt = loss + slope
    g0 = q00 * tilt * tilt + 2.0 * slope * q01 * tilt + slope * slope * q11
    g1 = slope * q01 - decay * (1.0 - lam) * q00
    loss2 = loss * loss
    c2 = decay * decay
    u = (2.0 * decay * loss2 - g1) / c2
    v = (loss2 * loss2 + g0) / c2
    root = jnp.sqrt(v * (v + 4.0 * u + 16.0))
    product = 4.0 * v / (v + root + jnp.sqrt(2.0 * v * (v + 2.0 * u + root)))
    total = 0.5 * (jnp.sqrt(u * u + 4.0 * u - 2.0 * v + 2.0 * root) - u)
    gain0 = total - 2.0 * loss
    gain1 = (product - loss2 - gain0 * tilt) / slope
    inverse = (1.0 - total + product) / c2
    inn = c2 / (1.0 - total + product)
    closed = (1.0 + slope - loss - gain0, slope, -slope - gain1, decay * (1.0 - lam))
    p00 = inn * ((1.0 - lam) * gain0 - lam * gain1) / decay
    p01 = inn * (lam * gain0 + (1.0 + lam) * gain1) / decay
    p11 = (
        p01 * (loss * (1.0 + decay) + 2.0 * slope * slope)
        + slope * decay * (1.0 + lam) * p00
        - q01
        + gain0 * gain1 * inn
    ) / (slope * decay * (1.0 - lam))
    return closed, gain0, gain1, inverse, (rho - p00, -p01, rho - p11)


def coefficients_kernel(blocks, me_ref, noise_ref, *refs):
    arguments, (const_ref, w_ref, g_ref, merge_ref, basis_ref, obs_ref) = (
        refs[:4],
        refs[4:10],
    )
    scale_ref, length_ref, sems = refs[10:]
    copies = [
        pltpu.make_async_copy(source, target, sems.at[k])
        for k, (source, target) in enumerate(
            zip(arguments, (scale_ref, length_ref, obs_ref, basis_ref))
        )
    ]
    for copy in copies:
        copy.start()
    for copy in copies[:2]:
        copy.wait()
    steps = w_ref.shape[1]
    width = scale_ref.shape[1]
    tile = (SUB, width)
    me = me_ref[0]
    scale2 = jnp.broadcast_to(scale_ref[...], tile)
    length = jnp.broadcast_to(length_ref[...], tile)
    noise_var = jnp.full(tile, noise_ref[0], F32)
    closed, gain0, gain1, inverse, excess = steady_state(scale2, length, noise_var)
    zero = jnp.zeros(tile, F32)

    squares, grams = [closed], [(inverse, zero, zero)]
    doublings = (steps * blocks).bit_length() - 1
    for _ in range(doublings):
        base = squares[-1]
        grams.append(mat_add(grams[-1], congruence(grams[-1], base)))
        squares.append(mat_mul(base, base))
    local = steps.bit_length() - 1
    consts = closed + (gain0, gain1, inverse) + squares[3] + squares[4] + squares[5]
    for place, value in enumerate(consts):
        const_ref[place] = value
    const_ref[len(consts)] = -1.0 / noise_var
    for level in range(blocks.bit_length() - 1):
        for place, value in enumerate(squares[local + level] + grams[local + level]):
            merge_ref[7 * level + place : 7 * level + place + 1, :] = value[0:1, :]

    row = lax.broadcasted_iota(jnp.int32, tile, 0)
    small, gram_small = squares[:3], grams[:3]
    behind = power(small, 7 - row, zero)
    gram = gramian(small, gram_small, 7 - row, zero)
    eight, gram_eight = squares[3], grams[3]
    parts = steps // SUB
    for part in range(parts - 1, -1, -1):
        rows = pl.ds(part * SUB, SUB)
        w_ref[0, rows, :] = behind[0] * gain0 + behind[1] * gain1
        w_ref[1, rows, :] = behind[2] * gain0 + behind[3] * gain1
        k0 = gain0 * gram[0] + gain1 * gram[1]
        k1 = gain0 * gram[1] + gain1 * gram[2]
        w_ref[2, rows, :] = inverse - (k0 * closed[0] + k1 * closed[2])
        w_ref[3, rows, :] = -(k0 * closed[1] + k1 * closed[3])
        if part:
            behind = mat_mul(behind, eight)
            gram = mat_add(gram_eight, congruence(gram, eight))
    ahead = power(small, row, zero)
    for part in range(parts):
        rows = pl.ds(part * SUB, SUB)
        u0, u1 = w_ref[2, rows, :], w_ref[3, rows, :]
        w_ref[2, rows, :] = u0 * ahead[0] + u1 * ahead[2]
        w_ref[3, rows, :] = u0 * ahead[1] + u1 * ahead[3]
        if part < parts - 1:
            ahead = mat_mul(ahead, eight)

    s = grams[-1]
    left = (
        1.0 + excess[0] * s[0] + excess[1] * s[1],
        excess[0] * s[1] + excess[1] * s[2],
        excess[1] * s[0] + excess[2] * s[1],
        1.0 + excess[1] * s[1] + excess[2] * s[2],
    )
    determ = 1.0 / (left[0] * left[3] - left[1] * left[2])
    start = mat_mul((left[3], -left[1], -left[2], left[0]), full(excess))
    start = tuple(x * determ for x in start)
    block_squares, block_grams = squares[local:-1], grams[local:-1]
    mine = jnp.full(tile, me, jnp.int32)
    to_me = power(block_squares, mine, zero)
    rest = full(gramian(block_squares, block_grams, blocks - 1 - mine, zero))
    to_state = mat_mul(to_me, start)
    to_adjoint = mat_mul(mat_mul(rest, mat_mul(to_me, block_squares[0])), start)
    for group in range(g_ref.shape[1] // SUB):
        rows = row + group * SUB
        kind = rows & 3
        line = rows >> 2
        span = jnp.where(line == 0, 1, jnp.left_shift(1, jnp.maximum(line - 1, 0)))
        near_me = jnp.where(line == 0, mine, mine ^ span)
        front = jnp.minimum((near_me // span) * span, blocks - 1)
        back = jnp.minimum(front + span - 1, blocks - 1)
        before, after = back < me, front > me
        gap = jnp.where(before, me - 1 - back, jnp.where(after, front - 1 - me, 0))
        reach = jnp.where(before, me - back, jnp.where(after, back - me, 0))
        near = power(block_squares, gap, zero)
        far = power(block_squares, reach, zero)
        origin = mat_trans(power(block_squares, front, zero))
        left_over = full(gramian(block_squares, block_grams, blocks - 1 - back, zero))
        end = mat_trans(mat_mul(power(block_squares, back, zero), block_squares[0]))
        first = mat_mul(end, left_over)
        state_b = mat_sub(mat_pick(before, near, (zero,) * 4), mat_mul(to_state, first))
        state_l = mat_mul(to_state, origin)
        cross = mat_pick(after, mat_mul(mat_trans(far), left_over), mat_mul(rest, far))
        adjoint_b = mat_sub(mat_mul(to_adjoint, first), cross)
        adjoint_l = mat_sub(
            mat_pick(after, mat_trans(near), (zero,) * 4), mat_mul(to_adjoint, origin)
        )
        place = pl.ds(group * SUB, SUB)
        for output, (from_b, from_l) in enumerate(
            ((adjoint_b[:2], adjoint_l[:2]), (adjoint_b[2:], adjoint_l[2:]),
             (state_b[:2], state_l[:2]), (state_b[2:], state_l[2:]))
        ):
            g_ref[output, place, :] = jnp.where(
                kind < 2,
                jnp.where(kind == 0, from_b[0], from_b[1]),
                jnp.where(kind == 2, from_l[0], from_l[1]),
            )
    for copy in copies[2:]:
        copy.wait()


def rotate_kernel(pieces, place_ref, *refs):
    obs_refs = refs[:pieces]
    basis_ref, w_ref, z_ref, sum_ref = refs[pieces:]
    depth = obs_refs[0].shape[1]
    z = None
    for piece, obs_ref in enumerate(obs_refs):
        begin = pl.multiple_of((place_ref[0] ^ piece) * depth, depth)
        term = jnp.dot(
            obs_ref[...], basis_ref[pl.ds(begin, depth), :], preferred_element_type=F32
        )
        z = term if z is None else z + term
    z_ref[...] = z
    for line in range(4):
        sum_ref[line : line + 1, :] = jnp.sum(w_ref[line] * z, axis=0, keepdims=True)


def pair_kernel(own_ref, mate_ref, out_ref):
    out_ref[0:4, :] = own_ref[...]
    out_ref[4:8, :] = mate_ref[...]


def merge_kernel(level, me_ref, own_ref, other_ref, merge_ref, mate_ref, out_ref):
    own, other = own_ref[...], other_ref[...]
    lower = jnp.full(own.shape, (me_ref[0] >> level) & 1, jnp.int32) == 0
    left, right = jnp.where(lower, own, other), jnp.where(lower, other, own)
    for at, ref in ((0, merge_ref), (4, mate_ref)):
        f00, f01, f10, f11, s00, s01, s11 = (
            ref[7 * level + k : 7 * level + k + 1, :] for k in range(7)
        )
        b0, b1 = left[at : at + 1, :], left[at + 1 : at + 2, :]
        a0 = right[at + 2 : at + 3, :] - s00 * b0 - s01 * b1
        a1 = right[at + 3 : at + 4, :] - s01 * b0 - s11 * b1
        out_ref[at : at + 1, :] = right[at : at + 1, :] + f00 * b0 + f01 * b1
        out_ref[at + 1 : at + 2, :] = right[at + 1 : at + 2, :] + f10 * b0 + f11 * b1
        out_ref[at + 2 : at + 3, :] = left[at + 2 : at + 3, :] + f00 * a0 + f10 * a1
        out_ref[at + 3 : at + 4, :] = left[at + 3 : at + 4, :] + f01 * a0 + f11 * a1


def pack_kernel(*refs):
    for place, ref in enumerate(refs[:-1]):
        refs[-1][8 * place : 8 * place + 4, :] = ref[4:8, :]
        refs[-1][8 * place + 4 : 8 * place + 8, :] = ref[0:4, :]


def shift(value, by):
    rows = value.shape[0]
    row = lax.broadcasted_iota(jnp.int32, value.shape, 0)
    keep = row >= by if by > 0 else row < rows + by
    return jnp.where(keep, pltpu.roll(value, by % rows, 0), 0.0)


def local_kernel(z_ref, const_ref, r_ref, scratch):
    steps, width = z_ref.shape
    span = steps // SUB
    lanes = 128
    for chunk in range(width // lanes):
        cols = pl.ds(chunk * lanes, lanes)
        scratch[chunk] = z_ref[:, cols]
    for chunk in range(width // lanes):
        cols = pl.ds(chunk * lanes, lanes)
        const = [const_ref[k, :, cols] for k in range(19)]
        f, (k0, k1, inverse) = const[0:4], const[4:7]
        jumps = (const[7:11], const[11:15], const[15:19])
        zero = jnp.zeros((SUB, lanes), F32)
        x0, x1 = zero, zero
        vs = []
        for t in range(span):
            z = scratch[chunk, pl.ds(t, SUB, stride=span), :]
            vs.append(z - x0)
            x0, x1 = f[0] * x0 + f[1] * x1 + k0 * z, f[2] * x0 + f[3] * x1 + k1 * z
        for level, jump in enumerate(jumps):
            s0, s1 = shift(x0, 1 << level), shift(x1, 1 << level)
            x0, x1 = x0 + jump[0] * s0 + jump[1] * s1, x1 + jump[2] * s0 + jump[3] * s1
        x0, x1 = shift(x0, 1), shift(x1, 1)
        for t in range(span):
            vs[t] = (vs[t] - x0) * inverse
            x0, x1 = f[0] * x0 + f[1] * x1, f[2] * x0 + f[3] * x1
        a0, a1 = zero, zero
        for t in range(span - 1, -1, -1):
            a0, a1 = f[0] * a0 + f[2] * a1 + vs[t], f[1] * a0 + f[3] * a1
        for level, jump in enumerate(jumps):
            s0, s1 = shift(a0, -(1 << level)), shift(a1, -(1 << level))
            a0, a1 = a0 + jump[0] * s0 + jump[2] * s1, a1 + jump[1] * s0 + jump[3] * s1
        a0, a1 = shift(a0, -1), shift(a1, -1)
        for t in range(span - 1, -1, -1):
            r = vs[t] - k0 * a0 - k1 * a1
            a0, a1 = f[0] * a0 + f[2] * a1 + vs[t], f[1] * a0 + f[3] * a1
            scratch[chunk, pl.ds(t, SUB, stride=span), :] = r
        r_ref[:, cols] = scratch[chunk]


def finish_kernel(pieces, place_ref, r_ref, w_ref, g_ref, const_ref, basis_ref, *refs):
    own_ref, here_ref, mate_ref = refs[:3]
    outs = refs[3:]
    odd = (place_ref[0] & 1) == 1
    own = own_ref[...]
    sums = [own]
    for part in range(here_ref.shape[0] // 8):
        here = here_ref[8 * part + 4 : 8 * part + 8, :]
        mate = mate_ref[8 * part : 8 * part + 4, :]
        sums.append(jnp.where(jnp.full(own.shape, odd), here, mate))
    depth = outs[0].shape[1]
    value = r_ref[...]
    for line in range(4):
        total = None
        for place, part in enumerate(sums):
            term = g_ref[line, pl.ds(4 * place, 4), :] * part
            total = term if total is None else total + term
        value = value - w_ref[line] * jnp.sum(total, axis=0, keepdims=True)
    scale = const_ref[19, 0:1, :]
    residual = (value * scale).astype(jnp.bfloat16)
    for piece in range(pieces - 1, -1, -1):
        begin = pl.multiple_of((place_ref[0] ^ piece) * depth, depth)
        outs[piece][...] = lax.dot_general(
            residual,
            basis_ref[pl.ds(begin, depth), :],
            (((1,), (1,)), ((), ())),
            preferred_element_type=F32,
        ).astype(outs[piece].dtype)


def exchange(value, axis, count):
    out = [value]
    for step in range(1, count):
        out.append(lax.ppermute(value, axis, [(a, a ^ step) for a in range(count)]))
    return out


def shards(observations, basis, eigvals, lengths, noise):
    steps, depth = observations.shape
    width = basis.shape[1]
    blocks, pieces = lax.axis_size("tm"), lax.axis_size("mode")
    me = lax.axis_index("tm").astype(jnp.int32).reshape(1)
    place = lax.axis_index("mode").astype(jnp.int32).reshape(1)
    rounds = blocks.bit_length() - 1
    vmem = pl.BlockSpec(memory_space=pltpu.VMEM)
    smem = pl.BlockSpec(memory_space=pltpu.SMEM)
    params = pltpu.CompilerParams(vmem_limit_bytes=VMEM_LIMIT)

    def shape(*dims, dtype=F32):
        return jax.ShapeDtypeStruct(dims, dtype)

    obs = exchange(observations, "mode", pieces)
    const, w, g, merge, basis, obs[0] = pl.pallas_call(
        functools.partial(coefficients_kernel, blocks),
        out_shape=(
            shape(20, SUB, width),
            shape(4, steps, width),
            shape(4, -(-4 * (rounds + 1) // SUB) * SUB, width),
            shape(-(-7 * rounds // SUB) * SUB, width),
            shape(*basis.shape, dtype=basis.dtype),
            shape(steps, depth, dtype=observations.dtype),
        ),
        in_specs=[smem] * 2 + [pl.BlockSpec(memory_space=pltpu.HBM)] * 4,
        out_specs=(vmem,) * 6,
        scratch_shapes=[
            pltpu.VMEM((1, width), F32),
            pltpu.VMEM((1, width), F32),
            pltpu.SemaphoreType.DMA((4,)),
        ],
        compiler_params=params,
        cost_estimate=pl.CostEstimate(flops=20000000, bytes_accessed=2000000, transcendentals=0),
        name="coefficients",
    )(
        me,
        noise,
        *(
            pltpu.with_memory_space_constraint(x, pltpu.HBM)
            for x in (
                eigvals.reshape(1, width),
                lengths.reshape(1, width),
                observations,
                basis,
            )
        ),
    )
    z, summary = pl.pallas_call(
        functools.partial(rotate_kernel, pieces),
        out_shape=(shape(steps, width), shape(4, width)),
        in_specs=[smem] + [vmem] * (pieces + 2),
        out_specs=(vmem,) * 2,
        compiler_params=params,
        name="rotate",
    )(place, *obs, basis, w)
    up = [(a, a + 1) for a in range(0, pieces, 2)]
    down = [(a + 1, a) for a in range(0, pieces, 2)]
    merge_mate = lax.ppermute(merge, "mode", up)
    paired = pl.pallas_call(
        pair_kernel,
        out_shape=shape(8, width),
        in_specs=[vmem] * 2,
        out_specs=vmem,
        compiler_params=params,
        name="pair",
    )(summary, lax.ppermute(summary, "mode", up))
    arrived = []
    for level in range(rounds):
        other = lax.ppermute(
            paired,
            ("tm", "mode"),
            [
                (a * pieces + b, (a ^ (1 << level)) * pieces + b)
                for a in range(blocks)
                for b in range(1, pieces, 2)
            ],
        )
        arrived.append(other)
        if level < rounds - 1:
            paired = pl.pallas_call(
                functools.partial(merge_kernel, level),
                out_shape=shape(8, width),
                in_specs=[smem] + [vmem] * 4,
                out_specs=vmem,
                compiler_params=params,
                name="merge",
            )(me, paired, other, merge, merge_mate)
    here = pl.pallas_call(
        pack_kernel,
        out_shape=shape(8 * rounds, width),
        in_specs=[vmem] * rounds,
        out_specs=vmem,
        compiler_params=params,
        name="pack",
    )(*arrived)
    mate = lax.ppermute(here, "mode", down)
    local = pl.pallas_call(
        local_kernel,
        out_shape=shape(steps, width),
        in_specs=[vmem] * 2,
        out_specs=vmem,
        scratch_shapes=[pltpu.VMEM((width // 128, steps, 128), F32)],
        compiler_params=params,
        cost_estimate=pl.CostEstimate(flops=10000000, bytes_accessed=1000000, transcendentals=0),
        name="local",
    )(z, const)
    parts = pl.pallas_call(
        functools.partial(finish_kernel, pieces),
        out_shape=(shape(steps, depth),)
        + (shape(steps, depth, dtype=jnp.bfloat16),) * (pieces - 1),
        in_specs=[smem] + [vmem] * 8,
        out_specs=(vmem,) * pieces,
        compiler_params=params,
        name="finish",
    )(place, local, w, g, const, basis, summary, here, mate)
    grad_obs = parts[0]
    for step in range(1, pieces):
        grad_obs = grad_obs + lax.ppermute(
            parts[step], "mode", [(a, a ^ step) for a in range(pieces)]
        ).astype(F32)
    return grad_obs


def solution(mesh):
    placed = (P("tm", "mode"), P(None, "mode"), P("mode"), P("mode"), P())
    return jax.shard_map(
        shards, mesh=mesh, in_specs=placed, out_specs=P("tm", "mode"), check_vma=False
    )
```

```python
import functools
import math

import jax
import jax.numpy as jnp
from jax import lax
from jax.experimental import pallas as pl
from jax.experimental.pallas import tpu as pltpu
from jax.sharding import PartitionSpec as P

F32 = jnp.float32
SUB = 8
VMEM_LIMIT = 24 * 1024 * 1024


def mat_mul(p, q):
    return (
        p[0] * q[0] + p[1] * q[2],
        p[0] * q[1] + p[1] * q[3],
        p[2] * q[0] + p[3] * q[2],
        p[2] * q[1] + p[3] * q[3],
    )


def mat_trans(p):
    return (p[0], p[2], p[1], p[3])


def mat_add(p, q):
    return tuple(a + b for a, b in zip(p, q))


def mat_sub(p, q):
    return tuple(a - b for a, b in zip(p, q))


def mat_pick(flag, p, q):
    return tuple(jnp.where(flag, a, b) for a, b in zip(p, q))


def full(s):
    return (s[0], s[1], s[1], s[2])


def congruence(s, f):
    t = (
        s[0] * f[0] + s[1] * f[2],
        s[0] * f[1] + s[1] * f[3],
        s[1] * f[0] + s[2] * f[2],
        s[1] * f[1] + s[2] * f[3],
    )
    return (f[0] * t[0] + f[2] * t[2], f[0] * t[1] + f[2] * t[3], f[1] * t[1] + f[3] * t[3])


def power(squares, exponent, like):
    one, zero = jnp.ones_like(like), jnp.zeros_like(like)
    out = None
    for bit, base in enumerate(squares):
        flag = (exponent & (1 << bit)) != 0
        if out is None:
            out = mat_pick(flag, base, (one, zero, zero, one))
        else:
            out = mat_pick(flag, mat_mul(out, base), out)
    return out


def gramian(squares, grams, count, like):
    zero = jnp.zeros_like(like)
    out = (zero, zero, zero)
    for bit, (base, gram) in enumerate(zip(squares, grams)):
        flag = (count & (1 << bit)) != 0
        out = mat_pick(flag, mat_add(gram, congruence(out, base)), out)
    return out


def steady_state(scale2, length, noise_var):
    lam = math.sqrt(3.0) / length
    decay = jnp.exp(-lam)
    twice = 2.0 * lam
    fall = jnp.exp(-twice)
    rho = scale2 / noise_var
    series = 1.0 / 604800.0
    for factor in (60480.0, 6720.0, 840.0, 120.0, 20.0, 4.0, 1.0):
        series = series * twice + 1.0 / factor
    lower = fall * twice * twice * twice * (1.0 / 6.0) * series
    loss = 1.0
    for order in (8, 7, 6, 5, 4, 3, 2):
        loss = 1.0 - lam * (1.0 / order) * loss
    loss = lam * loss
    q00 = rho * lower
    q01 = 2.0 * rho * lam * lam * fall
    q11 = rho * (lower + twice * fall)
    slope = decay * lam
    tilt = loss + slope
    g0 = q00 * tilt * tilt + 2.0 * slope * q01 * tilt + slope * slope * q11
    g1 = slope * q01 - decay * (1.0 - lam) * q00
    loss2 = loss * loss
    c2 = decay * decay
    u = (2.0 * decay * loss2 - g1) / c2
    v = (loss2 * loss2 + g0) / c2
    root = jnp.sqrt(v * (v + 4.0 * u + 16.0))
    product = 4.0 * v / (v + root + jnp.sqrt(2.0 * v * (v + 2.0 * u + root)))
    total = 0.5 * (jnp.sqrt(u * u + 4.0 * u - 2.0 * v + 2.0 * root) - u)
    gain0 = total - 2.0 * loss
    gain1 = (product - loss2 - gain0 * tilt) / slope
    inverse = (1.0 - total + product) / c2
    inn = c2 / (1.0 - total + product)
    closed = (1.0 + slope - loss - gain0, slope, -slope - gain1, decay * (1.0 - lam))
    p00 = inn * ((1.0 - lam) * gain0 - lam * gain1) / decay
    p01 = inn * (lam * gain0 + (1.0 + lam) * gain1) / decay
    p11 = (
        p01 * (loss * (1.0 + decay) + 2.0 * slope * slope)
        + slope * decay * (1.0 + lam) * p00
        - q01
        + gain0 * gain1 * inn
    ) / (slope * decay * (1.0 - lam))
    return closed, gain0, gain1, inverse, (rho - p00, -p01, rho - p11)


def coefficients_kernel(blocks, me_ref, noise_ref, *refs):
    arguments, (const_ref, w_ref, g_ref, merge_ref, basis_ref, obs_ref) = (
        refs[:4],
        refs[4:10],
    )
    scale_ref, length_ref, sems = refs[10:]
    copies = [
        pltpu.make_async_copy(source, target, sems.at[k])
        for k, (source, target) in enumerate(
            zip(arguments, (scale_ref, length_ref, obs_ref, basis_ref))
        )
    ]
    for copy in copies:
        copy.start()
    for copy in copies[:2]:
        copy.wait()
    steps = w_ref.shape[1]
    width = scale_ref.shape[1]
    tile = (SUB, width)
    me = me_ref[0]
    scale2 = jnp.broadcast_to(scale_ref[...], tile)
    length = jnp.broadcast_to(length_ref[...], tile)
    noise_var = jnp.full(tile, noise_ref[0], F32)
    closed, gain0, gain1, inverse, excess = steady_state(scale2, length, noise_var)
    zero = jnp.zeros(tile, F32)

    squares, grams = [closed], [(inverse, zero, zero)]
    doublings = (steps * blocks).bit_length() - 1
    for _ in range(doublings):
        base = squares[-1]
        grams.append(mat_add(grams[-1], congruence(grams[-1], base)))
        squares.append(mat_mul(base, base))
    local = steps.bit_length() - 1
    consts = closed + (gain0, gain1, inverse) + squares[3] + squares[4] + squares[5]
    for place, value in enumerate(consts):
        const_ref[place] = value
    const_ref[len(consts)] = -1.0 / noise_var
    for level in range(blocks.bit_length() - 1):
        for place, value in enumerate(squares[local + level] + grams[local + level]):
            merge_ref[7 * level + place : 7 * level + place + 1, :] = value[0:1, :]

    row = lax.broadcasted_iota(jnp.int32, tile, 0)
    small, gram_small = squares[:3], grams[:3]
    behind = power(small, 7 - row, zero)
    gram = gramian(small, gram_small, 7 - row, zero)
    eight, gram_eight = squares[3], grams[3]
    parts = steps // SUB
    for part in range(parts - 1, -1, -1):
        rows = pl.ds(part * SUB, SUB)
        w_ref[0, rows, :] = behind[0] * gain0 + behind[1] * gain1
        w_ref[1, rows, :] = behind[2] * gain0 + behind[3] * gain1
        k0 = gain0 * gram[0] + gain1 * gram[1]
        k1 = gain0 * gram[1] + gain1 * gram[2]
        w_ref[2, rows, :] = inverse - (k0 * closed[0] + k1 * closed[2])
        w_ref[3, rows, :] = -(k0 * closed[1] + k1 * closed[3])
        if part:
            behind = mat_mul(behind, eight)
            gram = mat_add(gram_eight, congruence(gram, eight))
    ahead = power(small, row, zero)
    for part in range(parts):
        rows = pl.ds(part * SUB, SUB)
        u0, u1 = w_ref[2, rows, :], w_ref[3, rows, :]
        w_ref[2, rows, :] = u0 * ahead[0] + u1 * ahead[2]
        w_ref[3, rows, :] = u0 * ahead[1] + u1 * ahead[3]
        if part < parts - 1:
            ahead = mat_mul(ahead, eight)

    s = grams[-1]
    left = (
        1.0 + excess[0] * s[0] + excess[1] * s[1],
        excess[0] * s[1] + excess[1] * s[2],
        excess[1] * s[0] + excess[2] * s[1],
        1.0 + excess[1] * s[1] + excess[2] * s[2],
    )
    determ = 1.0 / (left[0] * left[3] - left[1] * left[2])
    start = mat_mul((left[3], -left[1], -left[2], left[0]), full(excess))
    start = tuple(x * determ for x in start)
    block_squares, block_grams = squares[local:-1], grams[local:-1]
    mine = jnp.full(tile, me, jnp.int32)
    to_me = power(block_squares, mine, zero)
    rest = full(gramian(block_squares, block_grams, blocks - 1 - mine, zero))
    to_state = mat_mul(to_me, start)
    to_adjoint = mat_mul(mat_mul(rest, mat_mul(to_me, block_squares[0])), start)
    for group in range(g_ref.shape[1] // SUB):
        rows = row + group * SUB
        kind = rows & 3
        line = rows >> 2
        span = jnp.where(line == 0, 1, jnp.left_shift(1, jnp.maximum(line - 1, 0)))
        near_me = jnp.where(line == 0, mine, mine ^ span)
        front = jnp.minimum((near_me // span) * span, blocks - 1)
        back = jnp.minimum(front + span - 1, blocks - 1)
        before, after = back < me, front > me
        gap = jnp.where(before, me - 1 - back, jnp.where(after, front - 1 - me, 0))
        reach = jnp.where(before, me - back, jnp.where(after, back - me, 0))
        near = power(block_squares, gap, zero)
        far = power(block_squares, reach, zero)
        origin = mat_trans(power(block_squares, front, zero))
        left_over = full(gramian(block_squares, block_grams, blocks - 1 - back, zero))
        end = mat_trans(mat_mul(power(block_squares, back, zero), block_squares[0]))
        first = mat_mul(end, left_over)
        state_b = mat_sub(mat_pick(before, near, (zero,) * 4), mat_mul(to_state, first))
        state_l = mat_mul(to_state, origin)
        cross = mat_pick(after, mat_mul(mat_trans(far), left_over), mat_mul(rest, far))
        adjoint_b = mat_sub(mat_mul(to_adjoint, first), cross)
        adjoint_l = mat_sub(
            mat_pick(after, mat_trans(near), (zero,) * 4), mat_mul(to_adjoint, origin)
        )
        place = pl.ds(group * SUB, SUB)
        for output, (from_b, from_l) in enumerate(
            ((adjoint_b[:2], adjoint_l[:2]), (adjoint_b[2:], adjoint_l[2:]),
             (state_b[:2], state_l[:2]), (state_b[2:], state_l[2:]))
        ):
            g_ref[output, place, :] = jnp.where(
                kind < 2,
                jnp.where(kind == 0, from_b[0], from_b[1]),
                jnp.where(kind == 2, from_l[0], from_l[1]),
            )
    for copy in copies[2:]:
        copy.wait()


def rotate_kernel(pieces, place_ref, *refs):
    obs_refs = refs[:pieces]
    basis_ref, w_ref, z_ref, sum_ref = refs[pieces:]
    depth = obs_refs[0].shape[1]
    z = None
    for piece, obs_ref in enumerate(obs_refs):
        begin = pl.multiple_of((place_ref[0] ^ piece) * depth, depth)
        term = jnp.dot(
            obs_ref[...], basis_ref[pl.ds(begin, depth), :], preferred_element_type=F32
        )
        z = term if z is None else z + term
    z_ref[...] = z
    for line in range(4):
        sum_ref[line : line + 1, :] = jnp.sum(w_ref[line] * z, axis=0, keepdims=True)


def pair_kernel(own_ref, mate_ref, out_ref):
    out_ref[0:4, :] = own_ref[...]
    out_ref[4:8, :] = mate_ref[...]


def merge_kernel(level, me_ref, own_ref, other_ref, merge_ref, mate_ref, out_ref):
    own, other = own_ref[...], other_ref[...]
    lower = jnp.full(own.shape, (me_ref[0] >> level) & 1, jnp.int32) == 0
    left, right = jnp.where(lower, own, other), jnp.where(lower, other, own)
    for at, ref in ((0, merge_ref), (4, mate_ref)):
        f00, f01, f10, f11, s00, s01, s11 = (
            ref[7 * level + k : 7 * level + k + 1, :] for k in range(7)
        )
        b0, b1 = left[at : at + 1, :], left[at + 1 : at + 2, :]
        a0 = right[at + 2 : at + 3, :] - s00 * b0 - s01 * b1
        a1 = right[at + 3 : at + 4, :] - s01 * b0 - s11 * b1
        out_ref[at : at + 1, :] = right[at : at + 1, :] + f00 * b0 + f01 * b1
        out_ref[at + 1 : at + 2, :] = right[at + 1 : at + 2, :] + f10 * b0 + f11 * b1
        out_ref[at + 2 : at + 3, :] = left[at + 2 : at + 3, :] + f00 * a0 + f10 * a1
        out_ref[at + 3 : at + 4, :] = left[at + 3 : at + 4, :] + f01 * a0 + f11 * a1


def pack_kernel(*refs):
    for place, ref in enumerate(refs[:-1]):
        refs[-1][8 * place : 8 * place + 4, :] = ref[4:8, :]
        refs[-1][8 * place + 4 : 8 * place + 8, :] = ref[0:4, :]


def shift(value, by):
    rows = value.shape[0]
    row = lax.broadcasted_iota(jnp.int32, value.shape, 0)
    keep = row >= by if by > 0 else row < rows + by
    return jnp.where(keep, pltpu.roll(value, by % rows, 0), 0.0)


def local_kernel(z_ref, const_ref, r_ref, scratch):
    steps, width = z_ref.shape
    span = steps // SUB
    lanes = 128
    for chunk in range(width // lanes):
        cols = pl.ds(chunk * lanes, lanes)
        scratch[chunk] = z_ref[:, cols]
    for chunk in range(width // lanes):
        cols = pl.ds(chunk * lanes, lanes)
        const = [const_ref[k, :, cols] for k in range(19)]
        f, (k0, k1, inverse) = const[0:4], const[4:7]
        jumps = (const[7:11], const[11:15], const[15:19])
        zero = jnp.zeros((SUB, lanes), F32)
        x0, x1 = zero, zero
        vs = []
        for t in range(span):
            z = scratch[chunk, pl.ds(t, SUB, stride=span), :]
            vs.append(z - x0)
            x0, x1 = f[0] * x0 + f[1] * x1 + k0 * z, f[2] * x0 + f[3] * x1 + k1 * z
        for level, jump in enumerate(jumps):
            s0, s1 = shift(x0, 1 << level), shift(x1, 1 << level)
            x0, x1 = x0 + jump[0] * s0 + jump[1] * s1, x1 + jump[2] * s0 + jump[3] * s1
        x0, x1 = shift(x0, 1), shift(x1, 1)
        for t in range(span):
            vs[t] = (vs[t] - x0) * inverse
            x0, x1 = f[0] * x0 + f[1] * x1, f[2] * x0 + f[3] * x1
        a0, a1 = zero, zero
        for t in range(span - 1, -1, -1):
            a0, a1 = f[0] * a0 + f[2] * a1 + vs[t], f[1] * a0 + f[3] * a1
        for level, jump in enumerate(jumps):
            s0, s1 = shift(a0, -(1 << level)), shift(a1, -(1 << level))
            a0, a1 = a0 + jump[0] * s0 + jump[2] * s1, a1 + jump[1] * s0 + jump[3] * s1
        a0, a1 = shift(a0, -1), shift(a1, -1)
        for t in range(span - 1, -1, -1):
            r = vs[t] - k0 * a0 - k1 * a1
            a0, a1 = f[0] * a0 + f[2] * a1 + vs[t], f[1] * a0 + f[3] * a1
            scratch[chunk, pl.ds(t, SUB, stride=span), :] = r
        r_ref[:, cols] = scratch[chunk]


def finish_kernel(pieces, place_ref, r_ref, w_ref, g_ref, const_ref, basis_ref, *refs):
    own_ref, here_ref, mate_ref = refs[:3]
    outs = refs[3:]
    odd = (place_ref[0] & 1) == 1
    own = own_ref[...]
    sums = [own]
    for part in range(here_ref.shape[0] // 8):
        here = here_ref[8 * part + 4 : 8 * part + 8, :]
        mate = mate_ref[8 * part : 8 * part + 4, :]
        sums.append(jnp.where(jnp.full(own.shape, odd), here, mate))
    depth = outs[0].shape[1]
    value = r_ref[...]
    for line in range(4):
        total = None
        for place, part in enumerate(sums):
            term = g_ref[line, pl.ds(4 * place, 4), :] * part
            total = term if total is None else total + term
        value = value - w_ref[line] * jnp.sum(total, axis=0, keepdims=True)
    scale = const_ref[19, 0:1, :]
    residual = (value * scale).astype(jnp.bfloat16)
    for piece in range(pieces - 1, -1, -1):
        begin = pl.multiple_of((place_ref[0] ^ piece) * depth, depth)
        outs[piece][...] = lax.dot_general(
            residual,
            basis_ref[pl.ds(begin, depth), :],
            (((1,), (1,)), ((), ())),
            preferred_element_type=F32,
        ).astype(outs[piece].dtype)


def exchange(value, axis, count):
    out = [value]
    for step in range(1, count):
        out.append(lax.ppermute(value, axis, [(a, a ^ step) for a in range(count)]))
    return out


def shards(observations, basis, eigvals, lengths, noise):
    steps, depth = observations.shape
    width = basis.shape[1]
    blocks, pieces = lax.axis_size("tm"), lax.axis_size("mode")
    me = lax.axis_index("tm").astype(jnp.int32).reshape(1)
    place = lax.axis_index("mode").astype(jnp.int32).reshape(1)
    rounds = blocks.bit_length() - 1
    vmem = pl.BlockSpec(memory_space=pltpu.VMEM)
    smem = pl.BlockSpec(memory_space=pltpu.SMEM)
    params = pltpu.CompilerParams(vmem_limit_bytes=VMEM_LIMIT)

    def shape(*dims, dtype=F32):
        return jax.ShapeDtypeStruct(dims, dtype)

    obs = exchange(observations, "mode", pieces)
    const, w, g, merge, basis, obs[0] = pl.pallas_call(
        functools.partial(coefficients_kernel, blocks),
        out_shape=(
            shape(20, SUB, width),
            shape(4, steps, width),
            shape(4, -(-4 * (rounds + 1) // SUB) * SUB, width),
            shape(-(-7 * rounds // SUB) * SUB, width),
            shape(*basis.shape, dtype=basis.dtype),
            shape(steps, depth, dtype=observations.dtype),
        ),
        in_specs=[smem] * 2 + [pl.BlockSpec(memory_space=pltpu.HBM)] * 4,
        out_specs=(vmem,) * 6,
        scratch_shapes=[
            pltpu.VMEM((1, width), F32),
            pltpu.VMEM((1, width), F32),
            pltpu.SemaphoreType.DMA((4,)),
        ],
        compiler_params=params,
        cost_estimate=pl.CostEstimate(flops=20000000, bytes_accessed=2000000, transcendentals=0),
        name="coefficients",
    )(
        me,
        noise,
        *(
            pltpu.with_memory_space_constraint(x, pltpu.HBM)
            for x in (
                eigvals.reshape(1, width),
                lengths.reshape(1, width),
                observations,
                basis,
            )
        ),
    )
    z, summary = pl.pallas_call(
        functools.partial(rotate_kernel, pieces),
        out_shape=(shape(steps, width), shape(4, width)),
        in_specs=[smem] + [vmem] * (pieces + 2),
        out_specs=(vmem,) * 2,
        compiler_params=params,
        name="rotate",
    )(place, *obs, basis, w)
    swap = [(a, a ^ 1) for a in range(pieces)]
    merge_mate = lax.ppermute(merge, "mode", swap)
    paired = pl.pallas_call(
        pair_kernel,
        out_shape=shape(8, width),
        in_specs=[vmem] * 2,
        out_specs=vmem,
        compiler_params=params,
        name="pair",
    )(summary, lax.ppermute(summary, "mode", swap))
    arrived = []
    for level in range(rounds):
        other = lax.ppermute(
            paired,
            ("tm", "mode"),
            [
                (a * pieces + b, (a ^ ((b & 1) << level)) * pieces + b)
                for a in range(blocks)
                for b in range(pieces)
            ],
        )
        arrived.append(other)
        if level < rounds - 1:
            paired = pl.pallas_call(
                functools.partial(merge_kernel, level),
                out_shape=shape(8, width),
                in_specs=[smem] + [vmem] * 4,
                out_specs=vmem,
                compiler_params=params,
                name="merge",
            )(me, paired, other, merge, merge_mate)
    here = pl.pallas_call(
        pack_kernel,
        out_shape=shape(8 * rounds, width),
        in_specs=[vmem] * rounds,
        out_specs=vmem,
        compiler_params=params,
        name="pack",
    )(*arrived)
    mate = lax.ppermute(here, "mode", swap)
    local = pl.pallas_call(
        local_kernel,
        out_shape=shape(steps, width),
        in_specs=[vmem] * 2,
        out_specs=vmem,
        scratch_shapes=[pltpu.VMEM((width // 128, steps, 128), F32)],
        compiler_params=params,
        cost_estimate=pl.CostEstimate(flops=10000000, bytes_accessed=1000000, transcendentals=0),
        name="local",
    )(z, const)
    parts = pl.pallas_call(
        functools.partial(finish_kernel, pieces),
        out_shape=(shape(steps, depth),)
        + (shape(steps, depth, dtype=jnp.bfloat16),) * (pieces - 1),
        in_specs=[smem] + [vmem] * 8,
        out_specs=(vmem,) * pieces,
        compiler_params=params,
        name="finish",
    )(place, local, w, g, const, basis, summary, here, mate)
    grad_obs = parts[0]
    for step in range(1, pieces):
        grad_obs = grad_obs + lax.ppermute(
            parts[step], "mode", [(a, a ^ step) for a in range(pieces)]
        ).astype(F32)
    return grad_obs


def solution(mesh):
    placed = (P("tm", "mode"), P(None, "mode"), P("mode"), P("mode"), P())
    return jax.shard_map(
        shards, mesh=mesh, in_specs=placed, out_specs=P("tm", "mode"), check_vma=False
    )
```

```python
import functools
import math

import jax
import jax.numpy as jnp
from jax import lax
from jax.experimental import pallas as pl
from jax.experimental.pallas import tpu as pltpu
from jax.sharding import PartitionSpec as P

F32 = jnp.float32
SUB = 8
VMEM_LIMIT = 24 * 1024 * 1024


def mat_mul(p, q):
    return (
        p[0] * q[0] + p[1] * q[2],
        p[0] * q[1] + p[1] * q[3],
        p[2] * q[0] + p[3] * q[2],
        p[2] * q[1] + p[3] * q[3],
    )


def mat_trans(p):
    return (p[0], p[2], p[1], p[3])


def mat_add(p, q):
    return tuple(a + b for a, b in zip(p, q))


def mat_sub(p, q):
    return tuple(a - b for a, b in zip(p, q))


def mat_pick(flag, p, q):
    return tuple(jnp.where(flag, a, b) for a, b in zip(p, q))


def full(s):
    return (s[0], s[1], s[1], s[2])


def congruence(s, f):
    t = (
        s[0] * f[0] + s[1] * f[2],
        s[0] * f[1] + s[1] * f[3],
        s[1] * f[0] + s[2] * f[2],
        s[1] * f[1] + s[2] * f[3],
    )
    return (f[0] * t[0] + f[2] * t[2], f[0] * t[1] + f[2] * t[3], f[1] * t[1] + f[3] * t[3])


def power(squares, exponent, like):
    one, zero = jnp.ones_like(like), jnp.zeros_like(like)
    out = None
    for bit, base in enumerate(squares):
        flag = (exponent & (1 << bit)) != 0
        if out is None:
            out = mat_pick(flag, base, (one, zero, zero, one))
        else:
            out = mat_pick(flag, mat_mul(out, base), out)
    return out


def gramian(squares, grams, count, like):
    zero = jnp.zeros_like(like)
    out = (zero, zero, zero)
    for bit, (base, gram) in enumerate(zip(squares, grams)):
        flag = (count & (1 << bit)) != 0
        out = mat_pick(flag, mat_add(gram, congruence(out, base)), out)
    return out


def steady_state(scale2, length, noise_var):
    lam = math.sqrt(3.0) / length
    decay = jnp.exp(-lam)
    twice = 2.0 * lam
    fall = jnp.exp(-twice)
    rho = scale2 / noise_var
    series = 1.0 / 604800.0
    for factor in (60480.0, 6720.0, 840.0, 120.0, 20.0, 4.0, 1.0):
        series = series * twice + 1.0 / factor
    lower = fall * twice * twice * twice * (1.0 / 6.0) * series
    loss = 1.0
    for order in (8, 7, 6, 5, 4, 3, 2):
        loss = 1.0 - lam * (1.0 / order) * loss
    loss = lam * loss
    q00 = rho * lower
    q01 = 2.0 * rho * lam * lam * fall
    q11 = rho * (lower + twice * fall)
    slope = decay * lam
    tilt = loss + slope
    g0 = q00 * tilt * tilt + 2.0 * slope * q01 * tilt + slope * slope * q11
    g1 = slope * q01 - decay * (1.0 - lam) * q00
    loss2 = loss * loss
    c2 = decay * decay
    u = (2.0 * decay * loss2 - g1) / c2
    v = (loss2 * loss2 + g0) / c2
    root = jnp.sqrt(v * (v + 4.0 * u + 16.0))
    product = 4.0 * v / (v + root + jnp.sqrt(2.0 * v * (v + 2.0 * u + root)))
    total = 0.5 * (jnp.sqrt(u * u + 4.0 * u - 2.0 * v + 2.0 * root) - u)
    gain0 = total - 2.0 * loss
    gain1 = (product - loss2 - gain0 * tilt) / slope
    inverse = (1.0 - total + product) / c2
    inn = c2 / (1.0 - total + product)
    closed = (1.0 + slope - loss - gain0, slope, -slope - gain1, decay * (1.0 - lam))
    p00 = inn * ((1.0 - lam) * gain0 - lam * gain1) / decay
    p01 = inn * (lam * gain0 + (1.0 + lam) * gain1) / decay
    p11 = (
        p01 * (loss * (1.0 + decay) + 2.0 * slope * slope)
        + slope * decay * (1.0 + lam) * p00
        - q01
        + gain0 * gain1 * inn
    ) / (slope * decay * (1.0 - lam))
    return closed, gain0, gain1, inverse, (rho - p00, -p01, rho - p11)


def coefficients_kernel(blocks, me_ref, noise_ref, *refs):
    arguments, (const_ref, w_ref, g_ref, merge_ref, basis_ref, obs_ref) = (
        refs[:4],
        refs[4:10],
    )
    scale_ref, length_ref, sems = refs[10:]
    copies = [
        pltpu.make_async_copy(source, target, sems.at[k])
        for k, (source, target) in enumerate(
            zip(arguments, (scale_ref, length_ref, obs_ref, basis_ref))
        )
    ]
    for copy in copies:
        copy.start()
    for copy in copies[:2]:
        copy.wait()
    steps = w_ref.shape[1]
    width = scale_ref.shape[1]
    tile = (SUB, width)
    me = me_ref[0]
    scale2 = jnp.broadcast_to(scale_ref[...], tile)
    length = jnp.broadcast_to(length_ref[...], tile)
    noise_var = jnp.full(tile, noise_ref[0], F32)
    closed, gain0, gain1, inverse, excess = steady_state(scale2, length, noise_var)
    zero = jnp.zeros(tile, F32)

    squares, grams = [closed], [(inverse, zero, zero)]
    doublings = (steps * blocks).bit_length() - 1
    for _ in range(doublings):
        base = squares[-1]
        grams.append(mat_add(grams[-1], congruence(grams[-1], base)))
        squares.append(mat_mul(base, base))
    local = steps.bit_length() - 1
    consts = closed + (gain0, gain1, inverse) + squares[3] + squares[4] + squares[5]
    for place, value in enumerate(consts):
        const_ref[place] = value
    const_ref[len(consts)] = -1.0 / noise_var
    for level in range(blocks.bit_length() - 1):
        for place, value in enumerate(squares[local + level] + grams[local + level]):
            merge_ref[7 * level + place : 7 * level + place + 1, :] = value[0:1, :]

    row = lax.broadcasted_iota(jnp.int32, tile, 0)
    small, gram_small = squares[:3], grams[:3]
    behind = power(small, 7 - row, zero)
    gram = gramian(small, gram_small, 7 - row, zero)
    eight, gram_eight = squares[3], grams[3]
    parts = steps // SUB
    for part in range(parts - 1, -1, -1):
        rows = pl.ds(part * SUB, SUB)
        w_ref[0, rows, :] = behind[0] * gain0 + behind[1] * gain1
        w_ref[1, rows, :] = behind[2] * gain0 + behind[3] * gain1
        k0 = gain0 * gram[0] + gain1 * gram[1]
        k1 = gain0 * gram[1] + gain1 * gram[2]
        w_ref[2, rows, :] = inverse - (k0 * closed[0] + k1 * closed[2])
        w_ref[3, rows, :] = -(k0 * closed[1] + k1 * closed[3])
        if part:
            behind = mat_mul(behind, eight)
            gram = mat_add(gram_eight, congruence(gram, eight))
    ahead = power(small, row, zero)
    for part in range(parts):
        rows = pl.ds(part * SUB, SUB)
        u0, u1 = w_ref[2, rows, :], w_ref[3, rows, :]
        w_ref[2, rows, :] = u0 * ahead[0] + u1 * ahead[2]
        w_ref[3, rows, :] = u0 * ahead[1] + u1 * ahead[3]
        if part < parts - 1:
            ahead = mat_mul(ahead, eight)

    s = grams[-1]
    left = (
        1.0 + excess[0] * s[0] + excess[1] * s[1],
        excess[0] * s[1] + excess[1] * s[2],
        excess[1] * s[0] + excess[2] * s[1],
        1.0 + excess[1] * s[1] + excess[2] * s[2],
    )
    determ = 1.0 / (left[0] * left[3] - left[1] * left[2])
    start = mat_mul((left[3], -left[1], -left[2], left[0]), full(excess))
    start = tuple(x * determ for x in start)
    block_squares, block_grams = squares[local:-1], grams[local:-1]
    mine = jnp.full(tile, me, jnp.int32)
    to_me = power(block_squares, mine, zero)
    rest = full(gramian(block_squares, block_grams, blocks - 1 - mine, zero))
    to_state = mat_mul(to_me, start)
    to_adjoint = mat_mul(mat_mul(rest, mat_mul(to_me, block_squares[0])), start)
    for group in range(g_ref.shape[1] // SUB):
        rows = row + group * SUB
        kind = rows & 3
        line = rows >> 2
        span = jnp.where(line < 4, 1, jnp.left_shift(1, jnp.maximum(line - 2, 0)))
        near_me = mine ^ jnp.where(line < 4, line, span)
        front = jnp.minimum((near_me // span) * span, blocks - 1)
        back = jnp.minimum(front + span - 1, blocks - 1)
        before, after = back < me, front > me
        gap = jnp.where(before, me - 1 - back, jnp.where(after, front - 1 - me, 0))
        reach = jnp.where(before, me - back, jnp.where(after, back - me, 0))
        near = power(block_squares, gap, zero)
        far = power(block_squares, reach, zero)
        origin = mat_trans(power(block_squares, front, zero))
        left_over = full(gramian(block_squares, block_grams, blocks - 1 - back, zero))
        end = mat_trans(mat_mul(power(block_squares, back, zero), block_squares[0]))
        first = mat_mul(end, left_over)
        state_b = mat_sub(mat_pick(before, near, (zero,) * 4), mat_mul(to_state, first))
        state_l = mat_mul(to_state, origin)
        cross = mat_pick(after, mat_mul(mat_trans(far), left_over), mat_mul(rest, far))
        adjoint_b = mat_sub(mat_mul(to_adjoint, first), cross)
        adjoint_l = mat_sub(
            mat_pick(after, mat_trans(near), (zero,) * 4), mat_mul(to_adjoint, origin)
        )
        place = pl.ds(group * SUB, SUB)
        for output, (from_b, from_l) in enumerate(
            ((adjoint_b[:2], adjoint_l[:2]), (adjoint_b[2:], adjoint_l[2:]),
             (state_b[:2], state_l[:2]), (state_b[2:], state_l[2:]))
        ):
            g_ref[output, place, :] = jnp.where(
                kind < 2,
                jnp.where(kind == 0, from_b[0], from_b[1]),
                jnp.where(kind == 2, from_l[0], from_l[1]),
            )
    for copy in copies[2:]:
        copy.wait()


def rotate_kernel(first, place_ref, *refs):
    pieces, others = first
    obs_refs, (basis_ref, *refs) = refs[: len(pieces)], refs[len(pieces) :]
    depth = obs_refs[0].shape[1]
    z = None if others is None else refs[0][...]
    for piece, obs_ref in zip(pieces, obs_refs):
        begin = pl.multiple_of((place_ref[0] ^ piece) * depth, depth)
        term = jnp.dot(
            obs_ref[...], basis_ref[pl.ds(begin, depth), :], preferred_element_type=F32
        )
        z = term if z is None else z + term
    if others is None:
        refs[0][...] = z
        return
    _, w_ref, z_ref, sum_ref = refs
    z_ref[...] = z
    for line in range(4):
        sum_ref[line : line + 1, :] = jnp.sum(w_ref[line] * z, axis=0, keepdims=True)


def merge(level, me, own, other, merge_ref):
    lower = jnp.full(own.shape, (me >> level) & 1, jnp.int32) == 0
    left, right = jnp.where(lower, own, other), jnp.where(lower, other, own)
    f00, f01, f10, f11, s00, s01, s11 = (
        merge_ref[7 * level + k : 7 * level + k + 1, :] for k in range(7)
    )
    b0, b1 = left[0:1, :], left[1:2, :]
    a0 = right[2:3, :] - s00 * b0 - s01 * b1
    a1 = right[3:4, :] - s01 * b0 - s11 * b1
    return jnp.concatenate(
        (
            right[0:1, :] + f00 * b0 + f01 * b1,
            right[1:2, :] + f10 * b0 + f11 * b1,
            left[2:3, :] + f00 * a0 + f10 * a1,
            left[3:4, :] + f01 * a0 + f11 * a1,
        ),
        axis=0,
    )


def merge_kernel(level, me_ref, merge_ref, *refs):
    *parts, out_ref = refs
    me = me_ref[0]
    parts = [ref[...] for ref in parts]
    if level:
        out_ref[...] = merge(level, me, parts[0], parts[1], merge_ref)
    else:
        near = merge(0, me, parts[0], parts[1], merge_ref)
        far = merge(0, me, parts[2], parts[3], merge_ref)
        out_ref[...] = merge(1, me, near, far, merge_ref)


def shift(value, by):
    rows = value.shape[0]
    row = lax.broadcasted_iota(jnp.int32, value.shape, 0)
    keep = row >= by if by > 0 else row < rows + by
    return jnp.where(keep, pltpu.roll(value, by % rows, 0), 0.0)


def local_kernel(z_ref, const_ref, r_ref, scratch):
    steps, width = z_ref.shape
    span = steps // SUB
    lanes = 128
    for chunk in range(width // lanes):
        cols = pl.ds(chunk * lanes, lanes)
        scratch[chunk] = z_ref[:, cols]
    for chunk in range(width // lanes):
        cols = pl.ds(chunk * lanes, lanes)
        const = [const_ref[k, :, cols] for k in range(19)]
        f, (k0, k1, inverse) = const[0:4], const[4:7]
        jumps = (const[7:11], const[11:15], const[15:19])
        zero = jnp.zeros((SUB, lanes), F32)
        x0, x1 = zero, zero
        vs = []
        for t in range(span):
            z = scratch[chunk, pl.ds(t, SUB, stride=span), :]
            vs.append(z - x0)
            x0, x1 = f[0] * x0 + f[1] * x1 + k0 * z, f[2] * x0 + f[3] * x1 + k1 * z
        for level, jump in enumerate(jumps):
            s0, s1 = shift(x0, 1 << level), shift(x1, 1 << level)
            x0, x1 = x0 + jump[0] * s0 + jump[1] * s1, x1 + jump[2] * s0 + jump[3] * s1
        x0, x1 = shift(x0, 1), shift(x1, 1)
        for t in range(span):
            vs[t] = (vs[t] - x0) * inverse
            x0, x1 = f[0] * x0 + f[1] * x1, f[2] * x0 + f[3] * x1
        a0, a1 = zero, zero
        for t in range(span - 1, -1, -1):
            a0, a1 = f[0] * a0 + f[2] * a1 + vs[t], f[1] * a0 + f[3] * a1
        for level, jump in enumerate(jumps):
            s0, s1 = shift(a0, -(1 << level)), shift(a1, -(1 << level))
            a0, a1 = a0 + jump[0] * s0 + jump[2] * s1, a1 + jump[1] * s0 + jump[3] * s1
        a0, a1 = shift(a0, -1), shift(a1, -1)
        for t in range(span - 1, -1, -1):
            r = vs[t] - k0 * a0 - k1 * a1
            a0, a1 = f[0] * a0 + f[2] * a1 + vs[t], f[1] * a0 + f[3] * a1
            scratch[chunk, pl.ds(t, SUB, stride=span), :] = r
        r_ref[:, cols] = scratch[chunk]


def rotate_back(residual, pieces, place_ref, basis_ref, outs):
    depth = outs[0].shape[1]
    for piece, out_ref in zip(pieces, outs):
        begin = pl.multiple_of((place_ref[0] ^ piece) * depth, depth)
        out_ref[...] = lax.dot_general(
            residual,
            basis_ref[pl.ds(begin, depth), :],
            (((1,), (1,)), ((), ())),
            preferred_element_type=F32,
        ).astype(out_ref.dtype)


def finish_kernel(pieces, place_ref, r_ref, w_ref, g_ref, const_ref, basis_ref, *refs):
    *sums, residual_ref = refs[: -len(pieces)]
    value = r_ref[...]
    for line in range(4):
        total = None
        for place, sum_ref in enumerate(sums):
            term = g_ref[line, pl.ds(4 * place, 4), :] * sum_ref[...]
            total = term if total is None else total + term
        value = value - w_ref[line] * jnp.sum(total, axis=0, keepdims=True)
    scale = const_ref[19, 0:1, :]
    residual = (value * scale).astype(jnp.bfloat16)
    residual_ref[...] = residual
    rotate_back(residual, pieces, place_ref, basis_ref, refs[-len(pieces) :])


def rest_kernel(pieces, place_ref, residual_ref, basis_ref, *outs):
    rotate_back(residual_ref[...], pieces, place_ref, basis_ref, outs)


def exchange(value, axis, count):
    out = [value]
    for step in range(1, count):
        out.append(lax.ppermute(value, axis, [(a, a ^ step) for a in range(count)]))
    return out


def shards(observations, basis, eigvals, lengths, noise):
    steps, depth = observations.shape
    width = basis.shape[1]
    blocks, pieces = lax.axis_size("tm"), lax.axis_size("mode")
    me = lax.axis_index("tm").astype(jnp.int32).reshape(1)
    place = lax.axis_index("mode").astype(jnp.int32).reshape(1)
    rounds = blocks.bit_length() - 1
    vmem = pl.BlockSpec(memory_space=pltpu.VMEM)
    smem = pl.BlockSpec(memory_space=pltpu.SMEM)
    params = pltpu.CompilerParams(vmem_limit_bytes=VMEM_LIMIT)

    def shape(*dims, dtype=F32):
        return jax.ShapeDtypeStruct(dims, dtype)

    obs = exchange(observations, "mode", pieces)
    const, w, g, merges, basis, obs[0] = pl.pallas_call(
        functools.partial(coefficients_kernel, blocks),
        out_shape=(
            shape(20, SUB, width),
            shape(4, steps, width),
            shape(4, -(-4 * (rounds + 2) // SUB) * SUB, width),
            shape(-(-7 * rounds // SUB) * SUB, width),
            shape(*basis.shape, dtype=basis.dtype),
            shape(steps, depth, dtype=observations.dtype),
        ),
        in_specs=[smem] * 2 + [pl.BlockSpec(memory_space=pltpu.HBM)] * 4,
        out_specs=(vmem,) * 6,
        scratch_shapes=[
            pltpu.VMEM((1, width), F32),
            pltpu.VMEM((1, width), F32),
            pltpu.SemaphoreType.DMA((4,)),
        ],
        compiler_params=params,
        cost_estimate=pl.CostEstimate(flops=20000000, bytes_accessed=2000000, transcendentals=0),
        name="coefficients",
    )(
        me,
        noise,
        *(
            pltpu.with_memory_space_constraint(x, pltpu.HBM)
            for x in (
                eigvals.reshape(1, width),
                lengths.reshape(1, width),
                observations,
                basis,
            )
        ),
    )
    last = min(2, pieces - 1)
    early = [piece for piece in range(pieces) if piece != last]
    z = pl.pallas_call(
        functools.partial(rotate_kernel, (early, None)),
        out_shape=shape(steps, width),
        in_specs=[smem] + [vmem] * pieces,
        out_specs=vmem,
        compiler_params=params,
        name="rotate_early",
    )(place, *(obs[piece] for piece in early), basis)
    z, summary = pl.pallas_call(
        functools.partial(rotate_kernel, ([last], early)),
        out_shape=(shape(steps, width), shape(4, width)),
        in_specs=[smem] + [vmem] * 4,
        out_specs=(vmem,) * 2,
        compiler_params=params,
        name="rotate_last",
    )(place, obs[last], basis, z, w)
    sums = [summary]
    for step in range(1, 4):
        sums.append(lax.ppermute(summary, "tm", [(a, a ^ step) for a in range(blocks)]))
    for level in range(2, rounds):
        summary = pl.pallas_call(
            functools.partial(merge_kernel, 0 if level == 2 else level - 1),
            out_shape=shape(4, width),
            in_specs=[smem] + [vmem] * (5 if level == 2 else 3),
            out_specs=vmem,
            compiler_params=params,
            name="merge",
        )(me, merges, *(sums if level == 2 else (summary, sums[-1])))
        step = 1 << level
        sums.append(lax.ppermute(summary, "tm", [(a, a ^ step) for a in range(blocks)]))
    local = pl.pallas_call(
        local_kernel,
        out_shape=shape(steps, width),
        in_specs=[vmem] * 2,
        out_specs=vmem,
        scratch_shapes=[pltpu.VMEM((width // 128, steps, 128), F32)],
        compiler_params=params,
        cost_estimate=pl.CostEstimate(flops=10000000, bytes_accessed=1000000, transcendentals=0),
        name="local",
    )(z, const)
    far = list(range(2, pieces))
    near = list(range(min(2, pieces)))
    residual, *parts = pl.pallas_call(
        functools.partial(finish_kernel, far),
        out_shape=(shape(steps, width, dtype=jnp.bfloat16),)
        + (shape(steps, depth, dtype=jnp.bfloat16),) * len(far),
        in_specs=[smem] + [vmem] * (5 + len(sums)),
        out_specs=(vmem,) * (1 + len(far)),
        compiler_params=params,
        name="finish",
    )(place, local, w, g, const, basis, *sums)
    arrived = [
        lax.ppermute(part, "mode", [(a, a ^ piece) for a in range(pieces)])
        for piece, part in zip(far, parts)
    ]
    grad_obs, *parts = pl.pallas_call(
        functools.partial(rest_kernel, near),
        out_shape=(shape(steps, depth),)
        + (shape(steps, depth, dtype=jnp.bfloat16),) * (len(near) - 1),
        in_specs=[smem] + [vmem] * 2,
        out_specs=(vmem,) * len(near),
        compiler_params=params,
        cost_estimate=pl.CostEstimate(flops=80000000, bytes_accessed=1500000, transcendentals=0),
        name="rest",
    )(place, residual, basis)
    for piece, part in zip(near[1:], parts):
        swap = [(a, a ^ piece) for a in range(pieces)]
        grad_obs = grad_obs + lax.ppermute(part, "mode", swap).astype(F32)
    for part in arrived:
        grad_obs = grad_obs + part.astype(F32)
    return grad_obs


def solution(mesh):
    placed = (P("tm", "mode"), P(None, "mode"), P("mode"), P("mode"), P())
    return jax.shard_map(
        shards, mesh=mesh, in_specs=placed, out_specs=P("tm", "mode"), check_vma=False
    )
```

```python
import functools
import math

import jax
import jax.numpy as jnp
from jax import lax
from jax.experimental import pallas as pl
from jax.experimental.pallas import tpu as pltpu
from jax.sharding import PartitionSpec as P

F32 = jnp.float32
SUB = 8
VMEM_LIMIT = 24 * 1024 * 1024


def mat_mul(p, q):
    return (
        p[0] * q[0] + p[1] * q[2],
        p[0] * q[1] + p[1] * q[3],
        p[2] * q[0] + p[3] * q[2],
        p[2] * q[1] + p[3] * q[3],
    )


def mat_trans(p):
    return (p[0], p[2], p[1], p[3])


def mat_add(p, q):
    return tuple(a + b for a, b in zip(p, q))


def mat_sub(p, q):
    return tuple(a - b for a, b in zip(p, q))


def mat_pick(flag, p, q):
    return tuple(jnp.where(flag, a, b) for a, b in zip(p, q))


def full(s):
    return (s[0], s[1], s[1], s[2])


def congruence(s, f):
    t = (
        s[0] * f[0] + s[1] * f[2],
        s[0] * f[1] + s[1] * f[3],
        s[1] * f[0] + s[2] * f[2],
        s[1] * f[1] + s[2] * f[3],
    )
    return (f[0] * t[0] + f[2] * t[2], f[0] * t[1] + f[2] * t[3], f[1] * t[1] + f[3] * t[3])


def power(squares, exponent, like):
    one, zero = jnp.ones_like(like), jnp.zeros_like(like)
    out = None
    for bit, base in enumerate(squares):
        flag = (exponent & (1 << bit)) != 0
        if out is None:
            out = mat_pick(flag, base, (one, zero, zero, one))
        else:
            out = mat_pick(flag, mat_mul(out, base), out)
    return out


def gramian(squares, grams, count, like):
    zero = jnp.zeros_like(like)
    out = (zero, zero, zero)
    for bit, (base, gram) in enumerate(zip(squares, grams)):
        flag = (count & (1 << bit)) != 0
        out = mat_pick(flag, mat_add(gram, congruence(out, base)), out)
    return out


def steady_state(scale2, length, noise_var):
    lam = math.sqrt(3.0) / length
    decay = jnp.exp(-lam)
    twice = 2.0 * lam
    fall = jnp.exp(-twice)
    rho = scale2 / noise_var
    series = 1.0 / 604800.0
    for factor in (60480.0, 6720.0, 840.0, 120.0, 20.0, 4.0, 1.0):
        series = series * twice + 1.0 / factor
    lower = fall * twice * twice * twice * (1.0 / 6.0) * series
    loss = 1.0
    for order in (8, 7, 6, 5, 4, 3, 2):
        loss = 1.0 - lam * (1.0 / order) * loss
    loss = lam * loss
    q00 = rho * lower
    q01 = 2.0 * rho * lam * lam * fall
    q11 = rho * (lower + twice * fall)
    slope = decay * lam
    tilt = loss + slope
    g0 = q00 * tilt * tilt + 2.0 * slope * q01 * tilt + slope * slope * q11
    g1 = slope * q01 - decay * (1.0 - lam) * q00
    loss2 = loss * loss
    c2 = decay * decay
    u = (2.0 * decay * loss2 - g1) / c2
    v = (loss2 * loss2 + g0) / c2
    root = jnp.sqrt(v * (v + 4.0 * u + 16.0))
    product = 4.0 * v / (v + root + jnp.sqrt(2.0 * v * (v + 2.0 * u + root)))
    total = 0.5 * (jnp.sqrt(u * u + 4.0 * u - 2.0 * v + 2.0 * root) - u)
    gain0 = total - 2.0 * loss
    gain1 = (product - loss2 - gain0 * tilt) / slope
    inverse = (1.0 - total + product) / c2
    inn = c2 / (1.0 - total + product)
    closed = (1.0 + slope - loss - gain0, slope, -slope - gain1, decay * (1.0 - lam))
    p00 = inn * ((1.0 - lam) * gain0 - lam * gain1) / decay
    p01 = inn * (lam * gain0 + (1.0 + lam) * gain1) / decay
    p11 = (
        p01 * (loss * (1.0 + decay) + 2.0 * slope * slope)
        + slope * decay * (1.0 + lam) * p00
        - q01
        + gain0 * gain1 * inn
    ) / (slope * decay * (1.0 - lam))
    return closed, gain0, gain1, inverse, (rho - p00, -p01, rho - p11)


def coefficients_kernel(blocks, me_ref, noise_ref, *refs):
    arguments, (const_ref, w_ref, g_ref, merge_ref, basis_ref, obs_ref) = (
        refs[:4],
        refs[4:10],
    )
    scale_ref, length_ref, sems = refs[10:]
    copies = [
        pltpu.make_async_copy(source, target, sems.at[k])
        for k, (source, target) in enumerate(
            zip(arguments, (scale_ref, length_ref, obs_ref, basis_ref))
        )
    ]
    for copy in copies:
        copy.start()
    for copy in copies[:2]:
        copy.wait()
    steps = w_ref.shape[1]
    width = scale_ref.shape[1]
    tile = (SUB, width)
    me = me_ref[0]
    scale2 = jnp.broadcast_to(scale_ref[...], tile)
    length = jnp.broadcast_to(length_ref[...], tile)
    noise_var = jnp.full(tile, noise_ref[0], F32)
    closed, gain0, gain1, inverse, excess = steady_state(scale2, length, noise_var)
    zero = jnp.zeros(tile, F32)

    squares, grams = [closed], [(inverse, zero, zero)]
    doublings = (steps * blocks).bit_length() - 1
    for _ in range(doublings):
        base = squares[-1]
        grams.append(mat_add(grams[-1], congruence(grams[-1], base)))
        squares.append(mat_mul(base, base))
    local = steps.bit_length() - 1
    consts = closed + (gain0, gain1, inverse) + squares[3] + squares[4] + squares[5]
    for place, value in enumerate(consts):
        const_ref[place] = value
    const_ref[len(consts)] = -1.0 / noise_var
    for level in range(blocks.bit_length() - 1):
        for place, value in enumerate(squares[local + level] + grams[local + level]):
            merge_ref[7 * level + place : 7 * level + place + 1, :] = value[0:1, :]

    row = lax.broadcasted_iota(jnp.int32, tile, 0)
    small, gram_small = squares[:3], grams[:3]
    behind = power(small, 7 - row, zero)
    gram = gramian(small, gram_small, 7 - row, zero)
    eight, gram_eight = squares[3], grams[3]
    parts = steps // SUB
    for part in range(parts - 1, -1, -1):
        rows = pl.ds(part * SUB, SUB)
        w_ref[0, rows, :] = behind[0] * gain0 + behind[1] * gain1
        w_ref[1, rows, :] = behind[2] * gain0 + behind[3] * gain1
        k0 = gain0 * gram[0] + gain1 * gram[1]
        k1 = gain0 * gram[1] + gain1 * gram[2]
        w_ref[2, rows, :] = inverse - (k0 * closed[0] + k1 * closed[2])
        w_ref[3, rows, :] = -(k0 * closed[1] + k1 * closed[3])
        if part:
            behind = mat_mul(behind, eight)
            gram = mat_add(gram_eight, congruence(gram, eight))
    ahead = power(small, row, zero)
    for part in range(parts):
        rows = pl.ds(part * SUB, SUB)
        u0, u1 = w_ref[2, rows, :], w_ref[3, rows, :]
        w_ref[2, rows, :] = u0 * ahead[0] + u1 * ahead[2]
        w_ref[3, rows, :] = u0 * ahead[1] + u1 * ahead[3]
        if part < parts - 1:
            ahead = mat_mul(ahead, eight)

    s = grams[-1]
    left = (
        1.0 + excess[0] * s[0] + excess[1] * s[1],
        excess[0] * s[1] + excess[1] * s[2],
        excess[1] * s[0] + excess[2] * s[1],
        1.0 + excess[1] * s[1] + excess[2] * s[2],
    )
    determ = 1.0 / (left[0] * left[3] - left[1] * left[2])
    start = mat_mul((left[3], -left[1], -left[2], left[0]), full(excess))
    start = tuple(x * determ for x in start)
    block_squares, block_grams = squares[local:-1], grams[local:-1]
    mine = jnp.full(tile, me, jnp.int32)
    to_me = power(block_squares, mine, zero)
    rest = full(gramian(block_squares, block_grams, blocks - 1 - mine, zero))
    to_state = mat_mul(to_me, start)
    to_adjoint = mat_mul(mat_mul(rest, mat_mul(to_me, block_squares[0])), start)
    for group in range(g_ref.shape[1] // SUB):
        rows = row + group * SUB
        kind = rows & 3
        line = rows >> 2
        span = jnp.where(line < 4, 1, jnp.left_shift(1, jnp.maximum(line - 2, 0)))
        near_me = mine ^ jnp.where(line < 4, line, span)
        front = jnp.minimum((near_me // span) * span, blocks - 1)
        back = jnp.minimum(front + span - 1, blocks - 1)
        before, after = back < me, front > me
        gap = jnp.where(before, me - 1 - back, jnp.where(after, front - 1 - me, 0))
        reach = jnp.where(before, me - back, jnp.where(after, back - me, 0))
        near = power(block_squares, gap, zero)
        far = power(block_squares, reach, zero)
        origin = mat_trans(power(block_squares, front, zero))
        left_over = full(gramian(block_squares, block_grams, blocks - 1 - back, zero))
        end = mat_trans(mat_mul(power(block_squares, back, zero), block_squares[0]))
        first = mat_mul(end, left_over)
        state_b = mat_sub(mat_pick(before, near, (zero,) * 4), mat_mul(to_state, first))
        state_l = mat_mul(to_state, origin)
        cross = mat_pick(after, mat_mul(mat_trans(far), left_over), mat_mul(rest, far))
        adjoint_b = mat_sub(mat_mul(to_adjoint, first), cross)
        adjoint_l = mat_sub(
            mat_pick(after, mat_trans(near), (zero,) * 4), mat_mul(to_adjoint, origin)
        )
        place = pl.ds(group * SUB, SUB)
        for output, (from_b, from_l) in enumerate(
            ((adjoint_b[:2], adjoint_l[:2]), (adjoint_b[2:], adjoint_l[2:]),
             (state_b[:2], state_l[:2]), (state_b[2:], state_l[2:]))
        ):
            g_ref[output, place, :] = jnp.where(
                kind < 2,
                jnp.where(kind == 0, from_b[0], from_b[1]),
                jnp.where(kind == 2, from_l[0], from_l[1]),
            )
    for copy in copies[2:]:
        copy.wait()


def rotate_kernel(first, place_ref, *refs):
    pieces, others = first
    obs_refs, (basis_ref, *refs) = refs[: len(pieces)], refs[len(pieces) :]
    depth = obs_refs[0].shape[1]
    z = None if others is None else refs[0][...]
    for piece, obs_ref in zip(pieces, obs_refs):
        begin = pl.multiple_of((place_ref[0] ^ piece) * depth, depth)
        term = jnp.dot(
            obs_ref[...], basis_ref[pl.ds(begin, depth), :], preferred_element_type=F32
        )
        z = term if z is None else z + term
    if others is None:
        refs[0][...] = z
        return
    _, w_ref, z_ref, sum_ref = refs
    z_ref[...] = z
    for line in range(4):
        sum_ref[line : line + 1, :] = jnp.sum(w_ref[line] * z, axis=0, keepdims=True)


def merge(level, me, own, other, merge_ref):
    lower = jnp.full(own.shape, (me >> level) & 1, jnp.int32) == 0
    left, right = jnp.where(lower, own, other), jnp.where(lower, other, own)
    f00, f01, f10, f11, s00, s01, s11 = (
        merge_ref[7 * level + k : 7 * level + k + 1, :] for k in range(7)
    )
    b0, b1 = left[0:1, :], left[1:2, :]
    a0 = right[2:3, :] - s00 * b0 - s01 * b1
    a1 = right[3:4, :] - s01 * b0 - s11 * b1
    return jnp.concatenate(
        (
            right[0:1, :] + f00 * b0 + f01 * b1,
            right[1:2, :] + f10 * b0 + f11 * b1,
            left[2:3, :] + f00 * a0 + f10 * a1,
            left[3:4, :] + f01 * a0 + f11 * a1,
        ),
        axis=0,
    )


def merge_kernel(level, me_ref, merge_ref, *refs):
    *parts, out_ref = refs
    me = me_ref[0]
    parts = [ref[...] for ref in parts]
    if level:
        out_ref[...] = merge(level, me, parts[0], parts[1], merge_ref)
    else:
        near = merge(0, me, parts[0], parts[1], merge_ref)
        far = merge(0, me, parts[2], parts[3], merge_ref)
        out_ref[...] = merge(1, me, near, far, merge_ref)


def shift(value, by):
    rows = value.shape[0]
    row = lax.broadcasted_iota(jnp.int32, value.shape, 0)
    keep = row >= by if by > 0 else row < rows + by
    return jnp.where(keep, pltpu.roll(value, by % rows, 0), 0.0)


def local_kernel(z_ref, const_ref, r_ref, scratch):
    steps, width = z_ref.shape
    span = steps // SUB
    lanes = 128
    for chunk in range(width // lanes):
        cols = pl.ds(chunk * lanes, lanes)
        scratch[chunk] = z_ref[:, cols]
    for chunk in range(width // lanes):
        cols = pl.ds(chunk * lanes, lanes)
        const = [const_ref[k, :, cols] for k in range(19)]
        f, (k0, k1, inverse) = const[0:4], const[4:7]
        jumps = (const[7:11], const[11:15], const[15:19])
        zero = jnp.zeros((SUB, lanes), F32)
        x0, x1 = zero, zero
        vs = []
        for t in range(span):
            z = scratch[chunk, pl.ds(t, SUB, stride=span), :]
            vs.append(z - x0)
            x0, x1 = f[0] * x0 + f[1] * x1 + k0 * z, f[2] * x0 + f[3] * x1 + k1 * z
        for level, jump in enumerate(jumps):
            s0, s1 = shift(x0, 1 << level), shift(x1, 1 << level)
            x0, x1 = x0 + jump[0] * s0 + jump[1] * s1, x1 + jump[2] * s0 + jump[3] * s1
        x0, x1 = shift(x0, 1), shift(x1, 1)
        for t in range(span):
            vs[t] = (vs[t] - x0) * inverse
            x0, x1 = f[0] * x0 + f[1] * x1, f[2] * x0 + f[3] * x1
        a0, a1 = zero, zero
        for t in range(span - 1, -1, -1):
            a0, a1 = f[0] * a0 + f[2] * a1 + vs[t], f[1] * a0 + f[3] * a1
        for level, jump in enumerate(jumps):
            s0, s1 = shift(a0, -(1 << level)), shift(a1, -(1 << level))
            a0, a1 = a0 + jump[0] * s0 + jump[2] * s1, a1 + jump[1] * s0 + jump[3] * s1
        a0, a1 = shift(a0, -1), shift(a1, -1)
        for t in range(span - 1, -1, -1):
            r = vs[t] - k0 * a0 - k1 * a1
            a0, a1 = f[0] * a0 + f[2] * a1 + vs[t], f[1] * a0 + f[3] * a1
            scratch[chunk, pl.ds(t, SUB, stride=span), :] = r
        r_ref[:, cols] = scratch[chunk]


def rotate_back(residual, pieces, place_ref, basis_ref, outs):
    depth = outs[0].shape[1]
    for piece, out_ref in zip(pieces, outs):
        begin = pl.multiple_of((place_ref[0] ^ piece) * depth, depth)
        out_ref[...] = lax.dot_general(
            residual,
            basis_ref[pl.ds(begin, depth), :],
            (((1,), (1,)), ((), ())),
            preferred_element_type=F32,
        ).astype(out_ref.dtype)


def finish_kernel(pieces, place_ref, r_ref, w_ref, g_ref, const_ref, basis_ref, *refs):
    *sums, residual_ref = refs[: -len(pieces)]
    value = r_ref[...]
    for line in range(4):
        total = None
        for place, sum_ref in enumerate(sums):
            term = g_ref[line, pl.ds(4 * place, 4), :] * sum_ref[...]
            total = term if total is None else total + term
        value = value - w_ref[line] * jnp.sum(total, axis=0, keepdims=True)
    scale = const_ref[19, 0:1, :]
    residual = (value * scale).astype(jnp.bfloat16)
    residual_ref[...] = residual
    rotate_back(residual, pieces, place_ref, basis_ref, refs[-len(pieces) :])


def rest_kernel(pieces, place_ref, residual_ref, basis_ref, *outs):
    rotate_back(residual_ref[...], pieces, place_ref, basis_ref, outs)


def exchange(value, axis, count):
    out = [value]
    for step in range(1, count):
        out.append(lax.ppermute(value, axis, [(a, a ^ step) for a in range(count)]))
    return out


def shards(observations, basis, eigvals, lengths, noise):
    steps, depth = observations.shape
    width = basis.shape[1]
    blocks, pieces = lax.axis_size("tm"), lax.axis_size("mode")
    me = lax.axis_index("tm").astype(jnp.int32).reshape(1)
    place = lax.axis_index("mode").astype(jnp.int32).reshape(1)
    rounds = blocks.bit_length() - 1
    vmem = pl.BlockSpec(memory_space=pltpu.VMEM)
    smem = pl.BlockSpec(memory_space=pltpu.SMEM)
    params = pltpu.CompilerParams(vmem_limit_bytes=VMEM_LIMIT)

    def shape(*dims, dtype=F32):
        return jax.ShapeDtypeStruct(dims, dtype)

    obs = exchange(observations, "mode", pieces)
    const, w, g, merges, basis, obs[0] = pl.pallas_call(
        functools.partial(coefficients_kernel, blocks),
        out_shape=(
            shape(20, SUB, width),
            shape(4, steps, width),
            shape(4, -(-4 * (rounds + 2) // SUB) * SUB, width),
            shape(-(-7 * rounds // SUB) * SUB, width),
            shape(*basis.shape, dtype=basis.dtype),
            shape(steps, depth, dtype=observations.dtype),
        ),
        in_specs=[smem] * 2 + [pl.BlockSpec(memory_space=pltpu.HBM)] * 4,
        out_specs=(vmem,) * 6,
        scratch_shapes=[
            pltpu.VMEM((1, width), F32),
            pltpu.VMEM((1, width), F32),
            pltpu.SemaphoreType.DMA((4,)),
        ],
        compiler_params=params,
        cost_estimate=pl.CostEstimate(flops=20000000, bytes_accessed=2000000, transcendentals=0),
        name="coefficients",
    )(
        me,
        noise,
        *(
            pltpu.with_memory_space_constraint(x, pltpu.HBM)
            for x in (
                eigvals.reshape(1, width),
                lengths.reshape(1, width),
                observations,
                basis,
            )
        ),
    )
    last = pieces - 1
    early = [0, *range(2, last), 1]
    z = pl.pallas_call(
        functools.partial(rotate_kernel, (early, None)),
        out_shape=shape(steps, width),
        in_specs=[smem] + [vmem] * pieces,
        out_specs=vmem,
        compiler_params=params,
        name="rotate_early",
    )(place, *(obs[piece] for piece in early), basis)
    z, summary = pl.pallas_call(
        functools.partial(rotate_kernel, ([last], early)),
        out_shape=(shape(steps, width), shape(4, width)),
        in_specs=[smem] + [vmem] * 4,
        out_specs=(vmem,) * 2,
        compiler_params=params,
        name="rotate_last",
    )(place, obs[last], basis, z, w)
    sums = [summary]
    for step in range(1, 4):
        sums.append(lax.ppermute(summary, "tm", [(a, a ^ step) for a in range(blocks)]))
    for level in range(2, rounds):
        summary = pl.pallas_call(
            functools.partial(merge_kernel, 0 if level == 2 else level - 1),
            out_shape=shape(4, width),
            in_specs=[smem] + [vmem] * (5 if level == 2 else 3),
            out_specs=vmem,
            compiler_params=params,
            name="merge",
        )(me, merges, *(sums if level == 2 else (summary, sums[-1])))
        step = 1 << level
        sums.append(lax.ppermute(summary, "tm", [(a, a ^ step) for a in range(blocks)]))
    local = pl.pallas_call(
        local_kernel,
        out_shape=shape(steps, width),
        in_specs=[vmem] * 2,
        out_specs=vmem,
        scratch_shapes=[pltpu.VMEM((width // 128, steps, 128), F32)],
        compiler_params=params,
        cost_estimate=pl.CostEstimate(flops=10000000, bytes_accessed=1000000, transcendentals=0),
        name="local",
    )(z, const)
    far = list(range(2, pieces)) + [1]
    near = [0]
    residual, *parts = pl.pallas_call(
        functools.partial(finish_kernel, far),
        out_shape=(shape(steps, width, dtype=jnp.bfloat16),)
        + (shape(steps, depth, dtype=jnp.bfloat16),) * len(far),
        in_specs=[smem] + [vmem] * (5 + len(sums)),
        out_specs=(vmem,) * (1 + len(far)),
        compiler_params=params,
        name="finish",
    )(place, local, w, g, const, basis, *sums)
    arrived = [
        lax.ppermute(part, "mode", [(a, a ^ piece) for a in range(pieces)])
        for piece, part in zip(far, parts)
    ]
    grad_obs = pl.pallas_call(
        functools.partial(rest_kernel, near),
        out_shape=shape(steps, depth),
        in_specs=[smem] + [vmem] * 2,
        out_specs=vmem,
        compiler_params=params,
        cost_estimate=pl.CostEstimate(flops=80000000, bytes_accessed=1500000, transcendentals=0),
        name="rest",
    )(place, residual, basis)
    for part in arrived:
        grad_obs = grad_obs + part.astype(F32)
    return grad_obs


def solution(mesh):
    placed = (P("tm", "mode"), P(None, "mode"), P("mode"), P("mode"), P())
    return jax.shard_map(
        shards, mesh=mesh, in_specs=placed, out_specs=P("tm", "mode"), check_vma=False
    )
```

```python
import functools
import math

import jax
import jax.numpy as jnp
from jax import lax
from jax.experimental import pallas as pl
from jax.experimental.pallas import tpu as pltpu
from jax.sharding import PartitionSpec as P

F32 = jnp.float32
SUB = 8
VMEM_LIMIT = 24 * 1024 * 1024


def mat_mul(p, q):
    return (
        p[0] * q[0] + p[1] * q[2],
        p[0] * q[1] + p[1] * q[3],
        p[2] * q[0] + p[3] * q[2],
        p[2] * q[1] + p[3] * q[3],
    )


def mat_trans(p):
    return (p[0], p[2], p[1], p[3])


def mat_add(p, q):
    return tuple(a + b for a, b in zip(p, q))


def mat_sub(p, q):
    return tuple(a - b for a, b in zip(p, q))


def mat_pick(flag, p, q):
    return tuple(jnp.where(flag, a, b) for a, b in zip(p, q))


def full(s):
    return (s[0], s[1], s[1], s[2])


def congruence(s, f):
    t = (
        s[0] * f[0] + s[1] * f[2],
        s[0] * f[1] + s[1] * f[3],
        s[1] * f[0] + s[2] * f[2],
        s[1] * f[1] + s[2] * f[3],
    )
    return (f[0] * t[0] + f[2] * t[2], f[0] * t[1] + f[2] * t[3], f[1] * t[1] + f[3] * t[3])


def power(squares, exponent, like):
    one, zero = jnp.ones_like(like), jnp.zeros_like(like)
    out = None
    for bit, base in enumerate(squares):
        flag = (exponent & (1 << bit)) != 0
        if out is None:
            out = mat_pick(flag, base, (one, zero, zero, one))
        else:
            out = mat_pick(flag, mat_mul(out, base), out)
    return out


def gramian(squares, grams, count, like):
    zero = jnp.zeros_like(like)
    out = (zero, zero, zero)
    for bit, (base, gram) in enumerate(zip(squares, grams)):
        flag = (count & (1 << bit)) != 0
        out = mat_pick(flag, mat_add(gram, congruence(out, base)), out)
    return out


def steady_state(scale2, length, noise_var):
    lam = math.sqrt(3.0) / length
    decay = jnp.exp(-lam)
    twice = 2.0 * lam
    fall = jnp.exp(-twice)
    rho = scale2 / noise_var
    series = 1.0 / 604800.0
    for factor in (60480.0, 6720.0, 840.0, 120.0, 20.0, 4.0, 1.0):
        series = series * twice + 1.0 / factor
    lower = fall * twice * twice * twice * (1.0 / 6.0) * series
    loss = 1.0
    for order in (8, 7, 6, 5, 4, 3, 2):
        loss = 1.0 - lam * (1.0 / order) * loss
    loss = lam * loss
    q00 = rho * lower
    q01 = 2.0 * rho * lam * lam * fall
    q11 = rho * (lower + twice * fall)
    slope = decay * lam
    tilt = loss + slope
    g0 = q00 * tilt * tilt + 2.0 * slope * q01 * tilt + slope * slope * q11
    g1 = slope * q01 - decay * (1.0 - lam) * q00
    loss2 = loss * loss
    c2 = decay * decay
    u = (2.0 * decay * loss2 - g1) / c2
    v = (loss2 * loss2 + g0) / c2
    root = jnp.sqrt(v * (v + 4.0 * u + 16.0))
    product = 4.0 * v / (v + root + jnp.sqrt(2.0 * v * (v + 2.0 * u + root)))
    total = 0.5 * (jnp.sqrt(u * u + 4.0 * u - 2.0 * v + 2.0 * root) - u)
    gain0 = total - 2.0 * loss
    gain1 = (product - loss2 - gain0 * tilt) / slope
    inverse = (1.0 - total + product) / c2
    inn = c2 / (1.0 - total + product)
    closed = (1.0 + slope - loss - gain0, slope, -slope - gain1, decay * (1.0 - lam))
    p00 = inn * ((1.0 - lam) * gain0 - lam * gain1) / decay
    p01 = inn * (lam * gain0 + (1.0 + lam) * gain1) / decay
    p11 = (
        p01 * (loss * (1.0 + decay) + 2.0 * slope * slope)
        + slope * decay * (1.0 + lam) * p00
        - q01
        + gain0 * gain1 * inn
    ) / (slope * decay * (1.0 - lam))
    return closed, gain0, gain1, inverse, (rho - p00, -p01, rho - p11)


def coefficients_kernel(blocks, noise_ref, *refs):
    arguments, (const_ref, w_ref, merge_ref, basis_ref, obs_ref) = refs[:4], refs[4:9]
    scale_ref, length_ref, sems = refs[9:]
    targets = (scale_ref, length_ref, obs_ref, basis_ref)
    copies = [
        pltpu.make_async_copy(source, target, sems.at[k])
        for k, (source, target) in enumerate(zip(arguments, targets))
    ]
    for copy in copies:
        copy.start()
    for copy in copies[:2]:
        copy.wait()
    steps = w_ref.shape[1]
    width = scale_ref.shape[1]
    tile = (SUB, width)
    scale2 = jnp.broadcast_to(scale_ref[...], tile)
    length = jnp.broadcast_to(length_ref[...], tile)
    noise_var = jnp.full(tile, noise_ref[0], F32)
    closed, gain0, gain1, inverse, excess = steady_state(scale2, length, noise_var)
    zero = jnp.zeros(tile, F32)

    squares, grams = [closed], [(inverse, zero, zero)]
    doublings = (steps * blocks).bit_length() - 1
    for _ in range(doublings):
        base = squares[-1]
        grams.append(mat_add(grams[-1], congruence(grams[-1], base)))
        squares.append(mat_mul(base, base))
    local = steps.bit_length() - 1
    consts = closed + (gain0, gain1, inverse) + squares[3] + squares[4] + squares[5]
    for place, value in enumerate(consts):
        const_ref[place] = value
    const_ref[len(consts)] = -1.0 / noise_var
    rounds = blocks.bit_length() - 1
    groups = squares[local:-1] + [()], grams[local:], [()] * rounds + [excess]
    values = [value for group in zip(*groups) for part in group for value in part]
    for place, value in enumerate(values):
        merge_ref[place : place + 1, :] = value[0:1, :]

    row = lax.broadcasted_iota(jnp.int32, tile, 0)
    small, gram_small = squares[:3], grams[:3]
    behind = power(small, 7 - row, zero)
    gram = gramian(small, gram_small, 7 - row, zero)
    eight, gram_eight = squares[3], grams[3]
    parts = steps // SUB
    for part in range(parts - 1, -1, -1):
        rows = pl.ds(part * SUB, SUB)
        w_ref[0, rows, :] = behind[0] * gain0 + behind[1] * gain1
        w_ref[1, rows, :] = behind[2] * gain0 + behind[3] * gain1
        k0 = gain0 * gram[0] + gain1 * gram[1]
        k1 = gain0 * gram[1] + gain1 * gram[2]
        w_ref[2, rows, :] = inverse - (k0 * closed[0] + k1 * closed[2])
        w_ref[3, rows, :] = -(k0 * closed[1] + k1 * closed[3])
        if part:
            behind = mat_mul(behind, eight)
            gram = mat_add(gram_eight, congruence(gram, eight))
    ahead = power(small, row, zero)
    for part in range(parts):
        rows = pl.ds(part * SUB, SUB)
        u0, u1 = w_ref[2, rows, :], w_ref[3, rows, :]
        w_ref[2, rows, :] = u0 * ahead[0] + u1 * ahead[2]
        w_ref[3, rows, :] = u0 * ahead[1] + u1 * ahead[3]
        if part < parts - 1:
            ahead = mat_mul(ahead, eight)

    for copy in copies[2:]:
        copy.wait()


def rotate_kernel(first, place_ref, *refs):
    pieces, others = first
    obs_refs, (basis_ref, *refs) = refs[: len(pieces)], refs[len(pieces) :]
    depth = obs_refs[0].shape[1]
    z = None if others is None else refs[0][...]
    for piece, obs_ref in zip(pieces, obs_refs):
        begin = pl.multiple_of((place_ref[0] ^ piece) * depth, depth)
        term = jnp.dot(
            obs_ref[...], basis_ref[pl.ds(begin, depth), :], preferred_element_type=F32
        )
        z = term if z is None else z + term
    if others is None:
        refs[0][...] = z
        return
    _, w_ref, z_ref, sum_ref = refs
    z_ref[...] = z
    for line in range(4):
        sum_ref[line : line + 1, :] = jnp.sum(w_ref[line] * z, axis=0, keepdims=True)


def merge(level, me, own, other, merge_ref):
    lower = jnp.full(own.shape, (me >> level) & 1, jnp.int32) == 0
    left, right = jnp.where(lower, own, other), jnp.where(lower, other, own)
    f00, f01, f10, f11, s00, s01, s11 = (
        merge_ref[7 * level + k : 7 * level + k + 1, :] for k in range(7)
    )
    b0, b1 = left[0:1, :], left[1:2, :]
    a0 = right[2:3, :] - s00 * b0 - s01 * b1
    a1 = right[3:4, :] - s01 * b0 - s11 * b1
    return jnp.concatenate(
        (
            right[0:1, :] + f00 * b0 + f01 * b1,
            right[1:2, :] + f10 * b0 + f11 * b1,
            left[2:3, :] + f00 * a0 + f10 * a1,
            left[3:4, :] + f01 * a0 + f11 * a1,
        ),
        axis=0,
    )


def merge_kernel(level, me_ref, merge_ref, *refs):
    *parts, out_ref = refs
    me = me_ref[0]
    parts = [ref[...] for ref in parts]
    if level:
        out_ref[...] = merge(level, me, parts[0], parts[1], merge_ref)
    else:
        near = merge(0, me, parts[0], parts[1], merge_ref)
        far = merge(0, me, parts[2], parts[3], merge_ref)
        out_ref[...] = merge(1, me, near, far, merge_ref)


def shift(value, by):
    rows = value.shape[0]
    row = lax.broadcasted_iota(jnp.int32, value.shape, 0)
    keep = row >= by if by > 0 else row < rows + by
    return jnp.where(keep, pltpu.roll(value, by % rows, 0), 0.0)


def reach(blocks, me, merge_ref, g_ref):
    tile = (SUB, merge_ref.shape[1])
    rounds = blocks.bit_length() - 1
    values = [
        jnp.broadcast_to(merge_ref[k : k + 1, :], tile) for k in range(7 * rounds + 6)
    ]
    block_squares = [tuple(values[7 * k : 7 * k + 4]) for k in range(rounds)]
    block_grams = [tuple(values[7 * k + 4 : 7 * k + 7]) for k in range(rounds)]
    s, excess = values[-6:-3], values[-3:]
    zero = jnp.zeros(tile, F32)
    row = lax.broadcasted_iota(jnp.int32, tile, 0)
    left = (
        1.0 + excess[0] * s[0] + excess[1] * s[1],
        excess[0] * s[1] + excess[1] * s[2],
        excess[1] * s[0] + excess[2] * s[1],
        1.0 + excess[1] * s[1] + excess[2] * s[2],
    )
    determ = 1.0 / (left[0] * left[3] - left[1] * left[2])
    start = mat_mul((left[3], -left[1], -left[2], left[0]), full(excess))
    start = tuple(x * determ for x in start)
    mine = jnp.full(tile, me, jnp.int32)
    to_me = power(block_squares, mine, zero)
    rest = full(gramian(block_squares, block_grams, blocks - 1 - mine, zero))
    to_state = mat_mul(to_me, start)
    to_adjoint = mat_mul(mat_mul(rest, mat_mul(to_me, block_squares[0])), start)
    for group in range(g_ref.shape[1] // SUB):
        rows = row + group * SUB
        kind = rows & 3
        line = rows >> 2
        span = jnp.where(line < 4, 1, jnp.left_shift(1, jnp.maximum(line - 2, 0)))
        near_me = mine ^ jnp.where(line < 4, line, span)
        front = jnp.minimum((near_me // span) * span, blocks - 1)
        back = jnp.minimum(front + span - 1, blocks - 1)
        before, after = back < me, front > me
        gap = jnp.where(before, me - 1 - back, jnp.where(after, front - 1 - me, 0))
        reach = jnp.where(before, me - back, jnp.where(after, back - me, 0))
        near = power(block_squares, gap, zero)
        far = power(block_squares, reach, zero)
        origin = mat_trans(power(block_squares, front, zero))
        left_over = full(gramian(block_squares, block_grams, blocks - 1 - back, zero))
        end = mat_trans(mat_mul(power(block_squares, back, zero), block_squares[0]))
        first = mat_mul(end, left_over)
        state_b = mat_sub(mat_pick(before, near, (zero,) * 4), mat_mul(to_state, first))
        state_l = mat_mul(to_state, origin)
        cross = mat_pick(after, mat_mul(mat_trans(far), left_over), mat_mul(rest, far))
        adjoint_b = mat_sub(mat_mul(to_adjoint, first), cross)
        adjoint_l = mat_sub(
            mat_pick(after, mat_trans(near), (zero,) * 4), mat_mul(to_adjoint, origin)
        )
        place = pl.ds(group * SUB, SUB)
        for output, (from_b, from_l) in enumerate(
            ((adjoint_b[:2], adjoint_l[:2]), (adjoint_b[2:], adjoint_l[2:]),
             (state_b[:2], state_l[:2]), (state_b[2:], state_l[2:]))
        ):
            g_ref[output, place, :] = jnp.where(
                kind < 2,
                jnp.where(kind == 0, from_b[0], from_b[1]),
                jnp.where(kind == 2, from_l[0], from_l[1]),
            )


def local_kernel(blocks, me_ref, z_ref, const_ref, merge_ref, r_ref, g_ref, scratch):
    reach(blocks, me_ref[0], merge_ref, g_ref)
    steps, width = z_ref.shape
    span = steps // SUB
    lanes = 128
    for chunk in range(width // lanes):
        cols = pl.ds(chunk * lanes, lanes)
        scratch[chunk] = z_ref[:, cols]
    for chunk in range(width // lanes):
        cols = pl.ds(chunk * lanes, lanes)
        const = [const_ref[k, :, cols] for k in range(19)]
        f, (k0, k1, inverse) = const[0:4], const[4:7]
        jumps = (const[7:11], const[11:15], const[15:19])
        zero = jnp.zeros((SUB, lanes), F32)
        x0, x1 = zero, zero
        vs = []
        for t in range(span):
            z = scratch[chunk, pl.ds(t, SUB, stride=span), :]
            vs.append(z - x0)
            x0, x1 = f[0] * x0 + f[1] * x1 + k0 * z, f[2] * x0 + f[3] * x1 + k1 * z
        for level, jump in enumerate(jumps):
            s0, s1 = shift(x0, 1 << level), shift(x1, 1 << level)
            x0, x1 = x0 + jump[0] * s0 + jump[1] * s1, x1 + jump[2] * s0 + jump[3] * s1
        x0, x1 = shift(x0, 1), shift(x1, 1)
        for t in range(span):
            vs[t] = (vs[t] - x0) * inverse
            x0, x1 = f[0] * x0 + f[1] * x1, f[2] * x0 + f[3] * x1
        a0, a1 = zero, zero
        for t in range(span - 1, -1, -1):
            a0, a1 = f[0] * a0 + f[2] * a1 + vs[t], f[1] * a0 + f[3] * a1
        for level, jump in enumerate(jumps):
            s0, s1 = shift(a0, -(1 << level)), shift(a1, -(1 << level))
            a0, a1 = a0 + jump[0] * s0 + jump[2] * s1, a1 + jump[1] * s0 + jump[3] * s1
        a0, a1 = shift(a0, -1), shift(a1, -1)
        for t in range(span - 1, -1, -1):
            r = vs[t] - k0 * a0 - k1 * a1
            a0, a1 = f[0] * a0 + f[2] * a1 + vs[t], f[1] * a0 + f[3] * a1
            scratch[chunk, pl.ds(t, SUB, stride=span), :] = r
        r_ref[:, cols] = scratch[chunk]


def rotate_back(residual, pieces, place_ref, basis_ref, outs):
    depth = outs[0].shape[1]
    for piece, out_ref in zip(pieces, outs):
        begin = pl.multiple_of((place_ref[0] ^ piece) * depth, depth)
        out_ref[...] = lax.dot_general(
            residual,
            basis_ref[pl.ds(begin, depth), :],
            (((1,), (1,)), ((), ())),
            preferred_element_type=F32,
        ).astype(out_ref.dtype)


def finish_kernel(pieces, place_ref, r_ref, w_ref, g_ref, const_ref, basis_ref, *refs):
    *sums, residual_ref = refs[: -len(pieces)]
    value = r_ref[...]
    for line in range(4):
        total = None
        for place, sum_ref in enumerate(sums):
            term = g_ref[line, pl.ds(4 * place, 4), :] * sum_ref[...]
            total = term if total is None else total + term
        value = value - w_ref[line] * jnp.sum(total, axis=0, keepdims=True)
    scale = const_ref[19, 0:1, :]
    residual = (value * scale).astype(jnp.bfloat16)
    residual_ref[...] = residual
    rotate_back(residual, pieces, place_ref, basis_ref, refs[-len(pieces) :])


def rest_kernel(pieces, place_ref, residual_ref, basis_ref, *outs):
    rotate_back(residual_ref[...], pieces, place_ref, basis_ref, outs)


def exchange(value, axis, count):
    out = [value]
    for step in range(1, count):
        out.append(lax.ppermute(value, axis, [(a, a ^ step) for a in range(count)]))
    return out


def shards(observations, basis, eigvals, lengths, noise):
    steps, depth = observations.shape
    width = basis.shape[1]
    blocks, pieces = lax.axis_size("tm"), lax.axis_size("mode")
    me = lax.axis_index("tm").astype(jnp.int32).reshape(1)
    place = lax.axis_index("mode").astype(jnp.int32).reshape(1)
    rounds = blocks.bit_length() - 1
    vmem = pl.BlockSpec(memory_space=pltpu.VMEM)
    smem = pl.BlockSpec(memory_space=pltpu.SMEM)
    params = pltpu.CompilerParams(vmem_limit_bytes=VMEM_LIMIT)

    def shape(*dims, dtype=F32):
        return jax.ShapeDtypeStruct(dims, dtype)

    obs = exchange(observations, "mode", pieces)
    const, w, merges, basis, obs[0] = pl.pallas_call(
        functools.partial(coefficients_kernel, blocks),
        out_shape=(
            shape(20, SUB, width),
            shape(4, steps, width),
            shape(-(-(7 * rounds + 6) // SUB) * SUB, width),
            shape(*basis.shape, dtype=basis.dtype),
            shape(steps, depth, dtype=observations.dtype),
        ),
        in_specs=[smem] + [pl.BlockSpec(memory_space=pltpu.HBM)] * 4,
        out_specs=(vmem,) * 5,
        scratch_shapes=[
            pltpu.VMEM((1, width), F32),
            pltpu.VMEM((1, width), F32),
            pltpu.SemaphoreType.DMA((4,)),
        ],
        compiler_params=params,
        cost_estimate=pl.CostEstimate(flops=20000000, bytes_accessed=2000000, transcendentals=0),
        name="coefficients",
    )(
        noise,
        *(
            pltpu.with_memory_space_constraint(x, pltpu.HBM)
            for x in (
                eigvals.reshape(1, width),
                lengths.reshape(1, width),
                observations,
                basis,
            )
        ),
    )
    last = pieces - 1
    early = list(range(last))
    z = pl.pallas_call(
        functools.partial(rotate_kernel, (early, None)),
        out_shape=shape(steps, width),
        in_specs=[smem] + [vmem] * pieces,
        out_specs=vmem,
        compiler_params=params,
        name="rotate_early",
    )(place, *(obs[piece] for piece in early), basis)
    z, summary = pl.pallas_call(
        functools.partial(rotate_kernel, ([last], early)),
        out_shape=(shape(steps, width), shape(4, width)),
        in_specs=[smem] + [vmem] * 4,
        out_specs=(vmem,) * 2,
        compiler_params=params,
        name="rotate_last",
    )(place, obs[last], basis, z, w)
    sums = [summary]
    for step in range(1, 4):
        sums.append(lax.ppermute(summary, "tm", [(a, a ^ step) for a in range(blocks)]))
    for level in range(2, rounds):
        summary = pl.pallas_call(
            functools.partial(merge_kernel, 0 if level == 2 else level - 1),
            out_shape=shape(4, width),
            in_specs=[smem] + [vmem] * (5 if level == 2 else 3),
            out_specs=vmem,
            compiler_params=params,
            name="merge",
        )(me, merges, *(sums if level == 2 else (summary, sums[-1])))
        step = 1 << level
        sums.append(lax.ppermute(summary, "tm", [(a, a ^ step) for a in range(blocks)]))
    local, g = pl.pallas_call(
        functools.partial(local_kernel, blocks),
        out_shape=(shape(steps, width), shape(4, -(-4 * (rounds + 2) // SUB) * SUB, width)),
        in_specs=[smem] + [vmem] * 3,
        out_specs=(vmem,) * 2,
        scratch_shapes=[pltpu.VMEM((width // 128, steps, 128), F32)],
        compiler_params=params,
        cost_estimate=pl.CostEstimate(flops=10000000, bytes_accessed=1000000, transcendentals=0),
        name="local",
    )(me, z, const, merges)
    far = list(range(2, pieces)) + [1]
    near = [0]
    residual, *parts = pl.pallas_call(
        functools.partial(finish_kernel, far),
        out_shape=(shape(steps, width, dtype=jnp.bfloat16),)
        + (shape(steps, depth, dtype=jnp.bfloat16),) * len(far),
        in_specs=[smem] + [vmem] * (5 + len(sums)),
        out_specs=(vmem,) * (1 + len(far)),
        compiler_params=params,
        name="finish",
    )(place, local, w, g, const, basis, *sums)
    arrived = [
        lax.ppermute(part, "mode", [(a, a ^ piece) for a in range(pieces)])
        for piece, part in zip(far, parts)
    ]
    grad_obs = pl.pallas_call(
        functools.partial(rest_kernel, near),
        out_shape=shape(steps, depth),
        in_specs=[smem] + [vmem] * 2,
        out_specs=vmem,
        compiler_params=params,
        cost_estimate=pl.CostEstimate(flops=80000000, bytes_accessed=1500000, transcendentals=0),
        name="rest",
    )(place, residual, basis)
    for part in arrived:
        grad_obs = grad_obs + part.astype(F32)
    return grad_obs


def solution(mesh):
    placed = (P("tm", "mode"), P(None, "mode"), P("mode"), P("mode"), P())
    return jax.shard_map(
        shards, mesh=mesh, in_specs=placed, out_specs=P("tm", "mode"), check_vma=False
    )
```

```python
import functools
import math

import jax
import jax.numpy as jnp
from jax import lax
from jax.experimental import pallas as pl
from jax.experimental.pallas import tpu as pltpu
from jax.sharding import PartitionSpec as P

F32 = jnp.float32
SUB = 8
VMEM_LIMIT = 24 * 1024 * 1024


def mat_mul(p, q):
    return (
        p[0] * q[0] + p[1] * q[2],
        p[0] * q[1] + p[1] * q[3],
        p[2] * q[0] + p[3] * q[2],
        p[2] * q[1] + p[3] * q[3],
    )


def mat_trans(p):
    return (p[0], p[2], p[1], p[3])


def mat_add(p, q):
    return tuple(a + b for a, b in zip(p, q))


def mat_sub(p, q):
    return tuple(a - b for a, b in zip(p, q))


def mat_pick(flag, p, q):
    return tuple(jnp.where(flag, a, b) for a, b in zip(p, q))


def full(s):
    return (s[0], s[1], s[1], s[2])


def congruence(s, f):
    t = (
        s[0] * f[0] + s[1] * f[2],
        s[0] * f[1] + s[1] * f[3],
        s[1] * f[0] + s[2] * f[2],
        s[1] * f[1] + s[2] * f[3],
    )
    return (f[0] * t[0] + f[2] * t[2], f[0] * t[1] + f[2] * t[3], f[1] * t[1] + f[3] * t[3])


def power(squares, exponent, like):
    one, zero = jnp.ones_like(like), jnp.zeros_like(like)
    out = None
    for bit, base in enumerate(squares):
        flag = (exponent & (1 << bit)) != 0
        if out is None:
            out = mat_pick(flag, base, (one, zero, zero, one))
        else:
            out = mat_pick(flag, mat_mul(out, base), out)
    return out


def gramian(squares, grams, count, like):
    zero = jnp.zeros_like(like)
    out = (zero, zero, zero)
    for bit, (base, gram) in enumerate(zip(squares, grams)):
        flag = (count & (1 << bit)) != 0
        out = mat_pick(flag, mat_add(gram, congruence(out, base)), out)
    return out


def steady_state(scale2, length, noise_var):
    lam = math.sqrt(3.0) / length
    decay = jnp.exp(-lam)
    twice = 2.0 * lam
    fall = jnp.exp(-twice)
    rho = scale2 / noise_var
    series = 1.0 / 604800.0
    for factor in (60480.0, 6720.0, 840.0, 120.0, 20.0, 4.0, 1.0):
        series = series * twice + 1.0 / factor
    lower = fall * twice * twice * twice * (1.0 / 6.0) * series
    loss = 1.0
    for order in (8, 7, 6, 5, 4, 3, 2):
        loss = 1.0 - lam * (1.0 / order) * loss
    loss = lam * loss
    q00 = rho * lower
    q01 = 2.0 * rho * lam * lam * fall
    q11 = rho * (lower + twice * fall)
    slope = decay * lam
    tilt = loss + slope
    g0 = q00 * tilt * tilt + 2.0 * slope * q01 * tilt + slope * slope * q11
    g1 = slope * q01 - decay * (1.0 - lam) * q00
    loss2 = loss * loss
    c2 = decay * decay
    u = (2.0 * decay * loss2 - g1) / c2
    v = (loss2 * loss2 + g0) / c2
    root = jnp.sqrt(v * (v + 4.0 * u + 16.0))
    product = 4.0 * v / (v + root + jnp.sqrt(2.0 * v * (v + 2.0 * u + root)))
    total = 0.5 * (jnp.sqrt(u * u + 4.0 * u - 2.0 * v + 2.0 * root) - u)
    gain0 = total - 2.0 * loss
    gain1 = (product - loss2 - gain0 * tilt) / slope
    inverse = (1.0 - total + product) / c2
    inn = c2 / (1.0 - total + product)
    closed = (1.0 + slope - loss - gain0, slope, -slope - gain1, decay * (1.0 - lam))
    p00 = inn * ((1.0 - lam) * gain0 - lam * gain1) / decay
    p01 = inn * (lam * gain0 + (1.0 + lam) * gain1) / decay
    p11 = (
        p01 * (loss * (1.0 + decay) + 2.0 * slope * slope)
        + slope * decay * (1.0 + lam) * p00
        - q01
        + gain0 * gain1 * inn
    ) / (slope * decay * (1.0 - lam))
    return closed, gain0, gain1, inverse, (rho - p00, -p01, rho - p11)


def coefficients_kernel(blocks, noise_ref, *refs):
    arguments, (const_ref, w_ref, merge_ref, basis_ref, obs_ref) = refs[:4], refs[4:9]
    scale_ref, length_ref, sems = refs[9:]
    targets = (scale_ref, length_ref, obs_ref, basis_ref)
    copies = [
        pltpu.make_async_copy(source, target, sems.at[k])
        for k, (source, target) in enumerate(zip(arguments, targets))
    ]
    for copy in copies:
        copy.start()
    for copy in copies[:2]:
        copy.wait()
    steps = w_ref.shape[1]
    width = scale_ref.shape[1]
    tile = (SUB, width)
    scale2 = jnp.broadcast_to(scale_ref[...], tile)
    length = jnp.broadcast_to(length_ref[...], tile)
    noise_var = jnp.full(tile, noise_ref[0], F32)
    closed, gain0, gain1, inverse, excess = steady_state(scale2, length, noise_var)
    zero = jnp.zeros(tile, F32)

    squares, grams = [closed], [(inverse, zero, zero)]
    doublings = (steps * blocks).bit_length() - 1
    for _ in range(doublings):
        base = squares[-1]
        grams.append(mat_add(grams[-1], congruence(grams[-1], base)))
        squares.append(mat_mul(base, base))
    local = steps.bit_length() - 1
    consts = closed + (gain0, gain1, inverse) + squares[3] + squares[4] + squares[5]
    for place, value in enumerate(consts):
        const_ref[place] = value
    const_ref[len(consts)] = -1.0 / noise_var
    rounds = blocks.bit_length() - 1
    groups = squares[local:-1] + [()], grams[local:], [()] * rounds + [excess]
    values = [value for group in zip(*groups) for part in group for value in part]
    for place, value in enumerate(values):
        merge_ref[place : place + 1, :] = value[0:1, :]

    row = lax.broadcasted_iota(jnp.int32, tile, 0)
    small, gram_small = squares[:3], grams[:3]
    behind = power(small, 7 - row, zero)
    gram = gramian(small, gram_small, 7 - row, zero)
    eight, gram_eight = squares[3], grams[3]
    parts = steps // SUB
    for part in range(parts - 1, -1, -1):
        rows = pl.ds(part * SUB, SUB)
        w_ref[0, rows, :] = behind[0] * gain0 + behind[1] * gain1
        w_ref[1, rows, :] = behind[2] * gain0 + behind[3] * gain1
        k0 = gain0 * gram[0] + gain1 * gram[1]
        k1 = gain0 * gram[1] + gain1 * gram[2]
        w_ref[2, rows, :] = inverse - (k0 * closed[0] + k1 * closed[2])
        w_ref[3, rows, :] = -(k0 * closed[1] + k1 * closed[3])
        if part:
            behind = mat_mul(behind, eight)
            gram = mat_add(gram_eight, congruence(gram, eight))
    ahead = power(small, row, zero)
    for part in range(parts):
        rows = pl.ds(part * SUB, SUB)
        u0, u1 = w_ref[2, rows, :], w_ref[3, rows, :]
        w_ref[2, rows, :] = u0 * ahead[0] + u1 * ahead[2]
        w_ref[3, rows, :] = u0 * ahead[1] + u1 * ahead[3]
        if part < parts - 1:
            ahead = mat_mul(ahead, eight)

    for copy in copies[2:]:
        copy.wait()


def rotate_kernel(first, place_ref, *refs):
    pieces, others = first
    obs_refs, (basis_ref, *refs) = refs[: len(pieces)], refs[len(pieces) :]
    depth = obs_refs[0].shape[1]
    z = None if others is None else refs[0][...]
    for piece, obs_ref in zip(pieces, obs_refs):
        begin = pl.multiple_of((place_ref[0] ^ piece) * depth, depth)
        term = jnp.dot(
            obs_ref[...], basis_ref[pl.ds(begin, depth), :], preferred_element_type=F32
        )
        z = term if z is None else z + term
    if others is None:
        refs[0][...] = z
        return
    _, w_ref, z_ref, sum_ref, scratch, sem = refs
    for line in range(4):
        value = jnp.sum(w_ref[line] * z, axis=0, keepdims=True)
        for block in range(scratch.shape[0]):
            scratch[block, line : line + 1, :] = value
    copy = pltpu.make_async_copy(scratch, sum_ref, sem)
    copy.start()
    z_ref[...] = z
    copy.wait()


def shift(value, by):
    rows = value.shape[0]
    row = lax.broadcasted_iota(jnp.int32, value.shape, 0)
    keep = row >= by if by > 0 else row < rows + by
    return jnp.where(keep, pltpu.roll(value, by % rows, 0), 0.0)


def reach(blocks, me, merge_ref, g_ref):
    tile = (SUB, merge_ref.shape[1])
    rounds = blocks.bit_length() - 1
    values = [
        jnp.broadcast_to(merge_ref[k : k + 1, :], tile) for k in range(7 * rounds + 6)
    ]
    block_squares = [tuple(values[7 * k : 7 * k + 4]) for k in range(rounds)]
    block_grams = [tuple(values[7 * k + 4 : 7 * k + 7]) for k in range(rounds)]
    s, excess = values[-6:-3], values[-3:]
    zero = jnp.zeros(tile, F32)
    row = lax.broadcasted_iota(jnp.int32, tile, 0)
    left = (
        1.0 + excess[0] * s[0] + excess[1] * s[1],
        excess[0] * s[1] + excess[1] * s[2],
        excess[1] * s[0] + excess[2] * s[1],
        1.0 + excess[1] * s[1] + excess[2] * s[2],
    )
    determ = 1.0 / (left[0] * left[3] - left[1] * left[2])
    start = mat_mul((left[3], -left[1], -left[2], left[0]), full(excess))
    start = tuple(x * determ for x in start)
    mine = jnp.full(tile, me, jnp.int32)
    to_me = power(block_squares, mine, zero)
    rest = full(gramian(block_squares, block_grams, blocks - 1 - mine, zero))
    to_state = mat_mul(to_me, start)
    to_adjoint = mat_mul(mat_mul(rest, mat_mul(to_me, block_squares[0])), start)
    for group in range(g_ref.shape[1] // SUB):
        rows = row + group * SUB
        kind = rows & 3
        front = back = rows >> 2
        before, after = back < me, front > me
        gap = jnp.where(before, me - 1 - back, jnp.where(after, front - 1 - me, 0))
        reach = jnp.where(before, me - back, jnp.where(after, back - me, 0))
        near = power(block_squares, gap, zero)
        far = power(block_squares, reach, zero)
        origin = mat_trans(power(block_squares, front, zero))
        left_over = full(gramian(block_squares, block_grams, blocks - 1 - back, zero))
        end = mat_trans(mat_mul(power(block_squares, back, zero), block_squares[0]))
        first = mat_mul(end, left_over)
        state_b = mat_sub(mat_pick(before, near, (zero,) * 4), mat_mul(to_state, first))
        state_l = mat_mul(to_state, origin)
        cross = mat_pick(after, mat_mul(mat_trans(far), left_over), mat_mul(rest, far))
        adjoint_b = mat_sub(mat_mul(to_adjoint, first), cross)
        adjoint_l = mat_sub(
            mat_pick(after, mat_trans(near), (zero,) * 4), mat_mul(to_adjoint, origin)
        )
        place = pl.ds(group * SUB, SUB)
        for output, (from_b, from_l) in enumerate(
            ((adjoint_b[:2], adjoint_l[:2]), (adjoint_b[2:], adjoint_l[2:]),
             (state_b[:2], state_l[:2]), (state_b[2:], state_l[2:]))
        ):
            g_ref[output, place, :] = jnp.where(
                kind < 2,
                jnp.where(kind == 0, from_b[0], from_b[1]),
                jnp.where(kind == 2, from_l[0], from_l[1]),
            )


def local_kernel(blocks, me_ref, z_ref, const_ref, merge_ref, r_ref, g_ref, scratch):
    reach(blocks, me_ref[0], merge_ref, g_ref)
    steps, width = z_ref.shape
    span = steps // SUB
    lanes = 128
    for chunk in range(width // lanes):
        cols = pl.ds(chunk * lanes, lanes)
        scratch[chunk] = z_ref[:, cols]
    for chunk in range(width // lanes):
        cols = pl.ds(chunk * lanes, lanes)
        const = [const_ref[k, :, cols] for k in range(19)]
        f, (k0, k1, inverse) = const[0:4], const[4:7]
        jumps = (const[7:11], const[11:15], const[15:19])
        zero = jnp.zeros((SUB, lanes), F32)
        x0, x1 = zero, zero
        vs = []
        for t in range(span):
            z = scratch[chunk, pl.ds(t, SUB, stride=span), :]
            vs.append(z - x0)
            x0, x1 = f[0] * x0 + f[1] * x1 + k0 * z, f[2] * x0 + f[3] * x1 + k1 * z
        for level, jump in enumerate(jumps):
            s0, s1 = shift(x0, 1 << level), shift(x1, 1 << level)
            x0, x1 = x0 + jump[0] * s0 + jump[1] * s1, x1 + jump[2] * s0 + jump[3] * s1
        x0, x1 = shift(x0, 1), shift(x1, 1)
        for t in range(span):
            vs[t] = (vs[t] - x0) * inverse
            x0, x1 = f[0] * x0 + f[1] * x1, f[2] * x0 + f[3] * x1
        a0, a1 = zero, zero
        for t in range(span - 1, -1, -1):
            a0, a1 = f[0] * a0 + f[2] * a1 + vs[t], f[1] * a0 + f[3] * a1
        for level, jump in enumerate(jumps):
            s0, s1 = shift(a0, -(1 << level)), shift(a1, -(1 << level))
            a0, a1 = a0 + jump[0] * s0 + jump[2] * s1, a1 + jump[1] * s0 + jump[3] * s1
        a0, a1 = shift(a0, -1), shift(a1, -1)
        for t in range(span - 1, -1, -1):
            r = vs[t] - k0 * a0 - k1 * a1
            a0, a1 = f[0] * a0 + f[2] * a1 + vs[t], f[1] * a0 + f[3] * a1
            scratch[chunk, pl.ds(t, SUB, stride=span), :] = r
        r_ref[:, cols] = scratch[chunk]


def rotate_back(residual, pieces, place_ref, basis_ref, outs):
    depth = outs[0].shape[1]
    for piece, out_ref in zip(pieces, outs):
        begin = pl.multiple_of((place_ref[0] ^ piece) * depth, depth)
        out_ref[...] = lax.dot_general(
            residual,
            basis_ref[pl.ds(begin, depth), :],
            (((1,), (1,)), ((), ())),
            preferred_element_type=F32,
        ).astype(out_ref.dtype)


def finish_kernel(pieces, place_ref, r_ref, w_ref, g_ref, const_ref, basis_ref, *refs):
    sums_ref, residual_ref = refs[: -len(pieces)]
    value = r_ref[...]
    for line in range(4):
        total = None
        for block in range(sums_ref.shape[0]):
            term = g_ref[line, pl.ds(4 * block, 4), :] * sums_ref[block]
            total = term if total is None else total + term
        value = value - w_ref[line] * jnp.sum(total, axis=0, keepdims=True)
    scale = const_ref[19, 0:1, :]
    residual = (value * scale).astype(jnp.bfloat16)
    residual_ref[...] = residual
    rotate_back(residual, pieces, place_ref, basis_ref, refs[-len(pieces) :])


def rest_kernel(pieces, place_ref, residual_ref, basis_ref, *outs):
    rotate_back(residual_ref[...], pieces, place_ref, basis_ref, outs)


def exchange(value, axis, count):
    out = [value]
    for step in range(1, count):
        out.append(lax.ppermute(value, axis, [(a, a ^ step) for a in range(count)]))
    return out


def shards(observations, basis, eigvals, lengths, noise):
    steps, depth = observations.shape
    width = basis.shape[1]
    blocks, pieces = lax.axis_size("tm"), lax.axis_size("mode")
    me = lax.axis_index("tm").astype(jnp.int32).reshape(1)
    place = lax.axis_index("mode").astype(jnp.int32).reshape(1)
    rounds = blocks.bit_length() - 1
    vmem = pl.BlockSpec(memory_space=pltpu.VMEM)
    smem = pl.BlockSpec(memory_space=pltpu.SMEM)
    params = pltpu.CompilerParams(vmem_limit_bytes=VMEM_LIMIT)

    def shape(*dims, dtype=F32):
        return jax.ShapeDtypeStruct(dims, dtype)

    obs = exchange(observations, "mode", pieces)
    const, w, merges, basis, obs[0] = pl.pallas_call(
        functools.partial(coefficients_kernel, blocks),
        out_shape=(
            shape(20, SUB, width),
            shape(4, steps, width),
            shape(-(-(7 * rounds + 6) // SUB) * SUB, width),
            shape(*basis.shape, dtype=basis.dtype),
            shape(steps, depth, dtype=observations.dtype),
        ),
        in_specs=[smem] + [pl.BlockSpec(memory_space=pltpu.HBM)] * 4,
        out_specs=(vmem,) * 5,
        scratch_shapes=[
            pltpu.VMEM((1, width), F32),
            pltpu.VMEM((1, width), F32),
            pltpu.SemaphoreType.DMA((4,)),
        ],
        compiler_params=params,
        cost_estimate=pl.CostEstimate(flops=20000000, bytes_accessed=2000000, transcendentals=0),
        name="coefficients",
    )(
        noise,
        *(
            pltpu.with_memory_space_constraint(x, pltpu.HBM)
            for x in (
                eigvals.reshape(1, width),
                lengths.reshape(1, width),
                observations,
                basis,
            )
        ),
    )
    last = pieces - 1
    early = list(range(last))
    z = pl.pallas_call(
        functools.partial(rotate_kernel, (early, None)),
        out_shape=shape(steps, width),
        in_specs=[smem] + [vmem] * pieces,
        out_specs=vmem,
        compiler_params=params,
        name="rotate_early",
    )(place, *(obs[piece] for piece in early), basis)
    z, summary = pl.pallas_call(
        functools.partial(rotate_kernel, ([last], early)),
        out_shape=(shape(steps, width), shape(blocks, 4, width)),
        in_specs=[smem] + [vmem] * 4,
        out_specs=(vmem, pl.BlockSpec(memory_space=pltpu.HBM)),
        scratch_shapes=[pltpu.VMEM((blocks, 4, width), F32), pltpu.SemaphoreType.DMA],
        compiler_params=params,
        name="rotate_last",
    )(place, obs[last], basis, z, w)
    sums = lax.all_to_all(summary, "tm", 0, 0)
    local, g = pl.pallas_call(
        functools.partial(local_kernel, blocks),
        out_shape=(shape(steps, width), shape(4, 4 * blocks, width)),
        in_specs=[smem] + [vmem] * 3,
        out_specs=(vmem,) * 2,
        scratch_shapes=[pltpu.VMEM((width // 128, steps, 128), F32)],
        compiler_params=params,
        cost_estimate=pl.CostEstimate(flops=10000000, bytes_accessed=1000000, transcendentals=0),
        name="local",
    )(me, z, const, merges)
    far = list(range(2, pieces)) + [1]
    near = [0]
    residual, *parts = pl.pallas_call(
        functools.partial(finish_kernel, far),
        out_shape=(shape(steps, width, dtype=jnp.bfloat16),)
        + (shape(steps, depth, dtype=jnp.bfloat16),) * len(far),
        in_specs=[smem] + [vmem] * 6,
        out_specs=(vmem,) * (1 + len(far)),
        compiler_params=params,
        name="finish",
    )(place, local, w, g, const, basis, sums)
    arrived = [
        lax.ppermute(part, "mode", [(a, a ^ piece) for a in range(pieces)])
        for piece, part in zip(far, parts)
    ]
    grad_obs = pl.pallas_call(
        functools.partial(rest_kernel, near),
        out_shape=shape(steps, depth),
        in_specs=[smem] + [vmem] * 2,
        out_specs=vmem,
        compiler_params=params,
        cost_estimate=pl.CostEstimate(flops=80000000, bytes_accessed=1500000, transcendentals=0),
        name="rest",
    )(place, residual, basis)
    for part in arrived:
        grad_obs = grad_obs + part.astype(F32)
    return grad_obs


def solution(mesh):
    placed = (P("tm", "mode"), P(None, "mode"), P("mode"), P("mode"), P())
    return jax.shard_map(
        shards, mesh=mesh, in_specs=placed, out_specs=P("tm", "mode"), check_vma=False
    )
```

```python
import functools
import math

import jax
import jax.numpy as jnp
from jax import lax
from jax.experimental import pallas as pl
from jax.experimental.pallas import tpu as pltpu
from jax.sharding import PartitionSpec as P

F32 = jnp.float32
SUB = 8
VMEM_LIMIT = 24 * 1024 * 1024


def mat_mul(p, q):
    return (
        p[0] * q[0] + p[1] * q[2],
        p[0] * q[1] + p[1] * q[3],
        p[2] * q[0] + p[3] * q[2],
        p[2] * q[1] + p[3] * q[3],
    )


def mat_trans(p):
    return (p[0], p[2], p[1], p[3])


def mat_add(p, q):
    return tuple(a + b for a, b in zip(p, q))


def mat_sub(p, q):
    return tuple(a - b for a, b in zip(p, q))


def mat_pick(flag, p, q):
    return tuple(jnp.where(flag, a, b) for a, b in zip(p, q))


def full(s):
    return (s[0], s[1], s[1], s[2])


def congruence(s, f):
    t = (
        s[0] * f[0] + s[1] * f[2],
        s[0] * f[1] + s[1] * f[3],
        s[1] * f[0] + s[2] * f[2],
        s[1] * f[1] + s[2] * f[3],
    )
    return (f[0] * t[0] + f[2] * t[2], f[0] * t[1] + f[2] * t[3], f[1] * t[1] + f[3] * t[3])


def power(squares, exponent, like):
    one, zero = jnp.ones_like(like), jnp.zeros_like(like)
    out = None
    for bit, base in enumerate(squares):
        flag = (exponent & (1 << bit)) != 0
        if out is None:
            out = mat_pick(flag, base, (one, zero, zero, one))
        else:
            out = mat_pick(flag, mat_mul(out, base), out)
    return out


def gramian(squares, grams, count, like):
    zero = jnp.zeros_like(like)
    out = (zero, zero, zero)
    for bit, (base, gram) in enumerate(zip(squares, grams)):
        flag = (count & (1 << bit)) != 0
        out = mat_pick(flag, mat_add(gram, congruence(out, base)), out)
    return out


def steady_state(scale2, length, noise_var):
    lam = math.sqrt(3.0) / length
    decay = jnp.exp(-lam)
    twice = 2.0 * lam
    fall = jnp.exp(-twice)
    rho = scale2 / noise_var
    series = 1.0 / 604800.0
    for factor in (60480.0, 6720.0, 840.0, 120.0, 20.0, 4.0, 1.0):
        series = series * twice + 1.0 / factor
    lower = fall * twice * twice * twice * (1.0 / 6.0) * series
    loss = 1.0
    for order in (8, 7, 6, 5, 4, 3, 2):
        loss = 1.0 - lam * (1.0 / order) * loss
    loss = lam * loss
    q00 = rho * lower
    q01 = 2.0 * rho * lam * lam * fall
    q11 = rho * (lower + twice * fall)
    slope = decay * lam
    tilt = loss + slope
    g0 = q00 * tilt * tilt + 2.0 * slope * q01 * tilt + slope * slope * q11
    g1 = slope * q01 - decay * (1.0 - lam) * q00
    loss2 = loss * loss
    c2 = decay * decay
    u = (2.0 * decay * loss2 - g1) / c2
    v = (loss2 * loss2 + g0) / c2
    root = jnp.sqrt(v * (v + 4.0 * u + 16.0))
    product = 4.0 * v / (v + root + jnp.sqrt(2.0 * v * (v + 2.0 * u + root)))
    total = 0.5 * (jnp.sqrt(u * u + 4.0 * u - 2.0 * v + 2.0 * root) - u)
    gain0 = total - 2.0 * loss
    gain1 = (product - loss2 - gain0 * tilt) / slope
    inverse = (1.0 - total + product) / c2
    inn = c2 / (1.0 - total + product)
    closed = (1.0 + slope - loss - gain0, slope, -slope - gain1, decay * (1.0 - lam))
    p00 = inn * ((1.0 - lam) * gain0 - lam * gain1) / decay
    p01 = inn * (lam * gain0 + (1.0 + lam) * gain1) / decay
    p11 = (
        p01 * (loss * (1.0 + decay) + 2.0 * slope * slope)
        + slope * decay * (1.0 + lam) * p00
        - q01
        + gain0 * gain1 * inn
    ) / (slope * decay * (1.0 - lam))
    return closed, gain0, gain1, inverse, (rho - p00, -p01, rho - p11)


def coefficients_kernel(blocks, noise_ref, *refs):
    arguments, (const_ref, w_ref, merge_ref, basis_ref, obs_ref) = refs[:4], refs[4:9]
    scale_ref, length_ref, sems = refs[9:]
    targets = (scale_ref, length_ref, obs_ref, basis_ref)
    copies = [
        pltpu.make_async_copy(source, target, sems.at[k])
        for k, (source, target) in enumerate(zip(arguments, targets))
    ]
    for copy in copies:
        copy.start()
    for copy in copies[:2]:
        copy.wait()
    steps = w_ref.shape[1]
    width = scale_ref.shape[1]
    tile = (SUB, width)
    scale2 = jnp.broadcast_to(scale_ref[...], tile)
    length = jnp.broadcast_to(length_ref[...], tile)
    noise_var = jnp.full(tile, noise_ref[0], F32)
    closed, gain0, gain1, inverse, excess = steady_state(scale2, length, noise_var)
    zero = jnp.zeros(tile, F32)

    squares, grams = [closed], [(inverse, zero, zero)]
    doublings = (steps * blocks).bit_length() - 1
    for _ in range(doublings):
        base = squares[-1]
        grams.append(mat_add(grams[-1], congruence(grams[-1], base)))
        squares.append(mat_mul(base, base))
    local = steps.bit_length() - 1
    consts = closed + (gain0, gain1, inverse) + squares[3] + squares[4] + squares[5]
    for place, value in enumerate(consts):
        const_ref[place] = value
    const_ref[len(consts)] = -1.0 / noise_var
    rounds = blocks.bit_length() - 1
    groups = squares[local:-1] + [()], grams[local:], [()] * rounds + [excess]
    values = [value for group in zip(*groups) for part in group for value in part]
    for place, value in enumerate(values):
        merge_ref[place : place + 1, :] = value[0:1, :]

    row = lax.broadcasted_iota(jnp.int32, tile, 0)
    small, gram_small = squares[:3], grams[:3]
    behind = power(small, 7 - row, zero)
    gram = gramian(small, gram_small, 7 - row, zero)
    eight, gram_eight = squares[3], grams[3]
    parts = steps // SUB
    for part in range(parts - 1, -1, -1):
        rows = pl.ds(part * SUB, SUB)
        w_ref[0, rows, :] = behind[0] * gain0 + behind[1] * gain1
        w_ref[1, rows, :] = behind[2] * gain0 + behind[3] * gain1
        k0 = gain0 * gram[0] + gain1 * gram[1]
        k1 = gain0 * gram[1] + gain1 * gram[2]
        w_ref[2, rows, :] = inverse - (k0 * closed[0] + k1 * closed[2])
        w_ref[3, rows, :] = -(k0 * closed[1] + k1 * closed[3])
        if part:
            behind = mat_mul(behind, eight)
            gram = mat_add(gram_eight, congruence(gram, eight))
    ahead = power(small, row, zero)
    for part in range(parts):
        rows = pl.ds(part * SUB, SUB)
        u0, u1 = w_ref[2, rows, :], w_ref[3, rows, :]
        w_ref[2, rows, :] = u0 * ahead[0] + u1 * ahead[2]
        w_ref[3, rows, :] = u0 * ahead[1] + u1 * ahead[3]
        if part < parts - 1:
            ahead = mat_mul(ahead, eight)

    for copy in copies[2:]:
        copy.wait()


def rotate_kernel(first, place_ref, *refs):
    pieces, stage = first
    obs_refs, (basis_ref, *refs) = refs[: len(pieces)], refs[len(pieces) :]
    depth = obs_refs[0].shape[1]
    z = refs[0][...] if stage else None
    for piece, obs_ref in zip(pieces, obs_refs):
        begin = pl.multiple_of((place_ref[0] ^ piece) * depth, depth)
        term = jnp.dot(
            obs_ref[...], basis_ref[pl.ds(begin, depth), :], preferred_element_type=F32
        )
        z = term if z is None else z + term
    if stage < 2:
        refs[-1][...] = z
        return
    _, w_ref, z_ref, sum_ref = refs
    z_ref[...] = z
    for line in range(4):
        sum_ref[line : line + 1, :] = jnp.sum(w_ref[line] * z, axis=0, keepdims=True)


def merge(level, me, own, other, merge_ref):
    lower = jnp.full(own.shape, (me >> level) & 1, jnp.int32) == 0
    left, right = jnp.where(lower, own, other), jnp.where(lower, other, own)
    f00, f01, f10, f11, s00, s01, s11 = (
        merge_ref[7 * level + k : 7 * level + k + 1, :] for k in range(7)
    )
    b0, b1 = left[0:1, :], left[1:2, :]
    a0 = right[2:3, :] - s00 * b0 - s01 * b1
    a1 = right[3:4, :] - s01 * b0 - s11 * b1
    return jnp.concatenate(
        (
            right[0:1, :] + f00 * b0 + f01 * b1,
            right[1:2, :] + f10 * b0 + f11 * b1,
            left[2:3, :] + f00 * a0 + f10 * a1,
            left[3:4, :] + f01 * a0 + f11 * a1,
        ),
        axis=0,
    )


def merge_kernel(level, me_ref, merge_ref, *refs):
    *parts, out_ref = refs
    me = me_ref[0]
    parts = [ref[...] for ref in parts]
    if level:
        out_ref[...] = merge(level, me, parts[0], parts[1], merge_ref)
    else:
        near = merge(0, me, parts[0], parts[1], merge_ref)
        far = merge(0, me, parts[2], parts[3], merge_ref)
        out_ref[...] = merge(1, me, near, far, merge_ref)


def shift(value, by):
    rows = value.shape[0]
    row = lax.broadcasted_iota(jnp.int32, value.shape, 0)
    keep = row >= by if by > 0 else row < rows + by
    return jnp.where(keep, pltpu.roll(value, by % rows, 0), 0.0)


def reach(blocks, me, merge_ref, g_ref):
    tile = (SUB, merge_ref.shape[1])
    rounds = blocks.bit_length() - 1
    values = [
        jnp.broadcast_to(merge_ref[k : k + 1, :], tile) for k in range(7 * rounds + 6)
    ]
    block_squares = [tuple(values[7 * k : 7 * k + 4]) for k in range(rounds)]
    block_grams = [tuple(values[7 * k + 4 : 7 * k + 7]) for k in range(rounds)]
    s, excess = values[-6:-3], values[-3:]
    zero = jnp.zeros(tile, F32)
    row = lax.broadcasted_iota(jnp.int32, tile, 0)
    left = (
        1.0 + excess[0] * s[0] + excess[1] * s[1],
        excess[0] * s[1] + excess[1] * s[2],
        excess[1] * s[0] + excess[2] * s[1],
        1.0 + excess[1] * s[1] + excess[2] * s[2],
    )
    determ = 1.0 / (left[0] * left[3] - left[1] * left[2])
    start = mat_mul((left[3], -left[1], -left[2], left[0]), full(excess))
    start = tuple(x * determ for x in start)
    mine = jnp.full(tile, me, jnp.int32)
    to_me = power(block_squares, mine, zero)
    rest = full(gramian(block_squares, block_grams, blocks - 1 - mine, zero))
    to_state = mat_mul(to_me, start)
    to_adjoint = mat_mul(mat_mul(rest, mat_mul(to_me, block_squares[0])), start)
    for group in range(g_ref.shape[1] // SUB):
        rows = row + group * SUB
        kind = rows & 3
        line = rows >> 2
        span = jnp.where(line < 4, 1, jnp.left_shift(1, jnp.maximum(line - 2, 0)))
        near_me = mine ^ jnp.where(line < 4, line, span)
        front = jnp.minimum((near_me // span) * span, blocks - 1)
        back = jnp.minimum(front + span - 1, blocks - 1)
        before, after = back < me, front > me
        gap = jnp.where(before, me - 1 - back, jnp.where(after, front - 1 - me, 0))
        reach = jnp.where(before, me - back, jnp.where(after, back - me, 0))
        near = power(block_squares, gap, zero)
        far = power(block_squares, reach, zero)
        origin = mat_trans(power(block_squares, front, zero))
        left_over = full(gramian(block_squares, block_grams, blocks - 1 - back, zero))
        end = mat_trans(mat_mul(power(block_squares, back, zero), block_squares[0]))
        first = mat_mul(end, left_over)
        state_b = mat_sub(mat_pick(before, near, (zero,) * 4), mat_mul(to_state, first))
        state_l = mat_mul(to_state, origin)
        cross = mat_pick(after, mat_mul(mat_trans(far), left_over), mat_mul(rest, far))
        adjoint_b = mat_sub(mat_mul(to_adjoint, first), cross)
        adjoint_l = mat_sub(
            mat_pick(after, mat_trans(near), (zero,) * 4), mat_mul(to_adjoint, origin)
        )
        place = pl.ds(group * SUB, SUB)
        for output, (from_b, from_l) in enumerate(
            ((adjoint_b[:2], adjoint_l[:2]), (adjoint_b[2:], adjoint_l[2:]),
             (state_b[:2], state_l[:2]), (state_b[2:], state_l[2:]))
        ):
            g_ref[output, place, :] = jnp.where(
                kind < 2,
                jnp.where(kind == 0, from_b[0], from_b[1]),
                jnp.where(kind == 2, from_l[0], from_l[1]),
            )


def local_kernel(blocks, me_ref, z_ref, const_ref, merge_ref, r_ref, g_ref, scratch):
    reach(blocks, me_ref[0], merge_ref, g_ref)
    steps, width = z_ref.shape
    span = steps // SUB
    lanes = 128
    for chunk in range(width // lanes):
        cols = pl.ds(chunk * lanes, lanes)
        scratch[chunk] = z_ref[:, cols]
    for chunk in range(width // lanes):
        cols = pl.ds(chunk * lanes, lanes)
        const = [const_ref[k, :, cols] for k in range(19)]
        f, (k0, k1, inverse) = const[0:4], const[4:7]
        jumps = (const[7:11], const[11:15], const[15:19])
        zero = jnp.zeros((SUB, lanes), F32)
        x0, x1 = zero, zero
        vs = []
        for t in range(span):
            z = scratch[chunk, pl.ds(t, SUB, stride=span), :]
            vs.append(z - x0)
            x0, x1 = f[0] * x0 + f[1] * x1 + k0 * z, f[2] * x0 + f[3] * x1 + k1 * z
        for level, jump in enumerate(jumps):
            s0, s1 = shift(x0, 1 << level), shift(x1, 1 << level)
            x0, x1 = x0 + jump[0] * s0 + jump[1] * s1, x1 + jump[2] * s0 + jump[3] * s1
        x0, x1 = shift(x0, 1), shift(x1, 1)
        for t in range(span):
            vs[t] = (vs[t] - x0) * inverse
            x0, x1 = f[0] * x0 + f[1] * x1, f[2] * x0 + f[3] * x1
        a0, a1 = zero, zero
        for t in range(span - 1, -1, -1):
            a0, a1 = f[0] * a0 + f[2] * a1 + vs[t], f[1] * a0 + f[3] * a1
        for level, jump in enumerate(jumps):
            s0, s1 = shift(a0, -(1 << level)), shift(a1, -(1 << level))
            a0, a1 = a0 + jump[0] * s0 + jump[2] * s1, a1 + jump[1] * s0 + jump[3] * s1
        a0, a1 = shift(a0, -1), shift(a1, -1)
        for t in range(span - 1, -1, -1):
            r = vs[t] - k0 * a0 - k1 * a1
            a0, a1 = f[0] * a0 + f[2] * a1 + vs[t], f[1] * a0 + f[3] * a1
            scratch[chunk, pl.ds(t, SUB, stride=span), :] = r
        r_ref[:, cols] = scratch[chunk]


def rotate_back(residual, pieces, place_ref, basis_ref, outs):
    depth = outs[0].shape[1]
    for piece, out_ref in zip(pieces, outs):
        begin = pl.multiple_of((place_ref[0] ^ piece) * depth, depth)
        out_ref[...] = lax.dot_general(
            residual,
            basis_ref[pl.ds(begin, depth), :],
            (((1,), (1,)), ((), ())),
            preferred_element_type=F32,
        ).astype(out_ref.dtype)


def finish_kernel(pieces, place_ref, r_ref, w_ref, g_ref, const_ref, basis_ref, *refs):
    *sums, residual_ref = refs[: -len(pieces)]
    value = r_ref[...]
    for line in range(4):
        total = None
        for place, sum_ref in enumerate(sums):
            term = g_ref[line, pl.ds(4 * place, 4), :] * sum_ref[...]
            total = term if total is None else total + term
        value = value - w_ref[line] * jnp.sum(total, axis=0, keepdims=True)
    scale = const_ref[19, 0:1, :]
    residual = (value * scale).astype(jnp.bfloat16)
    residual_ref[...] = residual
    rotate_back(residual, pieces, place_ref, basis_ref, refs[-len(pieces) :])


def rest_kernel(pieces, place_ref, residual_ref, basis_ref, *outs):
    rotate_back(residual_ref[...], pieces, place_ref, basis_ref, outs)


def exchange(value, axis, count):
    out = [value]
    for step in range(1, count):
        out.append(lax.ppermute(value, axis, [(a, a ^ step) for a in range(count)]))
    return out


def shards(observations, basis, eigvals, lengths, noise):
    steps, depth = observations.shape
    width = basis.shape[1]
    blocks, pieces = lax.axis_size("tm"), lax.axis_size("mode")
    me = lax.axis_index("tm").astype(jnp.int32).reshape(1)
    place = lax.axis_index("mode").astype(jnp.int32).reshape(1)
    rounds = blocks.bit_length() - 1
    vmem = pl.BlockSpec(memory_space=pltpu.VMEM)
    smem = pl.BlockSpec(memory_space=pltpu.SMEM)
    params = pltpu.CompilerParams(vmem_limit_bytes=VMEM_LIMIT)

    def shape(*dims, dtype=F32):
        return jax.ShapeDtypeStruct(dims, dtype)

    obs = exchange(observations, "mode", pieces)
    const, w, merges, basis, obs[0] = pl.pallas_call(
        functools.partial(coefficients_kernel, blocks),
        out_shape=(
            shape(20, SUB, width),
            shape(4, steps, width),
            shape(-(-(7 * rounds + 6) // SUB) * SUB, width),
            shape(*basis.shape, dtype=basis.dtype),
            shape(steps, depth, dtype=observations.dtype),
        ),
        in_specs=[smem] + [pl.BlockSpec(memory_space=pltpu.HBM)] * 4,
        out_specs=(vmem,) * 5,
        scratch_shapes=[
            pltpu.VMEM((1, width), F32),
            pltpu.VMEM((1, width), F32),
            pltpu.SemaphoreType.DMA((4,)),
        ],
        compiler_params=params,
        cost_estimate=pl.CostEstimate(flops=20000000, bytes_accessed=2000000, transcendentals=0),
        name="coefficients",
    )(
        noise,
        *(
            pltpu.with_memory_space_constraint(x, pltpu.HBM)
            for x in (
                eigvals.reshape(1, width),
                lengths.reshape(1, width),
                observations,
                basis,
            )
        ),
    )
    *early, last = [[0, 1], *([piece] for piece in range(2, pieces))] if pieces > 2 else [[0], [1]]
    z = ()
    for group in early:
        z = pl.pallas_call(
            functools.partial(rotate_kernel, (group, len(z))),
            out_shape=shape(steps, width),
            in_specs=[smem] + [vmem] * (len(group) + 1 + len(z)),
            out_specs=vmem,
            compiler_params=params,
            name="rotate_early",
        )(place, *(obs[piece] for piece in group), basis, *z)
        z = (z,)
    z, summary = pl.pallas_call(
        functools.partial(rotate_kernel, (last, 2)),
        out_shape=(shape(steps, width), shape(4, width)),
        in_specs=[smem] + [vmem] * 4,
        out_specs=(vmem,) * 2,
        compiler_params=params,
        name="rotate_last",
    )(place, obs[last[0]], basis, *z, w)
    sums = [summary]
    for step in range(1, 4):
        sums.append(lax.ppermute(summary, "tm", [(a, a ^ step) for a in range(blocks)]))
    for level in range(2, rounds):
        summary = pl.pallas_call(
            functools.partial(merge_kernel, 0 if level == 2 else level - 1),
            out_shape=shape(4, width),
            in_specs=[smem] + [vmem] * (5 if level == 2 else 3),
            out_specs=vmem,
            compiler_params=params,
            name="merge",
        )(me, merges, *(sums if level == 2 else (summary, sums[-1])))
        step = 1 << level
        sums.append(lax.ppermute(summary, "tm", [(a, a ^ step) for a in range(blocks)]))
    local, g = pl.pallas_call(
        functools.partial(local_kernel, blocks),
        out_shape=(shape(steps, width), shape(4, -(-4 * (rounds + 2) // SUB) * SUB, width)),
        in_specs=[smem] + [vmem] * 3,
        out_specs=(vmem,) * 2,
        scratch_shapes=[pltpu.VMEM((width // 128, steps, 128), F32)],
        compiler_params=params,
        cost_estimate=pl.CostEstimate(flops=10000000, bytes_accessed=1000000, transcendentals=0),
        name="local",
    )(me, z, const, merges)
    far = list(range(pieces - 1, 0, -1))
    near = [0]
    residual, *parts = pl.pallas_call(
        functools.partial(finish_kernel, far),
        out_shape=(shape(steps, width, dtype=jnp.bfloat16),)
        + (shape(steps, depth, dtype=jnp.bfloat16),) * len(far),
        in_specs=[smem] + [vmem] * (5 + len(sums)),
        out_specs=(vmem,) * (1 + len(far)),
        compiler_params=params,
        name="finish",
    )(place, local, w, g, const, basis, *sums)
    arrived = [
        lax.ppermute(part, "mode", [(a, a ^ piece) for a in range(pieces)])
        for piece, part in zip(far, parts)
    ]
    grad_obs = pl.pallas_call(
        functools.partial(rest_kernel, near),
        out_shape=shape(steps, depth),
        in_specs=[smem] + [vmem] * 2,
        out_specs=vmem,
        compiler_params=params,
        cost_estimate=pl.CostEstimate(flops=80000000, bytes_accessed=1500000, transcendentals=0),
        name="rest",
    )(place, residual, basis)
    for part in arrived:
        grad_obs = grad_obs + part.astype(F32)
    return grad_obs


def solution(mesh):
    placed = (P("tm", "mode"), P(None, "mode"), P("mode"), P("mode"), P())
    return jax.shard_map(
        shards, mesh=mesh, in_specs=placed, out_specs=P("tm", "mode"), check_vma=False
    )
```

```python
import functools
import math

import jax
import jax.numpy as jnp
from jax import lax
from jax.experimental import pallas as pl
from jax.experimental.pallas import tpu as pltpu
from jax.sharding import PartitionSpec as P

F32 = jnp.float32
SUB = 8
VMEM_LIMIT = 24 * 1024 * 1024


def mat_mul(p, q):
    return (
        p[0] * q[0] + p[1] * q[2],
        p[0] * q[1] + p[1] * q[3],
        p[2] * q[0] + p[3] * q[2],
        p[2] * q[1] + p[3] * q[3],
    )


def mat_trans(p):
    return (p[0], p[2], p[1], p[3])


def mat_add(p, q):
    return tuple(a + b for a, b in zip(p, q))


def mat_sub(p, q):
    return tuple(a - b for a, b in zip(p, q))


def mat_pick(flag, p, q):
    return tuple(jnp.where(flag, a, b) for a, b in zip(p, q))


def full(s):
    return (s[0], s[1], s[1], s[2])


def congruence(s, f):
    t = (
        s[0] * f[0] + s[1] * f[2],
        s[0] * f[1] + s[1] * f[3],
        s[1] * f[0] + s[2] * f[2],
        s[1] * f[1] + s[2] * f[3],
    )
    return (f[0] * t[0] + f[2] * t[2], f[0] * t[1] + f[2] * t[3], f[1] * t[1] + f[3] * t[3])


def power(squares, exponent, like):
    one, zero = jnp.ones_like(like), jnp.zeros_like(like)
    out = None
    for bit, base in enumerate(squares):
        flag = (exponent & (1 << bit)) != 0
        if out is None:
            out = mat_pick(flag, base, (one, zero, zero, one))
        else:
            out = mat_pick(flag, mat_mul(out, base), out)
    return out


def gramian(squares, grams, count, like):
    zero = jnp.zeros_like(like)
    out = (zero, zero, zero)
    for bit, (base, gram) in enumerate(zip(squares, grams)):
        flag = (count & (1 << bit)) != 0
        out = mat_pick(flag, mat_add(gram, congruence(out, base)), out)
    return out


def steady_state(scale2, length, noise_var):
    lam = math.sqrt(3.0) / length
    decay = jnp.exp(-lam)
    twice = 2.0 * lam
    fall = jnp.exp(-twice)
    rho = scale2 / noise_var
    series = 1.0 / 604800.0
    for factor in (60480.0, 6720.0, 840.0, 120.0, 20.0, 4.0, 1.0):
        series = series * twice + 1.0 / factor
    lower = fall * twice * twice * twice * (1.0 / 6.0) * series
    loss = 1.0
    for order in (8, 7, 6, 5, 4, 3, 2):
        loss = 1.0 - lam * (1.0 / order) * loss
    loss = lam * loss
    q00 = rho * lower
    q01 = 2.0 * rho * lam * lam * fall
    q11 = rho * (lower + twice * fall)
    slope = decay * lam
    tilt = loss + slope
    g0 = q00 * tilt * tilt + 2.0 * slope * q01 * tilt + slope * slope * q11
    g1 = slope * q01 - decay * (1.0 - lam) * q00
    loss2 = loss * loss
    c2 = decay * decay
    u = (2.0 * decay * loss2 - g1) / c2
    v = (loss2 * loss2 + g0) / c2
    root = jnp.sqrt(v * (v + 4.0 * u + 16.0))
    product = 4.0 * v / (v + root + jnp.sqrt(2.0 * v * (v + 2.0 * u + root)))
    total = 0.5 * (jnp.sqrt(u * u + 4.0 * u - 2.0 * v + 2.0 * root) - u)
    gain0 = total - 2.0 * loss
    gain1 = (product - loss2 - gain0 * tilt) / slope
    inverse = (1.0 - total + product) / c2
    inn = c2 / (1.0 - total + product)
    closed = (1.0 + slope - loss - gain0, slope, -slope - gain1, decay * (1.0 - lam))
    p00 = inn * ((1.0 - lam) * gain0 - lam * gain1) / decay
    p01 = inn * (lam * gain0 + (1.0 + lam) * gain1) / decay
    p11 = (
        p01 * (loss * (1.0 + decay) + 2.0 * slope * slope)
        + slope * decay * (1.0 + lam) * p00
        - q01
        + gain0 * gain1 * inn
    ) / (slope * decay * (1.0 - lam))
    return closed, gain0, gain1, inverse, (rho - p00, -p01, rho - p11)


def coefficients_kernel(blocks, noise_ref, *refs):
    arguments, (const_ref, w_ref, merge_ref, basis_ref, obs_ref) = refs[:4], refs[4:9]
    scale_ref, length_ref, sems = refs[9:]
    targets = (scale_ref, length_ref, obs_ref, basis_ref)
    copies = [
        pltpu.make_async_copy(source, target, sems.at[k])
        for k, (source, target) in enumerate(zip(arguments, targets))
    ]
    for copy in copies:
        copy.start()
    for copy in copies[:2]:
        copy.wait()
    steps = w_ref.shape[1]
    width = scale_ref.shape[1]
    tile = (SUB, width)
    scale2 = jnp.broadcast_to(scale_ref[...], tile)
    length = jnp.broadcast_to(length_ref[...], tile)
    noise_var = jnp.full(tile, noise_ref[0], F32)
    closed, gain0, gain1, inverse, excess = steady_state(scale2, length, noise_var)
    zero = jnp.zeros(tile, F32)

    squares, grams = [closed], [(inverse, zero, zero)]
    doublings = (steps * blocks).bit_length() - 1
    for _ in range(doublings):
        base = squares[-1]
        grams.append(mat_add(grams[-1], congruence(grams[-1], base)))
        squares.append(mat_mul(base, base))
    local = steps.bit_length() - 1
    consts = closed + (gain0, gain1, inverse) + squares[3] + squares[4] + squares[5]
    for place, value in enumerate(consts):
        const_ref[place] = value
    const_ref[len(consts)] = -1.0 / noise_var
    rounds = blocks.bit_length() - 1
    groups = squares[local:-1] + [()], grams[local:], [()] * rounds + [excess]
    values = [value for group in zip(*groups) for part in group for value in part]
    for place, value in enumerate(values):
        merge_ref[place : place + 1, :] = value[0:1, :]

    row = lax.broadcasted_iota(jnp.int32, tile, 0)
    small, gram_small = squares[:3], grams[:3]
    behind = power(small, 7 - row, zero)
    gram = gramian(small, gram_small, 7 - row, zero)
    eight, gram_eight = squares[3], grams[3]
    parts = steps // SUB
    for part in range(parts - 1, -1, -1):
        rows = pl.ds(part * SUB, SUB)
        w_ref[0, rows, :] = behind[0] * gain0 + behind[1] * gain1
        w_ref[1, rows, :] = behind[2] * gain0 + behind[3] * gain1
        k0 = gain0 * gram[0] + gain1 * gram[1]
        k1 = gain0 * gram[1] + gain1 * gram[2]
        w_ref[2, rows, :] = inverse - (k0 * closed[0] + k1 * closed[2])
        w_ref[3, rows, :] = -(k0 * closed[1] + k1 * closed[3])
        if part:
            behind = mat_mul(behind, eight)
            gram = mat_add(gram_eight, congruence(gram, eight))
    ahead = power(small, row, zero)
    for part in range(parts):
        rows = pl.ds(part * SUB, SUB)
        u0, u1 = w_ref[2, rows, :], w_ref[3, rows, :]
        w_ref[2, rows, :] = u0 * ahead[0] + u1 * ahead[2]
        w_ref[3, rows, :] = u0 * ahead[1] + u1 * ahead[3]
        if part < parts - 1:
            ahead = mat_mul(ahead, eight)

    for copy in copies[2:]:
        copy.wait()


def rotate_kernel(first, place_ref, *refs):
    pieces, others = first
    obs_refs, (basis_ref, *refs) = refs[: len(pieces)], refs[len(pieces) :]
    depth = obs_refs[0].shape[1]
    z = None if others is None else refs[0][...]
    for piece, obs_ref in zip(pieces, obs_refs):
        begin = pl.multiple_of((place_ref[0] ^ piece) * depth, depth)
        term = jnp.dot(
            obs_ref[...], basis_ref[pl.ds(begin, depth), :], preferred_element_type=F32
        )
        z = term if z is None else z + term
    if others is None:
        refs[0][...] = z
        return
    _, w_ref, z_ref, sum_ref = refs
    z_ref[...] = z
    for line in range(4):
        sum_ref[line : line + 1, :] = jnp.sum(w_ref[line] * z, axis=0, keepdims=True)


def merge(level, me, own, other, merge_ref):
    lower = jnp.full(own.shape, (me >> level) & 1, jnp.int32) == 0
    left, right = jnp.where(lower, own, other), jnp.where(lower, other, own)
    f00, f01, f10, f11, s00, s01, s11 = (
        merge_ref[7 * level + k : 7 * level + k + 1, :] for k in range(7)
    )
    b0, b1 = left[0:1, :], left[1:2, :]
    a0 = right[2:3, :] - s00 * b0 - s01 * b1
    a1 = right[3:4, :] - s01 * b0 - s11 * b1
    return jnp.concatenate(
        (
            right[0:1, :] + f00 * b0 + f01 * b1,
            right[1:2, :] + f10 * b0 + f11 * b1,
            left[2:3, :] + f00 * a0 + f10 * a1,
            left[3:4, :] + f01 * a0 + f11 * a1,
        ),
        axis=0,
    )


def merge_kernel(level, me_ref, merge_ref, *refs):
    *parts, out_ref = refs
    me = me_ref[0]
    parts = [ref[...] for ref in parts]
    if level:
        out_ref[...] = merge(level, me, parts[0], parts[1], merge_ref)
    else:
        near = merge(0, me, parts[0], parts[1], merge_ref)
        far = merge(0, me, parts[2], parts[3], merge_ref)
        out_ref[...] = merge(1, me, near, far, merge_ref)


def shift(value, by):
    rows = value.shape[0]
    row = lax.broadcasted_iota(jnp.int32, value.shape, 0)
    keep = row >= by if by > 0 else row < rows + by
    return jnp.where(keep, pltpu.roll(value, by % rows, 0), 0.0)


def reach(blocks, me, merge_ref, g_ref):
    tile = (SUB, merge_ref.shape[1])
    rounds = blocks.bit_length() - 1
    values = [
        jnp.broadcast_to(merge_ref[k : k + 1, :], tile) for k in range(7 * rounds + 6)
    ]
    block_squares = [tuple(values[7 * k : 7 * k + 4]) for k in range(rounds)]
    block_grams = [tuple(values[7 * k + 4 : 7 * k + 7]) for k in range(rounds)]
    s, excess = values[-6:-3], values[-3:]
    zero = jnp.zeros(tile, F32)
    row = lax.broadcasted_iota(jnp.int32, tile, 0)
    left = (
        1.0 + excess[0] * s[0] + excess[1] * s[1],
        excess[0] * s[1] + excess[1] * s[2],
        excess[1] * s[0] + excess[2] * s[1],
        1.0 + excess[1] * s[1] + excess[2] * s[2],
    )
    determ = 1.0 / (left[0] * left[3] - left[1] * left[2])
    start = mat_mul((left[3], -left[1], -left[2], left[0]), full(excess))
    start = tuple(x * determ for x in start)
    mine = jnp.full(tile, me, jnp.int32)
    to_me = power(block_squares, mine, zero)
    rest = full(gramian(block_squares, block_grams, blocks - 1 - mine, zero))
    to_state = mat_mul(to_me, start)
    to_adjoint = mat_mul(mat_mul(rest, mat_mul(to_me, block_squares[0])), start)
    for group in range(g_ref.shape[1] // SUB):
        rows = row + group * SUB
        kind = rows & 3
        line = rows >> 2
        span = jnp.where(line < 4, 1, jnp.left_shift(1, jnp.maximum(line - 2, 0)))
        near_me = mine ^ jnp.where(line < 4, line, span)
        front = jnp.minimum((near_me // span) * span, blocks - 1)
        back = jnp.minimum(front + span - 1, blocks - 1)
        before, after = back < me, front > me
        gap = jnp.where(before, me - 1 - back, jnp.where(after, front - 1 - me, 0))
        reach = jnp.where(before, me - back, jnp.where(after, back - me, 0))
        near = power(block_squares, gap, zero)
        far = power(block_squares, reach, zero)
        origin = mat_trans(power(block_squares, front, zero))
        left_over = full(gramian(block_squares, block_grams, blocks - 1 - back, zero))
        end = mat_trans(mat_mul(power(block_squares, back, zero), block_squares[0]))
        first = mat_mul(end, left_over)
        state_b = mat_sub(mat_pick(before, near, (zero,) * 4), mat_mul(to_state, first))
        state_l = mat_mul(to_state, origin)
        cross = mat_pick(after, mat_mul(mat_trans(far), left_over), mat_mul(rest, far))
        adjoint_b = mat_sub(mat_mul(to_adjoint, first), cross)
        adjoint_l = mat_sub(
            mat_pick(after, mat_trans(near), (zero,) * 4), mat_mul(to_adjoint, origin)
        )
        place = pl.ds(group * SUB, SUB)
        for output, (from_b, from_l) in enumerate(
            ((adjoint_b[:2], adjoint_l[:2]), (adjoint_b[2:], adjoint_l[2:]),
             (state_b[:2], state_l[:2]), (state_b[2:], state_l[2:]))
        ):
            g_ref[output, place, :] = jnp.where(
                kind < 2,
                jnp.where(kind == 0, from_b[0], from_b[1]),
                jnp.where(kind == 2, from_l[0], from_l[1]),
            )


def local_kernel(blocks, me_ref, z_ref, const_ref, merge_ref, r_ref, g_ref, scratch):
    reach(blocks, me_ref[0], merge_ref, g_ref)
    steps, width = z_ref.shape
    span = steps // SUB
    lanes = 128
    for chunk in range(width // lanes):
        cols = pl.ds(chunk * lanes, lanes)
        scratch[chunk] = z_ref[:, cols]
    for chunk in range(width // lanes):
        cols = pl.ds(chunk * lanes, lanes)
        const = [const_ref[k, :, cols] for k in range(19)]
        f, (k0, k1, inverse) = const[0:4], const[4:7]
        jumps = (const[7:11], const[11:15], const[15:19])
        zero = jnp.zeros((SUB, lanes), F32)
        x0, x1 = zero, zero
        vs = []
        for t in range(span):
            z = scratch[chunk, pl.ds(t, SUB, stride=span), :]
            vs.append(z - x0)
            x0, x1 = f[0] * x0 + f[1] * x1 + k0 * z, f[2] * x0 + f[3] * x1 + k1 * z
        for level, jump in enumerate(jumps):
            s0, s1 = shift(x0, 1 << level), shift(x1, 1 << level)
            x0, x1 = x0 + jump[0] * s0 + jump[1] * s1, x1 + jump[2] * s0 + jump[3] * s1
        x0, x1 = shift(x0, 1), shift(x1, 1)
        for t in range(span):
            vs[t] = (vs[t] - x0) * inverse
            x0, x1 = f[0] * x0 + f[1] * x1, f[2] * x0 + f[3] * x1
        a0, a1 = zero, zero
        for t in range(span - 1, -1, -1):
            a0, a1 = f[0] * a0 + f[2] * a1 + vs[t], f[1] * a0 + f[3] * a1
        for level, jump in enumerate(jumps):
            s0, s1 = shift(a0, -(1 << level)), shift(a1, -(1 << level))
            a0, a1 = a0 + jump[0] * s0 + jump[2] * s1, a1 + jump[1] * s0 + jump[3] * s1
        a0, a1 = shift(a0, -1), shift(a1, -1)
        for t in range(span - 1, -1, -1):
            r = vs[t] - k0 * a0 - k1 * a1
            a0, a1 = f[0] * a0 + f[2] * a1 + vs[t], f[1] * a0 + f[3] * a1
            scratch[chunk, pl.ds(t, SUB, stride=span), :] = r
        r_ref[:, cols] = scratch[chunk]


def rotate_back(residual, pieces, place_ref, basis_ref, outs):
    depth = outs[0].shape[1]
    for piece, out_ref in zip(pieces, outs):
        begin = pl.multiple_of((place_ref[0] ^ piece) * depth, depth)
        out_ref[...] = lax.dot_general(
            residual,
            basis_ref[pl.ds(begin, depth), :],
            (((1,), (1,)), ((), ())),
            preferred_element_type=F32,
        ).astype(out_ref.dtype)


def finish_kernel(pieces, place_ref, r_ref, w_ref, g_ref, const_ref, basis_ref, *refs):
    *sums, residual_ref = refs[: -len(pieces)]
    value = r_ref[...]
    for line in range(4):
        total = None
        for place, sum_ref in enumerate(sums):
            term = g_ref[line, pl.ds(4 * place, 4), :] * sum_ref[...]
            total = term if total is None else total + term
        value = value - w_ref[line] * jnp.sum(total, axis=0, keepdims=True)
    scale = const_ref[19, 0:1, :]
    residual = (value * scale).astype(jnp.bfloat16)
    residual_ref[...] = residual
    rotate_back(residual, pieces, place_ref, basis_ref, refs[-len(pieces) :])


def rest_kernel(pieces, place_ref, residual_ref, basis_ref, *outs):
    rotate_back(residual_ref[...], pieces, place_ref, basis_ref, outs)


def add_kernel(own_ref, *refs):
    *parts, out_ref, total_ref, sems = refs
    quarter = own_ref.shape[0] // 4
    copies = []
    for k in range(4):
        rows = pl.ds(k * quarter, quarter)
        total = own_ref[rows, :]
        for part in parts:
            total = total + part[rows, :].astype(F32)
        total_ref[rows, :] = total
        copy = pltpu.make_async_copy(total_ref.at[rows, :], out_ref.at[rows, :], sems.at[k])
        copy.start()
        copies.append(copy)
    for copy in copies:
        copy.wait()


def exchange(value, axis, count):
    out = [value]
    for step in range(1, count):
        out.append(lax.ppermute(value, axis, [(a, a ^ step) for a in range(count)]))
    return out


def shards(observations, basis, eigvals, lengths, noise):
    steps, depth = observations.shape
    width = basis.shape[1]
    blocks, pieces = lax.axis_size("tm"), lax.axis_size("mode")
    me = lax.axis_index("tm").astype(jnp.int32).reshape(1)
    place = lax.axis_index("mode").astype(jnp.int32).reshape(1)
    rounds = blocks.bit_length() - 1
    vmem = pl.BlockSpec(memory_space=pltpu.VMEM)
    smem = pl.BlockSpec(memory_space=pltpu.SMEM)
    params = pltpu.CompilerParams(vmem_limit_bytes=VMEM_LIMIT)

    def shape(*dims, dtype=F32):
        return jax.ShapeDtypeStruct(dims, dtype)

    obs = exchange(observations, "mode", pieces)
    const, w, merges, basis, obs[0] = pl.pallas_call(
        functools.partial(coefficients_kernel, blocks),
        out_shape=(
            shape(20, SUB, width),
            shape(4, steps, width),
            shape(-(-(7 * rounds + 6) // SUB) * SUB, width),
            shape(*basis.shape, dtype=basis.dtype),
            shape(steps, depth, dtype=observations.dtype),
        ),
        in_specs=[smem] + [pl.BlockSpec(memory_space=pltpu.HBM)] * 4,
        out_specs=(vmem,) * 5,
        scratch_shapes=[
            pltpu.VMEM((1, width), F32),
            pltpu.VMEM((1, width), F32),
            pltpu.SemaphoreType.DMA((4,)),
        ],
        compiler_params=params,
        cost_estimate=pl.CostEstimate(flops=20000000, bytes_accessed=2000000, transcendentals=0),
        name="coefficients",
    )(
        noise,
        *(
            pltpu.with_memory_space_constraint(x, pltpu.HBM)
            for x in (
                eigvals.reshape(1, width),
                lengths.reshape(1, width),
                observations,
                basis,
            )
        ),
    )
    last = pieces - 1
    early = list(range(last))
    z = pl.pallas_call(
        functools.partial(rotate_kernel, (early, None)),
        out_shape=shape(steps, width),
        in_specs=[smem] + [vmem] * pieces,
        out_specs=vmem,
        compiler_params=params,
        name="rotate_early",
    )(place, *(obs[piece] for piece in early), basis)
    z, summary = pl.pallas_call(
        functools.partial(rotate_kernel, ([last], early)),
        out_shape=(shape(steps, width), shape(4, width)),
        in_specs=[smem] + [vmem] * 4,
        out_specs=(vmem,) * 2,
        compiler_params=params,
        name="rotate_last",
    )(place, obs[last], basis, z, w)
    sums = [summary]
    for step in range(1, 4):
        sums.append(lax.ppermute(summary, "tm", [(a, a ^ step) for a in range(blocks)]))
    for level in range(2, rounds):
        summary = pl.pallas_call(
            functools.partial(merge_kernel, 0 if level == 2 else level - 1),
            out_shape=shape(4, width),
            in_specs=[smem] + [vmem] * (5 if level == 2 else 3),
            out_specs=vmem,
            compiler_params=params,
            name="merge",
        )(me, merges, *(sums if level == 2 else (summary, sums[-1])))
        step = 1 << level
        sums.append(lax.ppermute(summary, "tm", [(a, a ^ step) for a in range(blocks)]))
    local, g = pl.pallas_call(
        functools.partial(local_kernel, blocks),
        out_shape=(shape(steps, width), shape(4, -(-4 * (rounds + 2) // SUB) * SUB, width)),
        in_specs=[smem] + [vmem] * 3,
        out_specs=(vmem,) * 2,
        scratch_shapes=[pltpu.VMEM((width // 128, steps, 128), F32)],
        compiler_params=params,
        cost_estimate=pl.CostEstimate(flops=10000000, bytes_accessed=1000000, transcendentals=0),
        name="local",
    )(me, z, const, merges)
    far = list(range(2, pieces)) + [1]
    near = [0]
    residual, *parts = pl.pallas_call(
        functools.partial(finish_kernel, far),
        out_shape=(shape(steps, width, dtype=jnp.bfloat16),)
        + (shape(steps, depth, dtype=jnp.bfloat16),) * len(far),
        in_specs=[smem] + [vmem] * (5 + len(sums)),
        out_specs=(vmem,) * (1 + len(far)),
        compiler_params=params,
        name="finish",
    )(place, local, w, g, const, basis, *sums)
    arrived = [
        lax.ppermute(part, "mode", [(a, a ^ piece) for a in range(pieces)])
        for piece, part in zip(far, parts)
    ]
    grad_obs = pl.pallas_call(
        functools.partial(rest_kernel, near),
        out_shape=shape(steps, depth),
        in_specs=[smem] + [vmem] * 2,
        out_specs=vmem,
        compiler_params=params,
        cost_estimate=pl.CostEstimate(flops=80000000, bytes_accessed=1500000, transcendentals=0),
        name="rest",
    )(place, residual, basis)
    return pl.pallas_call(
        add_kernel,
        out_shape=shape(steps, depth),
        in_specs=[vmem] * pieces,
        out_specs=pl.BlockSpec(memory_space=pltpu.HBM),
        scratch_shapes=[pltpu.VMEM((steps, depth), F32), pltpu.SemaphoreType.DMA((4,))],
        compiler_params=params,
        name="add",
    )(grad_obs, *arrived)


def solution(mesh):
    placed = (P("tm", "mode"), P(None, "mode"), P("mode"), P("mode"), P())
    return jax.shard_map(
        shards, mesh=mesh, in_specs=placed, out_specs=P("tm", "mode"), check_vma=False
    )
```

```python
import functools
import math

import jax
import jax.numpy as jnp
from jax import lax
from jax.experimental import pallas as pl
from jax.experimental.pallas import tpu as pltpu
from jax.sharding import PartitionSpec as P

F32 = jnp.float32
SUB = 8
NEAR = (2, 1, 3)
VMEM_LIMIT = 24 * 1024 * 1024


def mat_mul(p, q):
    return (
        p[0] * q[0] + p[1] * q[2],
        p[0] * q[1] + p[1] * q[3],
        p[2] * q[0] + p[3] * q[2],
        p[2] * q[1] + p[3] * q[3],
    )


def mat_trans(p):
    return (p[0], p[2], p[1], p[3])


def mat_add(p, q):
    return tuple(a + b for a, b in zip(p, q))


def mat_sub(p, q):
    return tuple(a - b for a, b in zip(p, q))


def mat_pick(flag, p, q):
    return tuple(jnp.where(flag, a, b) for a, b in zip(p, q))


def full(s):
    return (s[0], s[1], s[1], s[2])


def congruence(s, f):
    t = (
        s[0] * f[0] + s[1] * f[2],
        s[0] * f[1] + s[1] * f[3],
        s[1] * f[0] + s[2] * f[2],
        s[1] * f[1] + s[2] * f[3],
    )
    return (f[0] * t[0] + f[2] * t[2], f[0] * t[1] + f[2] * t[3], f[1] * t[1] + f[3] * t[3])


def power(squares, exponent, like):
    one, zero = jnp.ones_like(like), jnp.zeros_like(like)
    out = None
    for bit, base in enumerate(squares):
        flag = (exponent & (1 << bit)) != 0
        if out is None:
            out = mat_pick(flag, base, (one, zero, zero, one))
        else:
            out = mat_pick(flag, mat_mul(out, base), out)
    return out


def gramian(squares, grams, count, like):
    zero = jnp.zeros_like(like)
    out = (zero, zero, zero)
    for bit, (base, gram) in enumerate(zip(squares, grams)):
        flag = (count & (1 << bit)) != 0
        out = mat_pick(flag, mat_add(gram, congruence(out, base)), out)
    return out


def steady_state(scale2, length, noise_var):
    lam = math.sqrt(3.0) / length
    decay = jnp.exp(-lam)
    twice = 2.0 * lam
    fall = jnp.exp(-twice)
    rho = scale2 / noise_var
    series = 1.0 / 604800.0
    for factor in (60480.0, 6720.0, 840.0, 120.0, 20.0, 4.0, 1.0):
        series = series * twice + 1.0 / factor
    lower = fall * twice * twice * twice * (1.0 / 6.0) * series
    loss = 1.0
    for order in (8, 7, 6, 5, 4, 3, 2):
        loss = 1.0 - lam * (1.0 / order) * loss
    loss = lam * loss
    q00 = rho * lower
    q01 = 2.0 * rho * lam * lam * fall
    q11 = rho * (lower + twice * fall)
    slope = decay * lam
    tilt = loss + slope
    g0 = q00 * tilt * tilt + 2.0 * slope * q01 * tilt + slope * slope * q11
    g1 = slope * q01 - decay * (1.0 - lam) * q00
    loss2 = loss * loss
    c2 = decay * decay
    u = (2.0 * decay * loss2 - g1) / c2
    v = (loss2 * loss2 + g0) / c2
    root = jnp.sqrt(v * (v + 4.0 * u + 16.0))
    product = 4.0 * v / (v + root + jnp.sqrt(2.0 * v * (v + 2.0 * u + root)))
    total = 0.5 * (jnp.sqrt(u * u + 4.0 * u - 2.0 * v + 2.0 * root) - u)
    gain0 = total - 2.0 * loss
    gain1 = (product - loss2 - gain0 * tilt) / slope
    inverse = (1.0 - total + product) / c2
    inn = c2 / (1.0 - total + product)
    closed = (1.0 + slope - loss - gain0, slope, -slope - gain1, decay * (1.0 - lam))
    p00 = inn * ((1.0 - lam) * gain0 - lam * gain1) / decay
    p01 = inn * (lam * gain0 + (1.0 + lam) * gain1) / decay
    p11 = (
        p01 * (loss * (1.0 + decay) + 2.0 * slope * slope)
        + slope * decay * (1.0 + lam) * p00
        - q01
        + gain0 * gain1 * inn
    ) / (slope * decay * (1.0 - lam))
    return closed, gain0, gain1, inverse, (rho - p00, -p01, rho - p11)


def coefficients_kernel(blocks, noise_ref, *refs):
    arguments, (const_ref, w_ref, merge_ref, basis_ref, obs_ref) = refs[:4], refs[4:9]
    scale_ref, length_ref, sems = refs[9:]
    targets = (scale_ref, length_ref, obs_ref, basis_ref)
    copies = [
        pltpu.make_async_copy(source, target, sems.at[k])
        for k, (source, target) in enumerate(zip(arguments, targets))
    ]
    for copy in copies:
        copy.start()
    for copy in copies[:2]:
        copy.wait()
    steps = w_ref.shape[1]
    width = scale_ref.shape[1]
    tile = (SUB, width)
    scale2 = jnp.broadcast_to(scale_ref[...], tile)
    length = jnp.broadcast_to(length_ref[...], tile)
    noise_var = jnp.full(tile, noise_ref[0], F32)
    closed, gain0, gain1, inverse, excess = steady_state(scale2, length, noise_var)
    zero = jnp.zeros(tile, F32)

    squares, grams = [closed], [(inverse, zero, zero)]
    doublings = (steps * blocks).bit_length() - 1
    for _ in range(doublings):
        base = squares[-1]
        grams.append(mat_add(grams[-1], congruence(grams[-1], base)))
        squares.append(mat_mul(base, base))
    local = steps.bit_length() - 1
    consts = closed + (gain0, gain1, inverse) + squares[3] + squares[4] + squares[5]
    for place, value in enumerate(consts):
        const_ref[place] = value
    const_ref[len(consts)] = -1.0 / noise_var
    rounds = blocks.bit_length() - 1
    groups = squares[local:-1] + [()], grams[local:], [()] * rounds + [excess]
    values = [value for group in zip(*groups) for part in group for value in part]
    for place, value in enumerate(values):
        merge_ref[place : place + 1, :] = value[0:1, :]

    row = lax.broadcasted_iota(jnp.int32, tile, 0)
    small, gram_small = squares[:3], grams[:3]
    behind = power(small, 7 - row, zero)
    gram = gramian(small, gram_small, 7 - row, zero)
    eight, gram_eight = squares[3], grams[3]
    parts = steps // SUB
    for part in range(parts - 1, -1, -1):
        rows = pl.ds(part * SUB, SUB)
        w_ref[0, rows, :] = behind[0] * gain0 + behind[1] * gain1
        w_ref[1, rows, :] = behind[2] * gain0 + behind[3] * gain1
        k0 = gain0 * gram[0] + gain1 * gram[1]
        k1 = gain0 * gram[1] + gain1 * gram[2]
        w_ref[2, rows, :] = inverse - (k0 * closed[0] + k1 * closed[2])
        w_ref[3, rows, :] = -(k0 * closed[1] + k1 * closed[3])
        if part:
            behind = mat_mul(behind, eight)
            gram = mat_add(gram_eight, congruence(gram, eight))
    ahead = power(small, row, zero)
    for part in range(parts):
        rows = pl.ds(part * SUB, SUB)
        u0, u1 = w_ref[2, rows, :], w_ref[3, rows, :]
        w_ref[2, rows, :] = u0 * ahead[0] + u1 * ahead[2]
        w_ref[3, rows, :] = u0 * ahead[1] + u1 * ahead[3]
        if part < parts - 1:
            ahead = mat_mul(ahead, eight)

    for copy in copies[2:]:
        copy.wait()


def rotate_kernel(first, place_ref, *refs):
    pieces, others = first
    obs_refs, (basis_ref, *refs) = refs[: len(pieces)], refs[len(pieces) :]
    depth = obs_refs[0].shape[1]
    z = None if others is None else refs[0][...]
    for piece, obs_ref in zip(pieces, obs_refs):
        begin = pl.multiple_of((place_ref[0] ^ piece) * depth, depth)
        term = jnp.dot(
            obs_ref[...], basis_ref[pl.ds(begin, depth), :], preferred_element_type=F32
        )
        z = term if z is None else z + term
    if others is None:
        refs[0][...] = z
        return
    _, w_ref, z_ref, sum_ref = refs
    z_ref[...] = z
    for line in range(4):
        sum_ref[line : line + 1, :] = jnp.sum(w_ref[line] * z, axis=0, keepdims=True)


def merge(level, me, own, other, merge_ref):
    lower = jnp.full(own.shape, (me >> level) & 1, jnp.int32) == 0
    left, right = jnp.where(lower, own, other), jnp.where(lower, other, own)
    f00, f01, f10, f11, s00, s01, s11 = (
        merge_ref[7 * level + k : 7 * level + k + 1, :] for k in range(7)
    )
    b0, b1 = left[0:1, :], left[1:2, :]
    a0 = right[2:3, :] - s00 * b0 - s01 * b1
    a1 = right[3:4, :] - s01 * b0 - s11 * b1
    return jnp.concatenate(
        (
            right[0:1, :] + f00 * b0 + f01 * b1,
            right[1:2, :] + f10 * b0 + f11 * b1,
            left[2:3, :] + f00 * a0 + f10 * a1,
            left[3:4, :] + f01 * a0 + f11 * a1,
        ),
        axis=0,
    )


def merge_kernel(level, me_ref, merge_ref, *refs):
    *parts, out_ref = refs
    me = me_ref[0]
    parts = [ref[...] for ref in parts]
    if level:
        out_ref[...] = merge(level, me, parts[0], parts[1], merge_ref)
    else:
        near = merge(0, me, parts[0], parts[1 + NEAR.index(1)], merge_ref)
        far = merge(0, me, parts[1 + NEAR.index(2)], parts[1 + NEAR.index(3)], merge_ref)
        out_ref[...] = merge(1, me, near, far, merge_ref)


def shift(value, by):
    rows = value.shape[0]
    row = lax.broadcasted_iota(jnp.int32, value.shape, 0)
    keep = row >= by if by > 0 else row < rows + by
    return jnp.where(keep, pltpu.roll(value, by % rows, 0), 0.0)


def reach(blocks, me, merge_ref, g_ref):
    tile = (SUB, merge_ref.shape[1])
    rounds = blocks.bit_length() - 1
    values = [
        jnp.broadcast_to(merge_ref[k : k + 1, :], tile) for k in range(7 * rounds + 6)
    ]
    block_squares = [tuple(values[7 * k : 7 * k + 4]) for k in range(rounds)]
    block_grams = [tuple(values[7 * k + 4 : 7 * k + 7]) for k in range(rounds)]
    s, excess = values[-6:-3], values[-3:]
    zero = jnp.zeros(tile, F32)
    row = lax.broadcasted_iota(jnp.int32, tile, 0)
    left = (
        1.0 + excess[0] * s[0] + excess[1] * s[1],
        excess[0] * s[1] + excess[1] * s[2],
        excess[1] * s[0] + excess[2] * s[1],
        1.0 + excess[1] * s[1] + excess[2] * s[2],
    )
    determ = 1.0 / (left[0] * left[3] - left[1] * left[2])
    start = mat_mul((left[3], -left[1], -left[2], left[0]), full(excess))
    start = tuple(x * determ for x in start)
    mine = jnp.full(tile, me, jnp.int32)
    to_me = power(block_squares, mine, zero)
    rest = full(gramian(block_squares, block_grams, blocks - 1 - mine, zero))
    to_state = mat_mul(to_me, start)
    to_adjoint = mat_mul(mat_mul(rest, mat_mul(to_me, block_squares[0])), start)
    for group in range(g_ref.shape[1] // SUB):
        rows = row + group * SUB
        kind = rows & 3
        line = rows >> 2
        step = jnp.where(line == 1, NEAR[0], jnp.where(line == 2, NEAR[1], jnp.where(line == 3, NEAR[2], 0)))
        span = jnp.where(line < 4, 1, jnp.left_shift(1, jnp.maximum(line - 2, 0)))
        near_me = mine ^ jnp.where(line < 4, step, span)
        front = jnp.minimum((near_me // span) * span, blocks - 1)
        back = jnp.minimum(front + span - 1, blocks - 1)
        before, after = back < me, front > me
        gap = jnp.where(before, me - 1 - back, jnp.where(after, front - 1 - me, 0))
        reach = jnp.where(before, me - back, jnp.where(after, back - me, 0))
        near = power(block_squares, gap, zero)
        far = power(block_squares, reach, zero)
        origin = mat_trans(power(block_squares, front, zero))
        left_over = full(gramian(block_squares, block_grams, blocks - 1 - back, zero))
        end = mat_trans(mat_mul(power(block_squares, back, zero), block_squares[0]))
        first = mat_mul(end, left_over)
        state_b = mat_sub(mat_pick(before, near, (zero,) * 4), mat_mul(to_state, first))
        state_l = mat_mul(to_state, origin)
        cross = mat_pick(after, mat_mul(mat_trans(far), left_over), mat_mul(rest, far))
        adjoint_b = mat_sub(mat_mul(to_adjoint, first), cross)
        adjoint_l = mat_sub(
            mat_pick(after, mat_trans(near), (zero,) * 4), mat_mul(to_adjoint, origin)
        )
        place = pl.ds(group * SUB, SUB)
        for output, (from_b, from_l) in enumerate(
            ((adjoint_b[:2], adjoint_l[:2]), (adjoint_b[2:], adjoint_l[2:]),
             (state_b[:2], state_l[:2]), (state_b[2:], state_l[2:]))
        ):
            g_ref[output, place, :] = jnp.where(
                kind < 2,
                jnp.where(kind == 0, from_b[0], from_b[1]),
                jnp.where(kind == 2, from_l[0], from_l[1]),
            )


def local_kernel(blocks, me_ref, z_ref, const_ref, merge_ref, r_ref, g_ref, scratch):
    reach(blocks, me_ref[0], merge_ref, g_ref)
    steps, width = z_ref.shape
    span = steps // SUB
    lanes = 128
    for chunk in range(width // lanes):
        cols = pl.ds(chunk * lanes, lanes)
        scratch[chunk] = z_ref[:, cols]
    for chunk in range(width // lanes):
        cols = pl.ds(chunk * lanes, lanes)
        const = [const_ref[k, :, cols] for k in range(19)]
        f, (k0, k1, inverse) = const[0:4], const[4:7]
        jumps = (const[7:11], const[11:15], const[15:19])
        zero = jnp.zeros((SUB, lanes), F32)
        x0, x1 = zero, zero
        vs = []
        for t in range(span):
            z = scratch[chunk, pl.ds(t, SUB, stride=span), :]
            vs.append(z - x0)
            x0, x1 = f[0] * x0 + f[1] * x1 + k0 * z, f[2] * x0 + f[3] * x1 + k1 * z
        for level, jump in enumerate(jumps):
            s0, s1 = shift(x0, 1 << level), shift(x1, 1 << level)
            x0, x1 = x0 + jump[0] * s0 + jump[1] * s1, x1 + jump[2] * s0 + jump[3] * s1
        x0, x1 = shift(x0, 1), shift(x1, 1)
        for t in range(span):
            vs[t] = (vs[t] - x0) * inverse
            x0, x1 = f[0] * x0 + f[1] * x1, f[2] * x0 + f[3] * x1
        a0, a1 = zero, zero
        for t in range(span - 1, -1, -1):
            a0, a1 = f[0] * a0 + f[2] * a1 + vs[t], f[1] * a0 + f[3] * a1
        for level, jump in enumerate(jumps):
            s0, s1 = shift(a0, -(1 << level)), shift(a1, -(1 << level))
            a0, a1 = a0 + jump[0] * s0 + jump[2] * s1, a1 + jump[1] * s0 + jump[3] * s1
        a0, a1 = shift(a0, -1), shift(a1, -1)
        for t in range(span - 1, -1, -1):
            r = vs[t] - k0 * a0 - k1 * a1
            a0, a1 = f[0] * a0 + f[2] * a1 + vs[t], f[1] * a0 + f[3] * a1
            scratch[chunk, pl.ds(t, SUB, stride=span), :] = r
        r_ref[:, cols] = scratch[chunk]


def rotate_back(residual, pieces, place_ref, basis_ref, outs):
    depth = outs[0].shape[1]
    for piece, out_ref in zip(pieces, outs):
        begin = pl.multiple_of((place_ref[0] ^ piece) * depth, depth)
        out_ref[...] = lax.dot_general(
            residual,
            basis_ref[pl.ds(begin, depth), :],
            (((1,), (1,)), ((), ())),
            preferred_element_type=F32,
        ).astype(out_ref.dtype)


def finish_kernel(pieces, place_ref, r_ref, w_ref, g_ref, const_ref, basis_ref, *refs):
    *sums, residual_ref = refs[: -len(pieces)]
    value = r_ref[...]
    for line in range(4):
        total = None
        for place, sum_ref in enumerate(sums):
            term = g_ref[line, pl.ds(4 * place, 4), :] * sum_ref[...]
            total = term if total is None else total + term
        value = value - w_ref[line] * jnp.sum(total, axis=0, keepdims=True)
    scale = const_ref[19, 0:1, :]
    residual = (value * scale).astype(jnp.bfloat16)
    residual_ref[...] = residual
    rotate_back(residual, pieces, place_ref, basis_ref, refs[-len(pieces) :])


def rest_kernel(pieces, place_ref, residual_ref, basis_ref, *outs):
    rotate_back(residual_ref[...], pieces, place_ref, basis_ref, outs)


def exchange(value, axis, count):
    out = [value]
    for step in range(1, count):
        out.append(lax.ppermute(value, axis, [(a, a ^ step) for a in range(count)]))
    return out


def shards(observations, basis, eigvals, lengths, noise):
    steps, depth = observations.shape
    width = basis.shape[1]
    blocks, pieces = lax.axis_size("tm"), lax.axis_size("mode")
    me = lax.axis_index("tm").astype(jnp.int32).reshape(1)
    place = lax.axis_index("mode").astype(jnp.int32).reshape(1)
    rounds = blocks.bit_length() - 1
    vmem = pl.BlockSpec(memory_space=pltpu.VMEM)
    smem = pl.BlockSpec(memory_space=pltpu.SMEM)
    params = pltpu.CompilerParams(vmem_limit_bytes=VMEM_LIMIT)

    def shape(*dims, dtype=F32):
        return jax.ShapeDtypeStruct(dims, dtype)

    obs = exchange(observations, "mode", pieces)
    const, w, merges, basis, obs[0] = pl.pallas_call(
        functools.partial(coefficients_kernel, blocks),
        out_shape=(
            shape(20, SUB, width),
            shape(4, steps, width),
            shape(-(-(7 * rounds + 6) // SUB) * SUB, width),
            shape(*basis.shape, dtype=basis.dtype),
            shape(steps, depth, dtype=observations.dtype),
        ),
        in_specs=[smem] + [pl.BlockSpec(memory_space=pltpu.HBM)] * 4,
        out_specs=(vmem,) * 5,
        scratch_shapes=[
            pltpu.VMEM((1, width), F32),
            pltpu.VMEM((1, width), F32),
            pltpu.SemaphoreType.DMA((4,)),
        ],
        compiler_params=params,
        cost_estimate=pl.CostEstimate(flops=20000000, bytes_accessed=2000000, transcendentals=0),
        name="coefficients",
    )(
        noise,
        *(
            pltpu.with_memory_space_constraint(x, pltpu.HBM)
            for x in (
                eigvals.reshape(1, width),
                lengths.reshape(1, width),
                observations,
                basis,
            )
        ),
    )
    last = pieces - 1
    early = list(range(last))
    z = pl.pallas_call(
        functools.partial(rotate_kernel, (early, None)),
        out_shape=shape(steps, width),
        in_specs=[smem] + [vmem] * pieces,
        out_specs=vmem,
        compiler_params=params,
        name="rotate_early",
    )(place, *(obs[piece] for piece in early), basis)
    z, summary = pl.pallas_call(
        functools.partial(rotate_kernel, ([last], early)),
        out_shape=(shape(steps, width), shape(4, width)),
        in_specs=[smem] + [vmem] * 4,
        out_specs=(vmem,) * 2,
        compiler_params=params,
        name="rotate_last",
    )(place, obs[last], basis, z, w)
    sums = [summary]
    for step in NEAR:
        sums.append(lax.ppermute(summary, "tm", [(a, a ^ step) for a in range(blocks)]))
    for level in range(2, rounds):
        summary = pl.pallas_call(
            functools.partial(merge_kernel, 0 if level == 2 else level - 1),
            out_shape=shape(4, width),
            in_specs=[smem] + [vmem] * (5 if level == 2 else 3),
            out_specs=vmem,
            compiler_params=params,
            name="merge",
        )(me, merges, *(sums if level == 2 else (summary, sums[-1])))
        step = 1 << level
        sums.append(lax.ppermute(summary, "tm", [(a, a ^ step) for a in range(blocks)]))
    local, g = pl.pallas_call(
        functools.partial(local_kernel, blocks),
        out_shape=(shape(steps, width), shape(4, -(-4 * (rounds + 2) // SUB) * SUB, width)),
        in_specs=[smem] + [vmem] * 3,
        out_specs=(vmem,) * 2,
        scratch_shapes=[pltpu.VMEM((width // 128, steps, 128), F32)],
        compiler_params=params,
        cost_estimate=pl.CostEstimate(flops=10000000, bytes_accessed=1000000, transcendentals=0),
        name="local",
    )(me, z, const, merges)
    far = list(range(2, pieces)) + [1]
    near = [0]
    residual, *parts = pl.pallas_call(
        functools.partial(finish_kernel, far),
        out_shape=(shape(steps, width, dtype=jnp.bfloat16),)
        + (shape(steps, depth, dtype=jnp.bfloat16),) * len(far),
        in_specs=[smem] + [vmem] * (5 + len(sums)),
        out_specs=(vmem,) * (1 + len(far)),
        compiler_params=params,
        name="finish",
    )(place, local, w, g, const, basis, *sums)
    arrived = [
        lax.ppermute(part, "mode", [(a, a ^ piece) for a in range(pieces)])
        for piece, part in zip(far, parts)
    ]
    grad_obs = pl.pallas_call(
        functools.partial(rest_kernel, near),
        out_shape=shape(steps, depth),
        in_specs=[smem] + [vmem] * 2,
        out_specs=vmem,
        compiler_params=params,
        cost_estimate=pl.CostEstimate(flops=80000000, bytes_accessed=1500000, transcendentals=0),
        name="rest",
    )(place, residual, basis)
    for part in arrived:
        grad_obs = grad_obs + part.astype(F32)
    return grad_obs


def solution(mesh):
    placed = (P("tm", "mode"), P(None, "mode"), P("mode"), P("mode"), P())
    return jax.shard_map(
        shards, mesh=mesh, in_specs=placed, out_specs=P("tm", "mode"), check_vma=False
    )
```

```python
import functools
import math

import jax
import jax.numpy as jnp
from jax import lax
from jax.experimental import pallas as pl
from jax.experimental.pallas import tpu as pltpu
from jax.sharding import PartitionSpec as P

F32 = jnp.float32
SUB = 8
MIRROR, NEAR = 6, (2, 1, 3)
GROUP = (0, MIRROR) + tuple(step ^ other for step in NEAR for other in (0, MIRROR))
VMEM_LIMIT = 24 * 1024 * 1024


def mat_mul(p, q):
    return (
        p[0] * q[0] + p[1] * q[2],
        p[0] * q[1] + p[1] * q[3],
        p[2] * q[0] + p[3] * q[2],
        p[2] * q[1] + p[3] * q[3],
    )


def mat_trans(p):
    return (p[0], p[2], p[1], p[3])


def mat_add(p, q):
    return tuple(a + b for a, b in zip(p, q))


def mat_sub(p, q):
    return tuple(a - b for a, b in zip(p, q))


def mat_pick(flag, p, q):
    return tuple(jnp.where(flag, a, b) for a, b in zip(p, q))


def full(s):
    return (s[0], s[1], s[1], s[2])


def congruence(s, f):
    t = (
        s[0] * f[0] + s[1] * f[2],
        s[0] * f[1] + s[1] * f[3],
        s[1] * f[0] + s[2] * f[2],
        s[1] * f[1] + s[2] * f[3],
    )
    return (f[0] * t[0] + f[2] * t[2], f[0] * t[1] + f[2] * t[3], f[1] * t[1] + f[3] * t[3])


def power(squares, exponent, like):
    one, zero = jnp.ones_like(like), jnp.zeros_like(like)
    out = None
    for bit, base in enumerate(squares):
        flag = (exponent & (1 << bit)) != 0
        if out is None:
            out = mat_pick(flag, base, (one, zero, zero, one))
        else:
            out = mat_pick(flag, mat_mul(out, base), out)
    return out


def gramian(squares, grams, count, like):
    zero = jnp.zeros_like(like)
    out = (zero, zero, zero)
    for bit, (base, gram) in enumerate(zip(squares, grams)):
        flag = (count & (1 << bit)) != 0
        out = mat_pick(flag, mat_add(gram, congruence(out, base)), out)
    return out


def steady_state(scale2, length, noise_var):
    lam = math.sqrt(3.0) / length
    decay = jnp.exp(-lam)
    twice = 2.0 * lam
    fall = jnp.exp(-twice)
    rho = scale2 / noise_var
    series = 1.0 / 604800.0
    for factor in (60480.0, 6720.0, 840.0, 120.0, 20.0, 4.0, 1.0):
        series = series * twice + 1.0 / factor
    lower = fall * twice * twice * twice * (1.0 / 6.0) * series
    loss = 1.0
    for order in (8, 7, 6, 5, 4, 3, 2):
        loss = 1.0 - lam * (1.0 / order) * loss
    loss = lam * loss
    q00 = rho * lower
    q01 = 2.0 * rho * lam * lam * fall
    q11 = rho * (lower + twice * fall)
    slope = decay * lam
    tilt = loss + slope
    g0 = q00 * tilt * tilt + 2.0 * slope * q01 * tilt + slope * slope * q11
    g1 = slope * q01 - decay * (1.0 - lam) * q00
    loss2 = loss * loss
    c2 = decay * decay
    u = (2.0 * decay * loss2 - g1) / c2
    v = (loss2 * loss2 + g0) / c2
    root = jnp.sqrt(v * (v + 4.0 * u + 16.0))
    product = 4.0 * v / (v + root + jnp.sqrt(2.0 * v * (v + 2.0 * u + root)))
    total = 0.5 * (jnp.sqrt(u * u + 4.0 * u - 2.0 * v + 2.0 * root) - u)
    gain0 = total - 2.0 * loss
    gain1 = (product - loss2 - gain0 * tilt) / slope
    inverse = (1.0 - total + product) / c2
    inn = c2 / (1.0 - total + product)
    closed = (1.0 + slope - loss - gain0, slope, -slope - gain1, decay * (1.0 - lam))
    p00 = inn * ((1.0 - lam) * gain0 - lam * gain1) / decay
    p01 = inn * (lam * gain0 + (1.0 + lam) * gain1) / decay
    p11 = (
        p01 * (loss * (1.0 + decay) + 2.0 * slope * slope)
        + slope * decay * (1.0 + lam) * p00
        - q01
        + gain0 * gain1 * inn
    ) / (slope * decay * (1.0 - lam))
    return closed, gain0, gain1, inverse, (rho - p00, -p01, rho - p11)


def coefficients_kernel(blocks, noise_ref, *refs):
    arguments, (const_ref, w_ref, merge_ref, basis_ref, obs_ref) = refs[:4], refs[4:9]
    scale_ref, length_ref, sems = refs[9:]
    targets = (scale_ref, length_ref, obs_ref, basis_ref)
    copies = [
        pltpu.make_async_copy(source, target, sems.at[k])
        for k, (source, target) in enumerate(zip(arguments, targets))
    ]
    for copy in copies:
        copy.start()
    for copy in copies[:2]:
        copy.wait()
    steps = w_ref.shape[1]
    width = scale_ref.shape[1]
    tile = (SUB, width)
    scale2 = jnp.broadcast_to(scale_ref[...], tile)
    length = jnp.broadcast_to(length_ref[...], tile)
    noise_var = jnp.full(tile, noise_ref[0], F32)
    closed, gain0, gain1, inverse, excess = steady_state(scale2, length, noise_var)
    zero = jnp.zeros(tile, F32)

    squares, grams = [closed], [(inverse, zero, zero)]
    doublings = (steps * blocks).bit_length() - 1
    for _ in range(doublings):
        base = squares[-1]
        grams.append(mat_add(grams[-1], congruence(grams[-1], base)))
        squares.append(mat_mul(base, base))
    local = steps.bit_length() - 1
    consts = closed + (gain0, gain1, inverse) + squares[3] + squares[4] + squares[5]
    for place, value in enumerate(consts):
        const_ref[place] = value
    const_ref[len(consts)] = -1.0 / noise_var
    rounds = blocks.bit_length() - 1
    groups = squares[local:-1] + [()], grams[local:], [()] * rounds + [excess]
    values = [value for group in zip(*groups) for part in group for value in part]
    for place, value in enumerate(values):
        merge_ref[place : place + 1, :] = value[0:1, :]

    row = lax.broadcasted_iota(jnp.int32, tile, 0)
    small, gram_small = squares[:3], grams[:3]
    behind = power(small, 7 - row, zero)
    gram = gramian(small, gram_small, 7 - row, zero)
    eight, gram_eight = squares[3], grams[3]
    parts = steps // SUB
    for part in range(parts - 1, -1, -1):
        rows = pl.ds(part * SUB, SUB)
        w_ref[0, rows, :] = behind[0] * gain0 + behind[1] * gain1
        w_ref[1, rows, :] = behind[2] * gain0 + behind[3] * gain1
        k0 = gain0 * gram[0] + gain1 * gram[1]
        k1 = gain0 * gram[1] + gain1 * gram[2]
        w_ref[2, rows, :] = inverse - (k0 * closed[0] + k1 * closed[2])
        w_ref[3, rows, :] = -(k0 * closed[1] + k1 * closed[3])
        if part:
            behind = mat_mul(behind, eight)
            gram = mat_add(gram_eight, congruence(gram, eight))
    ahead = power(small, row, zero)
    for part in range(parts):
        rows = pl.ds(part * SUB, SUB)
        u0, u1 = w_ref[2, rows, :], w_ref[3, rows, :]
        w_ref[2, rows, :] = u0 * ahead[0] + u1 * ahead[2]
        w_ref[3, rows, :] = u0 * ahead[1] + u1 * ahead[3]
        if part < parts - 1:
            ahead = mat_mul(ahead, eight)

    for copy in copies[2:]:
        copy.wait()


def rotate_kernel(first, place_ref, *refs):
    pieces, others = first
    obs_refs, (basis_ref, *refs) = refs[: len(pieces)], refs[len(pieces) :]
    depth = obs_refs[0].shape[1]
    z = None if others is None else refs[0][...]
    for piece, obs_ref in zip(pieces, obs_refs):
        begin = pl.multiple_of((place_ref[0] ^ piece) * depth, depth)
        term = jnp.dot(
            obs_ref[...], basis_ref[pl.ds(begin, depth), :], preferred_element_type=F32
        )
        z = term if z is None else z + term
    if others is None:
        refs[0][...] = z
        return
    _, w_ref, z_ref, sum_ref = refs
    z_ref[...] = z
    for line in range(4):
        sum_ref[line : line + 1, :] = jnp.sum(w_ref[line] * z, axis=0, keepdims=True)


def merge(level, me, own, other, merge_ref):
    lower = jnp.full(own.shape, (me >> level) & 1, jnp.int32) == 0
    left, right = jnp.where(lower, own, other), jnp.where(lower, other, own)
    f00, f01, f10, f11, s00, s01, s11 = (
        merge_ref[7 * level + k : 7 * level + k + 1, :] for k in range(7)
    )
    b0, b1 = left[0:1, :], left[1:2, :]
    a0 = right[2:3, :] - s00 * b0 - s01 * b1
    a1 = right[3:4, :] - s01 * b0 - s11 * b1
    return jnp.concatenate(
        (
            right[0:1, :] + f00 * b0 + f01 * b1,
            right[1:2, :] + f10 * b0 + f11 * b1,
            left[2:3, :] + f00 * a0 + f10 * a1,
            left[3:4, :] + f01 * a0 + f11 * a1,
        ),
        axis=0,
    )


def pair_kernel(own_ref, other_ref, out_ref):
    out_ref[0:4, :] = own_ref[...]
    out_ref[4:8, :] = other_ref[...]


def merge_kernel(level, me_ref, merge_ref, *refs):
    *refs, out_ref = refs
    me = me_ref[0]
    if level > 2:
        out_ref[...] = merge(level, me, refs[0][...], refs[1][...], merge_ref)
        return
    parts = {}
    for place, step in enumerate(GROUP):
        parts[step] = refs[place // 2][4 * (place % 2) : 4 * (place % 2) + 4, :]
    for level, stride in enumerate((1, 2, 4)):
        parts = {
            step: merge(level, me ^ step, parts[step], parts[step ^ stride], merge_ref)
            for step in range(0, 8, 2 * stride)
        }
    out_ref[...] = parts[0]


def shift(value, by):
    rows = value.shape[0]
    row = lax.broadcasted_iota(jnp.int32, value.shape, 0)
    keep = row >= by if by > 0 else row < rows + by
    return jnp.where(keep, pltpu.roll(value, by % rows, 0), 0.0)


def reach(blocks, me, merge_ref, g_ref):
    tile = (SUB, merge_ref.shape[1])
    rounds = blocks.bit_length() - 1
    values = [
        jnp.broadcast_to(merge_ref[k : k + 1, :], tile) for k in range(7 * rounds + 6)
    ]
    block_squares = [tuple(values[7 * k : 7 * k + 4]) for k in range(rounds)]
    block_grams = [tuple(values[7 * k + 4 : 7 * k + 7]) for k in range(rounds)]
    s, excess = values[-6:-3], values[-3:]
    zero = jnp.zeros(tile, F32)
    row = lax.broadcasted_iota(jnp.int32, tile, 0)
    left = (
        1.0 + excess[0] * s[0] + excess[1] * s[1],
        excess[0] * s[1] + excess[1] * s[2],
        excess[1] * s[0] + excess[2] * s[1],
        1.0 + excess[1] * s[1] + excess[2] * s[2],
    )
    determ = 1.0 / (left[0] * left[3] - left[1] * left[2])
    start = mat_mul((left[3], -left[1], -left[2], left[0]), full(excess))
    start = tuple(x * determ for x in start)
    mine = jnp.full(tile, me, jnp.int32)
    to_me = power(block_squares, mine, zero)
    rest = full(gramian(block_squares, block_grams, blocks - 1 - mine, zero))
    to_state = mat_mul(to_me, start)
    to_adjoint = mat_mul(mat_mul(rest, mat_mul(to_me, block_squares[0])), start)
    for group in range(g_ref.shape[1] // SUB):
        rows = row + group * SUB
        kind = rows & 3
        line = rows >> 2
        step = jnp.zeros_like(line)
        for place, offset in enumerate(GROUP):
            step = jnp.where(line == place, offset, step)
        span = jnp.where(line < 8, 1, jnp.left_shift(1, jnp.maximum(line - 5, 0)))
        near_me = mine ^ jnp.where(line < 8, step, span)
        front = jnp.minimum((near_me // span) * span, blocks - 1)
        back = jnp.minimum(front + span - 1, blocks - 1)
        before, after = back < me, front > me
        gap = jnp.where(before, me - 1 - back, jnp.where(after, front - 1 - me, 0))
        reach = jnp.where(before, me - back, jnp.where(after, back - me, 0))
        near = power(block_squares, gap, zero)
        far = power(block_squares, reach, zero)
        origin = mat_trans(power(block_squares, front, zero))
        left_over = full(gramian(block_squares, block_grams, blocks - 1 - back, zero))
        end = mat_trans(mat_mul(power(block_squares, back, zero), block_squares[0]))
        first = mat_mul(end, left_over)
        state_b = mat_sub(mat_pick(before, near, (zero,) * 4), mat_mul(to_state, first))
        state_l = mat_mul(to_state, origin)
        cross = mat_pick(after, mat_mul(mat_trans(far), left_over), mat_mul(rest, far))
        adjoint_b = mat_sub(mat_mul(to_adjoint, first), cross)
        adjoint_l = mat_sub(
            mat_pick(after, mat_trans(near), (zero,) * 4), mat_mul(to_adjoint, origin)
        )
        place = pl.ds(group * SUB, SUB)
        for output, (from_b, from_l) in enumerate(
            ((adjoint_b[:2], adjoint_l[:2]), (adjoint_b[2:], adjoint_l[2:]),
             (state_b[:2], state_l[:2]), (state_b[2:], state_l[2:]))
        ):
            g_ref[output, place, :] = jnp.where(
                kind < 2,
                jnp.where(kind == 0, from_b[0], from_b[1]),
                jnp.where(kind == 2, from_l[0], from_l[1]),
            )


def local_kernel(blocks, me_ref, z_ref, const_ref, merge_ref, r_ref, g_ref, scratch):
    reach(blocks, me_ref[0], merge_ref, g_ref)
    steps, width = z_ref.shape
    span = steps // SUB
    lanes = 128
    for chunk in range(width // lanes):
        cols = pl.ds(chunk * lanes, lanes)
        scratch[chunk] = z_ref[:, cols]
    for chunk in range(width // lanes):
        cols = pl.ds(chunk * lanes, lanes)
        const = [const_ref[k, :, cols] for k in range(19)]
        f, (k0, k1, inverse) = const[0:4], const[4:7]
        jumps = (const[7:11], const[11:15], const[15:19])
        zero = jnp.zeros((SUB, lanes), F32)
        x0, x1 = zero, zero
        vs = []
        for t in range(span):
            z = scratch[chunk, pl.ds(t, SUB, stride=span), :]
            vs.append(z - x0)
            x0, x1 = f[0] * x0 + f[1] * x1 + k0 * z, f[2] * x0 + f[3] * x1 + k1 * z
        for level, jump in enumerate(jumps):
            s0, s1 = shift(x0, 1 << level), shift(x1, 1 << level)
            x0, x1 = x0 + jump[0] * s0 + jump[1] * s1, x1 + jump[2] * s0 + jump[3] * s1
        x0, x1 = shift(x0, 1), shift(x1, 1)
        for t in range(span):
            vs[t] = (vs[t] - x0) * inverse
            x0, x1 = f[0] * x0 + f[1] * x1, f[2] * x0 + f[3] * x1
        a0, a1 = zero, zero
        for t in range(span - 1, -1, -1):
            a0, a1 = f[0] * a0 + f[2] * a1 + vs[t], f[1] * a0 + f[3] * a1
        for level, jump in enumerate(jumps):
            s0, s1 = shift(a0, -(1 << level)), shift(a1, -(1 << level))
            a0, a1 = a0 + jump[0] * s0 + jump[2] * s1, a1 + jump[1] * s0 + jump[3] * s1
        a0, a1 = shift(a0, -1), shift(a1, -1)
        for t in range(span - 1, -1, -1):
            r = vs[t] - k0 * a0 - k1 * a1
            a0, a1 = f[0] * a0 + f[2] * a1 + vs[t], f[1] * a0 + f[3] * a1
            scratch[chunk, pl.ds(t, SUB, stride=span), :] = r
        r_ref[:, cols] = scratch[chunk]


def rotate_back(residual, pieces, place_ref, basis_ref, outs):
    depth = outs[0].shape[1]
    for piece, out_ref in zip(pieces, outs):
        begin = pl.multiple_of((place_ref[0] ^ piece) * depth, depth)
        out_ref[...] = lax.dot_general(
            residual,
            basis_ref[pl.ds(begin, depth), :],
            (((1,), (1,)), ((), ())),
            preferred_element_type=F32,
        ).astype(out_ref.dtype)


def finish_kernel(pieces, place_ref, r_ref, w_ref, g_ref, const_ref, basis_ref, *refs):
    *sums, residual_ref = refs[: -len(pieces)]
    value = r_ref[...]
    for line in range(4):
        total, place = 0.0, 0
        for sum_ref in sums:
            count = sum_ref.shape[0]
            term = g_ref[line, pl.ds(place, count), :] * sum_ref[...]
            total = total + jnp.sum(term, axis=0, keepdims=True) if count < SUB else total + term
            place += count
            if place == 4 * len(GROUP):
                total = jnp.sum(total, axis=0, keepdims=True)
        value = value - w_ref[line] * total
    scale = const_ref[19, 0:1, :]
    residual = (value * scale).astype(jnp.bfloat16)
    residual_ref[...] = residual
    rotate_back(residual, pieces, place_ref, basis_ref, refs[-len(pieces) :])


def rest_kernel(pieces, place_ref, residual_ref, basis_ref, *outs):
    rotate_back(residual_ref[...], pieces, place_ref, basis_ref, outs)


def exchange(value, axis, count):
    out = [value]
    for step in range(1, count):
        out.append(lax.ppermute(value, axis, [(a, a ^ step) for a in range(count)]))
    return out


def shards(observations, basis, eigvals, lengths, noise):
    steps, depth = observations.shape
    width = basis.shape[1]
    blocks, pieces = lax.axis_size("tm"), lax.axis_size("mode")
    me = lax.axis_index("tm").astype(jnp.int32).reshape(1)
    place = lax.axis_index("mode").astype(jnp.int32).reshape(1)
    rounds = blocks.bit_length() - 1
    vmem = pl.BlockSpec(memory_space=pltpu.VMEM)
    smem = pl.BlockSpec(memory_space=pltpu.SMEM)
    params = pltpu.CompilerParams(vmem_limit_bytes=VMEM_LIMIT)

    def shape(*dims, dtype=F32):
        return jax.ShapeDtypeStruct(dims, dtype)

    obs = exchange(observations, "mode", pieces)
    const, w, merges, basis, obs[0] = pl.pallas_call(
        functools.partial(coefficients_kernel, blocks),
        out_shape=(
            shape(20, SUB, width),
            shape(4, steps, width),
            shape(-(-(7 * rounds + 6) // SUB) * SUB, width),
            shape(*basis.shape, dtype=basis.dtype),
            shape(steps, depth, dtype=observations.dtype),
        ),
        in_specs=[smem] + [pl.BlockSpec(memory_space=pltpu.HBM)] * 4,
        out_specs=(vmem,) * 5,
        scratch_shapes=[
            pltpu.VMEM((1, width), F32),
            pltpu.VMEM((1, width), F32),
            pltpu.SemaphoreType.DMA((4,)),
        ],
        compiler_params=params,
        cost_estimate=pl.CostEstimate(flops=20000000, bytes_accessed=2000000, transcendentals=0),
        name="coefficients",
    )(
        noise,
        *(
            pltpu.with_memory_space_constraint(x, pltpu.HBM)
            for x in (
                eigvals.reshape(1, width),
                lengths.reshape(1, width),
                observations,
                basis,
            )
        ),
    )
    last = pieces - 1
    early = list(range(last))
    z = pl.pallas_call(
        functools.partial(rotate_kernel, (early, None)),
        out_shape=shape(steps, width),
        in_specs=[smem] + [vmem] * pieces,
        out_specs=vmem,
        compiler_params=params,
        name="rotate_early",
    )(place, *(obs[piece] for piece in early), basis)
    z, summary = pl.pallas_call(
        functools.partial(rotate_kernel, ([last], early)),
        out_shape=(shape(steps, width), shape(4, width)),
        in_specs=[smem] + [vmem] * 4,
        out_specs=(vmem,) * 2,
        compiler_params=params,
        name="rotate_last",
    )(place, obs[last], basis, z, w)
    pair = pl.pallas_call(
        pair_kernel,
        out_shape=shape(8, width),
        in_specs=[vmem] * 2,
        out_specs=vmem,
        compiler_params=params,
        name="pair",
    )(summary, lax.ppermute(summary, "tm", [(a, a ^ MIRROR) for a in range(blocks)]))
    sums = [pair]
    for step in NEAR:
        sums.append(lax.ppermute(pair, "tm", [(a, a ^ step) for a in range(blocks)]))
    for level in range(3, rounds):
        summary = pl.pallas_call(
            functools.partial(merge_kernel, level - 1),
            out_shape=shape(4, width),
            in_specs=[smem] + [vmem] * (5 if level == 3 else 3),
            out_specs=vmem,
            compiler_params=params,
            name="merge",
        )(me, merges, *(sums if level == 3 else (summary, sums[-1])))
        step = 1 << level
        sums.append(lax.ppermute(summary, "tm", [(a, a ^ step) for a in range(blocks)]))
    local, g = pl.pallas_call(
        functools.partial(local_kernel, blocks),
        out_shape=(shape(steps, width), shape(4, -(-4 * (rounds + 5) // SUB) * SUB, width)),
        in_specs=[smem] + [vmem] * 3,
        out_specs=(vmem,) * 2,
        scratch_shapes=[pltpu.VMEM((width // 128, steps, 128), F32)],
        compiler_params=params,
        cost_estimate=pl.CostEstimate(flops=10000000, bytes_accessed=1000000, transcendentals=0),
        name="local",
    )(me, z, const, merges)
    far = list(range(2, pieces)) + [1]
    near = [0]
    residual, *parts = pl.pallas_call(
        functools.partial(finish_kernel, far),
        out_shape=(shape(steps, width, dtype=jnp.bfloat16),)
        + (shape(steps, depth, dtype=jnp.bfloat16),) * len(far),
        in_specs=[smem] + [vmem] * (5 + len(sums)),
        out_specs=(vmem,) * (1 + len(far)),
        compiler_params=params,
        name="finish",
    )(place, local, w, g, const, basis, *sums)
    arrived = [
        lax.ppermute(part, "mode", [(a, a ^ piece) for a in range(pieces)])
        for piece, part in zip(far, parts)
    ]
    grad_obs = pl.pallas_call(
        functools.partial(rest_kernel, near),
        out_shape=shape(steps, depth),
        in_specs=[smem] + [vmem] * 2,
        out_specs=vmem,
        compiler_params=params,
        cost_estimate=pl.CostEstimate(flops=80000000, bytes_accessed=1500000, transcendentals=0),
        name="rest",
    )(place, residual, basis)
    for part in arrived:
        grad_obs = grad_obs + part.astype(F32)
    return grad_obs


def solution(mesh):
    placed = (P("tm", "mode"), P(None, "mode"), P("mode"), P("mode"), P())
    return jax.shard_map(
        shards, mesh=mesh, in_specs=placed, out_specs=P("tm", "mode"), check_vma=False
    )
```

```python
import functools
import math

import jax
import jax.numpy as jnp
from jax import lax
from jax.experimental import pallas as pl
from jax.experimental.pallas import tpu as pltpu
from jax.sharding import PartitionSpec as P

F32 = jnp.float32
SUB = 8
MIRROR, NEAR = 6, (3, 1, 2)
GROUP = (0, MIRROR) + tuple(step ^ other for step in NEAR for other in (0, MIRROR))
VMEM_LIMIT = 24 * 1024 * 1024


def mat_mul(p, q):
    return (
        p[0] * q[0] + p[1] * q[2],
        p[0] * q[1] + p[1] * q[3],
        p[2] * q[0] + p[3] * q[2],
        p[2] * q[1] + p[3] * q[3],
    )


def mat_trans(p):
    return (p[0], p[2], p[1], p[3])


def mat_add(p, q):
    return tuple(a + b for a, b in zip(p, q))


def mat_sub(p, q):
    return tuple(a - b for a, b in zip(p, q))


def mat_pick(flag, p, q):
    return tuple(jnp.where(flag, a, b) for a, b in zip(p, q))


def full(s):
    return (s[0], s[1], s[1], s[2])


def congruence(s, f):
    t = (
        s[0] * f[0] + s[1] * f[2],
        s[0] * f[1] + s[1] * f[3],
        s[1] * f[0] + s[2] * f[2],
        s[1] * f[1] + s[2] * f[3],
    )
    return (f[0] * t[0] + f[2] * t[2], f[0] * t[1] + f[2] * t[3], f[1] * t[1] + f[3] * t[3])


def power(squares, exponent, like):
    one, zero = jnp.ones_like(like), jnp.zeros_like(like)
    out = None
    for bit, base in enumerate(squares):
        flag = (exponent & (1 << bit)) != 0
        if out is None:
            out = mat_pick(flag, base, (one, zero, zero, one))
        else:
            out = mat_pick(flag, mat_mul(out, base), out)
    return out


def gramian(squares, grams, count, like):
    zero = jnp.zeros_like(like)
    out = (zero, zero, zero)
    for bit, (base, gram) in enumerate(zip(squares, grams)):
        flag = (count & (1 << bit)) != 0
        out = mat_pick(flag, mat_add(gram, congruence(out, base)), out)
    return out


def steady_state(scale2, length, noise_var):
    lam = math.sqrt(3.0) / length
    decay = jnp.exp(-lam)
    twice = 2.0 * lam
    fall = jnp.exp(-twice)
    rho = scale2 / noise_var
    series = 1.0 / 604800.0
    for factor in (60480.0, 6720.0, 840.0, 120.0, 20.0, 4.0, 1.0):
        series = series * twice + 1.0 / factor
    lower = fall * twice * twice * twice * (1.0 / 6.0) * series
    loss = 1.0
    for order in (8, 7, 6, 5, 4, 3, 2):
        loss = 1.0 - lam * (1.0 / order) * loss
    loss = lam * loss
    q00 = rho * lower
    q01 = 2.0 * rho * lam * lam * fall
    q11 = rho * (lower + twice * fall)
    slope = decay * lam
    tilt = loss + slope
    g0 = q00 * tilt * tilt + 2.0 * slope * q01 * tilt + slope * slope * q11
    g1 = slope * q01 - decay * (1.0 - lam) * q00
    loss2 = loss * loss
    c2 = decay * decay
    u = (2.0 * decay * loss2 - g1) / c2
    v = (loss2 * loss2 + g0) / c2
    root = jnp.sqrt(v * (v + 4.0 * u + 16.0))
    product = 4.0 * v / (v + root + jnp.sqrt(2.0 * v * (v + 2.0 * u + root)))
    total = 0.5 * (jnp.sqrt(u * u + 4.0 * u - 2.0 * v + 2.0 * root) - u)
    gain0 = total - 2.0 * loss
    gain1 = (product - loss2 - gain0 * tilt) / slope
    inverse = (1.0 - total + product) / c2
    inn = c2 / (1.0 - total + product)
    closed = (1.0 + slope - loss - gain0, slope, -slope - gain1, decay * (1.0 - lam))
    p00 = inn * ((1.0 - lam) * gain0 - lam * gain1) / decay
    p01 = inn * (lam * gain0 + (1.0 + lam) * gain1) / decay
    p11 = (
        p01 * (loss * (1.0 + decay) + 2.0 * slope * slope)
        + slope * decay * (1.0 + lam) * p00
        - q01
        + gain0 * gain1 * inn
    ) / (slope * decay * (1.0 - lam))
    return closed, gain0, gain1, inverse, (rho - p00, -p01, rho - p11)


def coefficients_kernel(blocks, noise_ref, *refs):
    arguments, (const_ref, w_ref, merge_ref, basis_ref, obs_ref) = refs[:4], refs[4:9]
    scale_ref, length_ref, sems = refs[9:]
    targets = (scale_ref, length_ref, obs_ref, basis_ref)
    copies = [
        pltpu.make_async_copy(source, target, sems.at[k])
        for k, (source, target) in enumerate(zip(arguments, targets))
    ]
    for copy in copies:
        copy.start()
    for copy in copies[:2]:
        copy.wait()
    steps = w_ref.shape[1]
    width = scale_ref.shape[1]
    tile = (SUB, width)
    scale2 = jnp.broadcast_to(scale_ref[...], tile)
    length = jnp.broadcast_to(length_ref[...], tile)
    noise_var = jnp.full(tile, noise_ref[0], F32)
    closed, gain0, gain1, inverse, excess = steady_state(scale2, length, noise_var)
    zero = jnp.zeros(tile, F32)

    squares, grams = [closed], [(inverse, zero, zero)]
    doublings = (steps * blocks).bit_length() - 1
    for _ in range(doublings):
        base = squares[-1]
        grams.append(mat_add(grams[-1], congruence(grams[-1], base)))
        squares.append(mat_mul(base, base))
    local = steps.bit_length() - 1
    consts = closed + (gain0, gain1, inverse) + squares[3] + squares[4] + squares[5]
    for place, value in enumerate(consts):
        const_ref[place] = value
    const_ref[len(consts)] = -1.0 / noise_var
    rounds = blocks.bit_length() - 1
    groups = squares[local:-1] + [()], grams[local:], [()] * rounds + [excess]
    values = [value for group in zip(*groups) for part in group for value in part]
    for place, value in enumerate(values):
        merge_ref[place : place + 1, :] = value[0:1, :]

    row = lax.broadcasted_iota(jnp.int32, tile, 0)
    small, gram_small = squares[:3], grams[:3]
    behind = power(small, 7 - row, zero)
    gram = gramian(small, gram_small, 7 - row, zero)
    eight, gram_eight = squares[3], grams[3]
    parts = steps // SUB
    for part in range(parts - 1, -1, -1):
        rows = pl.ds(part * SUB, SUB)
        w_ref[0, rows, :] = behind[0] * gain0 + behind[1] * gain1
        w_ref[1, rows, :] = behind[2] * gain0 + behind[3] * gain1
        k0 = gain0 * gram[0] + gain1 * gram[1]
        k1 = gain0 * gram[1] + gain1 * gram[2]
        w_ref[2, rows, :] = inverse - (k0 * closed[0] + k1 * closed[2])
        w_ref[3, rows, :] = -(k0 * closed[1] + k1 * closed[3])
        if part:
            behind = mat_mul(behind, eight)
            gram = mat_add(gram_eight, congruence(gram, eight))
    ahead = power(small, row, zero)
    for part in range(parts):
        rows = pl.ds(part * SUB, SUB)
        u0, u1 = w_ref[2, rows, :], w_ref[3, rows, :]
        w_ref[2, rows, :] = u0 * ahead[0] + u1 * ahead[2]
        w_ref[3, rows, :] = u0 * ahead[1] + u1 * ahead[3]
        if part < parts - 1:
            ahead = mat_mul(ahead, eight)

    for copy in copies[2:]:
        copy.wait()


def rotate_kernel(first, place_ref, *refs):
    pieces, stage = first
    obs_refs, (basis_ref, *refs) = refs[: len(pieces)], refs[len(pieces) :]
    depth = obs_refs[0].shape[1]
    z = refs[0][...] if stage else None
    for piece, obs_ref in zip(pieces, obs_refs):
        begin = pl.multiple_of((place_ref[0] ^ piece) * depth, depth)
        term = jnp.dot(
            obs_ref[...], basis_ref[pl.ds(begin, depth), :], preferred_element_type=F32
        )
        z = term if z is None else z + term
    if stage < 2:
        refs[-1][...] = z
        return
    _, w_ref, z_ref, sum_ref = refs
    z_ref[...] = z
    for line in range(4):
        sum_ref[line : line + 1, :] = jnp.sum(w_ref[line] * z, axis=0, keepdims=True)


def merge(level, me, own, other, merge_ref):
    lower = jnp.full(own.shape, (me >> level) & 1, jnp.int32) == 0
    left, right = jnp.where(lower, own, other), jnp.where(lower, other, own)
    f00, f01, f10, f11, s00, s01, s11 = (
        merge_ref[7 * level + k : 7 * level + k + 1, :] for k in range(7)
    )
    b0, b1 = left[0:1, :], left[1:2, :]
    a0 = right[2:3, :] - s00 * b0 - s01 * b1
    a1 = right[3:4, :] - s01 * b0 - s11 * b1
    return jnp.concatenate(
        (
            right[0:1, :] + f00 * b0 + f01 * b1,
            right[1:2, :] + f10 * b0 + f11 * b1,
            left[2:3, :] + f00 * a0 + f10 * a1,
            left[3:4, :] + f01 * a0 + f11 * a1,
        ),
        axis=0,
    )


def pair_kernel(own_ref, other_ref, out_ref):
    out_ref[0:4, :] = own_ref[...]
    out_ref[4:8, :] = other_ref[...]


def merge_kernel(level, me_ref, merge_ref, *refs):
    *refs, out_ref = refs
    me = me_ref[0]
    if level > 2:
        out_ref[...] = merge(level, me, refs[0][...], refs[1][...], merge_ref)
        return
    parts = {}
    for place, step in enumerate(GROUP):
        parts[step] = refs[place // 2][4 * (place % 2) : 4 * (place % 2) + 4, :]
    for level, stride in enumerate((1, 2, 4)):
        parts = {
            step: merge(level, me ^ step, parts[step], parts[step ^ stride], merge_ref)
            for step in range(0, 8, 2 * stride)
        }
    out_ref[...] = parts[0]


def shift(value, by):
    rows = value.shape[0]
    row = lax.broadcasted_iota(jnp.int32, value.shape, 0)
    keep = row >= by if by > 0 else row < rows + by
    return jnp.where(keep, pltpu.roll(value, by % rows, 0), 0.0)


def reach(blocks, me, merge_ref, g_ref):
    tile = (SUB, merge_ref.shape[1])
    rounds = blocks.bit_length() - 1
    values = [
        jnp.broadcast_to(merge_ref[k : k + 1, :], tile) for k in range(7 * rounds + 6)
    ]
    block_squares = [tuple(values[7 * k : 7 * k + 4]) for k in range(rounds)]
    block_grams = [tuple(values[7 * k + 4 : 7 * k + 7]) for k in range(rounds)]
    s, excess = values[-6:-3], values[-3:]
    zero = jnp.zeros(tile, F32)
    row = lax.broadcasted_iota(jnp.int32, tile, 0)
    left = (
        1.0 + excess[0] * s[0] + excess[1] * s[1],
        excess[0] * s[1] + excess[1] * s[2],
        excess[1] * s[0] + excess[2] * s[1],
        1.0 + excess[1] * s[1] + excess[2] * s[2],
    )
    determ = 1.0 / (left[0] * left[3] - left[1] * left[2])
    start = mat_mul((left[3], -left[1], -left[2], left[0]), full(excess))
    start = tuple(x * determ for x in start)
    mine = jnp.full(tile, me, jnp.int32)
    to_me = power(block_squares, mine, zero)
    rest = full(gramian(block_squares, block_grams, blocks - 1 - mine, zero))
    to_state = mat_mul(to_me, start)
    to_adjoint = mat_mul(mat_mul(rest, mat_mul(to_me, block_squares[0])), start)
    for group in range(g_ref.shape[1] // SUB):
        rows = row + group * SUB
        kind = rows & 3
        line = rows >> 2
        step = jnp.zeros_like(line)
        for place, offset in enumerate(GROUP):
            step = jnp.where(line == place, offset, step)
        span = jnp.where(line < 8, 1, jnp.left_shift(1, jnp.maximum(line - 5, 0)))
        near_me = mine ^ jnp.where(line < 8, step, span)
        front = jnp.minimum((near_me // span) * span, blocks - 1)
        back = jnp.minimum(front + span - 1, blocks - 1)
        before, after = back < me, front > me
        gap = jnp.where(before, me - 1 - back, jnp.where(after, front - 1 - me, 0))
        reach = jnp.where(before, me - back, jnp.where(after, back - me, 0))
        near = power(block_squares, gap, zero)
        far = power(block_squares, reach, zero)
        origin = mat_trans(power(block_squares, front, zero))
        left_over = full(gramian(block_squares, block_grams, blocks - 1 - back, zero))
        end = mat_trans(mat_mul(power(block_squares, back, zero), block_squares[0]))
        first = mat_mul(end, left_over)
        state_b = mat_sub(mat_pick(before, near, (zero,) * 4), mat_mul(to_state, first))
        state_l = mat_mul(to_state, origin)
        cross = mat_pick(after, mat_mul(mat_trans(far), left_over), mat_mul(rest, far))
        adjoint_b = mat_sub(mat_mul(to_adjoint, first), cross)
        adjoint_l = mat_sub(
            mat_pick(after, mat_trans(near), (zero,) * 4), mat_mul(to_adjoint, origin)
        )
        place = pl.ds(group * SUB, SUB)
        for output, (from_b, from_l) in enumerate(
            ((adjoint_b[:2], adjoint_l[:2]), (adjoint_b[2:], adjoint_l[2:]),
             (state_b[:2], state_l[:2]), (state_b[2:], state_l[2:]))
        ):
            g_ref[output, place, :] = jnp.where(
                kind < 2,
                jnp.where(kind == 0, from_b[0], from_b[1]),
                jnp.where(kind == 2, from_l[0], from_l[1]),
            )


def local_kernel(blocks, me_ref, z_ref, const_ref, merge_ref, r_ref, g_ref, scratch):
    reach(blocks, me_ref[0], merge_ref, g_ref)
    steps, width = z_ref.shape
    span = steps // SUB
    lanes = 128
    for chunk in range(width // lanes):
        cols = pl.ds(chunk * lanes, lanes)
        scratch[chunk] = z_ref[:, cols]
    for chunk in range(width // lanes):
        cols = pl.ds(chunk * lanes, lanes)
        const = [const_ref[k, :, cols] for k in range(19)]
        f, (k0, k1, inverse) = const[0:4], const[4:7]
        jumps = (const[7:11], const[11:15], const[15:19])
        zero = jnp.zeros((SUB, lanes), F32)
        x0, x1 = zero, zero
        vs = []
        for t in range(span):
            z = scratch[chunk, pl.ds(t, SUB, stride=span), :]
            vs.append(z - x0)
            x0, x1 = f[0] * x0 + f[1] * x1 + k0 * z, f[2] * x0 + f[3] * x1 + k1 * z
        for level, jump in enumerate(jumps):
            s0, s1 = shift(x0, 1 << level), shift(x1, 1 << level)
            x0, x1 = x0 + jump[0] * s0 + jump[1] * s1, x1 + jump[2] * s0 + jump[3] * s1
        x0, x1 = shift(x0, 1), shift(x1, 1)
        for t in range(span):
            vs[t] = (vs[t] - x0) * inverse
            x0, x1 = f[0] * x0 + f[1] * x1, f[2] * x0 + f[3] * x1
        a0, a1 = zero, zero
        for t in range(span - 1, -1, -1):
            a0, a1 = f[0] * a0 + f[2] * a1 + vs[t], f[1] * a0 + f[3] * a1
        for level, jump in enumerate(jumps):
            s0, s1 = shift(a0, -(1 << level)), shift(a1, -(1 << level))
            a0, a1 = a0 + jump[0] * s0 + jump[2] * s1, a1 + jump[1] * s0 + jump[3] * s1
        a0, a1 = shift(a0, -1), shift(a1, -1)
        for t in range(span - 1, -1, -1):
            r = vs[t] - k0 * a0 - k1 * a1
            a0, a1 = f[0] * a0 + f[2] * a1 + vs[t], f[1] * a0 + f[3] * a1
            scratch[chunk, pl.ds(t, SUB, stride=span), :] = r
        r_ref[:, cols] = scratch[chunk]


def rotate_back(residual, pieces, place_ref, basis_ref, outs):
    depth = outs[0].shape[1]
    for piece, out_ref in zip(pieces, outs):
        begin = pl.multiple_of((place_ref[0] ^ piece) * depth, depth)
        out_ref[...] = lax.dot_general(
            residual,
            basis_ref[pl.ds(begin, depth), :],
            (((1,), (1,)), ((), ())),
            preferred_element_type=F32,
        ).astype(out_ref.dtype)


def finish_kernel(pieces, place_ref, r_ref, w_ref, g_ref, const_ref, basis_ref, *refs):
    *sums, residual_ref = refs[: -len(pieces)]
    value = r_ref[...]
    for line in range(4):
        total, place = 0.0, 0
        for sum_ref in sums:
            count = sum_ref.shape[0]
            term = g_ref[line, pl.ds(place, count), :] * sum_ref[...]
            total = total + jnp.sum(term, axis=0, keepdims=True) if count < SUB else total + term
            place += count
            if place == 4 * len(GROUP):
                total = jnp.sum(total, axis=0, keepdims=True)
        value = value - w_ref[line] * total
    scale = const_ref[19, 0:1, :]
    residual = (value * scale).astype(jnp.bfloat16)
    residual_ref[...] = residual
    rotate_back(residual, pieces, place_ref, basis_ref, refs[-len(pieces) :])


def rest_kernel(pieces, place_ref, residual_ref, basis_ref, *outs):
    rotate_back(residual_ref[...], pieces, place_ref, basis_ref, outs)


def exchange(value, axis, count):
    out = [value]
    for step in range(1, count):
        out.append(lax.ppermute(value, axis, [(a, a ^ step) for a in range(count)]))
    return out


def shards(observations, basis, eigvals, lengths, noise):
    steps, depth = observations.shape
    width = basis.shape[1]
    blocks, pieces = lax.axis_size("tm"), lax.axis_size("mode")
    me = lax.axis_index("tm").astype(jnp.int32).reshape(1)
    place = lax.axis_index("mode").astype(jnp.int32).reshape(1)
    rounds = blocks.bit_length() - 1
    vmem = pl.BlockSpec(memory_space=pltpu.VMEM)
    smem = pl.BlockSpec(memory_space=pltpu.SMEM)
    params = pltpu.CompilerParams(vmem_limit_bytes=VMEM_LIMIT)

    def shape(*dims, dtype=F32):
        return jax.ShapeDtypeStruct(dims, dtype)

    obs = exchange(observations, "mode", pieces)
    const, w, merges, basis, obs[0] = pl.pallas_call(
        functools.partial(coefficients_kernel, blocks),
        out_shape=(
            shape(20, SUB, width),
            shape(4, steps, width),
            shape(-(-(7 * rounds + 6) // SUB) * SUB, width),
            shape(*basis.shape, dtype=basis.dtype),
            shape(steps, depth, dtype=observations.dtype),
        ),
        in_specs=[smem] + [pl.BlockSpec(memory_space=pltpu.HBM)] * 4,
        out_specs=(vmem,) * 5,
        scratch_shapes=[
            pltpu.VMEM((1, width), F32),
            pltpu.VMEM((1, width), F32),
            pltpu.SemaphoreType.DMA((4,)),
        ],
        compiler_params=params,
        cost_estimate=pl.CostEstimate(flops=20000000, bytes_accessed=2000000, transcendentals=0),
        name="coefficients",
    )(
        noise,
        *(
            pltpu.with_memory_space_constraint(x, pltpu.HBM)
            for x in (
                eigvals.reshape(1, width),
                lengths.reshape(1, width),
                observations,
                basis,
            )
        ),
    )
    last = pieces - 1
    z = ()
    for stage, group in enumerate(([0], list(range(last - 1, 0, -1)))):
        z = pl.pallas_call(
            functools.partial(rotate_kernel, (group, stage)),
            out_shape=shape(steps, width),
            in_specs=[smem] + [vmem] * (len(group) + 1 + len(z)),
            out_specs=vmem,
            compiler_params=params,
            name="rotate_early",
        )(place, *(obs[piece] for piece in group), basis, *z)
        z = (z,)
    z, summary = pl.pallas_call(
        functools.partial(rotate_kernel, ([last], 2)),
        out_shape=(shape(steps, width), shape(4, width)),
        in_specs=[smem] + [vmem] * 4,
        out_specs=(vmem,) * 2,
        compiler_params=params,
        name="rotate_last",
    )(place, obs[last], basis, *z, w)
    pair = pl.pallas_call(
        pair_kernel,
        out_shape=shape(8, width),
        in_specs=[vmem] * 2,
        out_specs=vmem,
        compiler_params=params,
        name="pair",
    )(summary, lax.ppermute(summary, "tm", [(a, a ^ MIRROR) for a in range(blocks)]))
    sums = [pair]
    for step in NEAR:
        sums.append(lax.ppermute(pair, "tm", [(a, a ^ step) for a in range(blocks)]))
    for level in range(3, rounds):
        summary = pl.pallas_call(
            functools.partial(merge_kernel, level - 1),
            out_shape=shape(4, width),
            in_specs=[smem] + [vmem] * (5 if level == 3 else 3),
            out_specs=vmem,
            compiler_params=params,
            name="merge",
        )(me, merges, *(sums if level == 3 else (summary, sums[-1])))
        step = 1 << level
        sums.append(lax.ppermute(summary, "tm", [(a, a ^ step) for a in range(blocks)]))
    local, g = pl.pallas_call(
        functools.partial(local_kernel, blocks),
        out_shape=(shape(steps, width), shape(4, -(-4 * (rounds + 5) // SUB) * SUB, width)),
        in_specs=[smem] + [vmem] * 3,
        out_specs=(vmem,) * 2,
        scratch_shapes=[pltpu.VMEM((width // 128, steps, 128), F32)],
        compiler_params=params,
        cost_estimate=pl.CostEstimate(flops=10000000, bytes_accessed=1000000, transcendentals=0),
        name="local",
    )(me, z, const, merges)
    residual, part_y, part_d = pl.pallas_call(
        functools.partial(finish_kernel, [2, 3]),
        out_shape=(shape(steps, width, dtype=jnp.bfloat16),)
        + (shape(steps, depth, dtype=jnp.bfloat16),) * 2,
        in_specs=[smem] + [vmem] * (5 + len(sums)),
        out_specs=(vmem,) * 3,
        compiler_params=params,
        name="finish",
    )(place, local, w, g, const, basis, *sums)
    from_y, from_d = (
        lax.ppermute(part, "mode", [(a, a ^ piece) for a in range(pieces)])
        for piece, part in ((2, part_y), (3, part_d))
    )
    own, part_m = pl.pallas_call(
        functools.partial(rest_kernel, [0, 1]),
        out_shape=(shape(steps, depth), shape(steps, depth, dtype=jnp.bfloat16)),
        in_specs=[smem] + [vmem] * 2,
        out_specs=(vmem,) * 2,
        compiler_params=params,
        name="rest",
    )(place, residual, basis)
    from_m = lax.ppermute(part_m, "mode", [(a, a ^ 1) for a in range(pieces)])
    own, from_y, from_d, from_m = (v.astype(F32) for v in (own, from_y, from_d, from_m))
    return (own + from_m) + (from_d + from_y)


def solution(mesh):
    placed = (P("tm", "mode"), P(None, "mode"), P("mode"), P("mode"), P())
    return jax.shard_map(
        shards, mesh=mesh, in_specs=placed, out_specs=P("tm", "mode"), check_vma=False
    )
```

```python
import functools
import math

import jax
import jax.numpy as jnp
from jax import lax
from jax.experimental import pallas as pl
from jax.experimental.pallas import tpu as pltpu
from jax.sharding import PartitionSpec as P

F32 = jnp.float32
SUB = 8
MIRROR, NEAR = 6, (3, 1, 2)
GROUP = (0, MIRROR) + tuple(step ^ other for step in NEAR for other in (0, MIRROR))
VMEM_LIMIT = 24 * 1024 * 1024


def mat_mul(p, q):
    return (
        p[0] * q[0] + p[1] * q[2],
        p[0] * q[1] + p[1] * q[3],
        p[2] * q[0] + p[3] * q[2],
        p[2] * q[1] + p[3] * q[3],
    )


def mat_trans(p):
    return (p[0], p[2], p[1], p[3])


def mat_add(p, q):
    return tuple(a + b for a, b in zip(p, q))


def mat_sub(p, q):
    return tuple(a - b for a, b in zip(p, q))


def mat_pick(flag, p, q):
    return tuple(jnp.where(flag, a, b) for a, b in zip(p, q))


def full(s):
    return (s[0], s[1], s[1], s[2])


def congruence(s, f):
    t = (
        s[0] * f[0] + s[1] * f[2],
        s[0] * f[1] + s[1] * f[3],
        s[1] * f[0] + s[2] * f[2],
        s[1] * f[1] + s[2] * f[3],
    )
    return (f[0] * t[0] + f[2] * t[2], f[0] * t[1] + f[2] * t[3], f[1] * t[1] + f[3] * t[3])


def power(squares, exponent, like):
    one, zero = jnp.ones_like(like), jnp.zeros_like(like)
    out = None
    for bit, base in enumerate(squares):
        flag = (exponent & (1 << bit)) != 0
        if out is None:
            out = mat_pick(flag, base, (one, zero, zero, one))
        else:
            out = mat_pick(flag, mat_mul(out, base), out)
    return out


def gramian(squares, grams, count, like):
    zero = jnp.zeros_like(like)
    out = (zero, zero, zero)
    for bit, (base, gram) in enumerate(zip(squares, grams)):
        flag = (count & (1 << bit)) != 0
        out = mat_pick(flag, mat_add(gram, congruence(out, base)), out)
    return out


def steady_state(scale2, length, noise_var):
    lam = math.sqrt(3.0) / length
    decay = jnp.exp(-lam)
    twice = 2.0 * lam
    fall = jnp.exp(-twice)
    rho = scale2 / noise_var
    series = 1.0 / 604800.0
    for factor in (60480.0, 6720.0, 840.0, 120.0, 20.0, 4.0, 1.0):
        series = series * twice + 1.0 / factor
    lower = fall * twice * twice * twice * (1.0 / 6.0) * series
    loss = 1.0
    for order in (8, 7, 6, 5, 4, 3, 2):
        loss = 1.0 - lam * (1.0 / order) * loss
    loss = lam * loss
    q00 = rho * lower
    q01 = 2.0 * rho * lam * lam * fall
    q11 = rho * (lower + twice * fall)
    slope = decay * lam
    tilt = loss + slope
    g0 = q00 * tilt * tilt + 2.0 * slope * q01 * tilt + slope * slope * q11
    g1 = slope * q01 - decay * (1.0 - lam) * q00
    loss2 = loss * loss
    c2 = decay * decay
    u = (2.0 * decay * loss2 - g1) / c2
    v = (loss2 * loss2 + g0) / c2
    root = jnp.sqrt(v * (v + 4.0 * u + 16.0))
    product = 4.0 * v / (v + root + jnp.sqrt(2.0 * v * (v + 2.0 * u + root)))
    total = 0.5 * (jnp.sqrt(u * u + 4.0 * u - 2.0 * v + 2.0 * root) - u)
    gain0 = total - 2.0 * loss
    gain1 = (product - loss2 - gain0 * tilt) / slope
    inverse = (1.0 - total + product) / c2
    inn = c2 / (1.0 - total + product)
    closed = (1.0 + slope - loss - gain0, slope, -slope - gain1, decay * (1.0 - lam))
    p00 = inn * ((1.0 - lam) * gain0 - lam * gain1) / decay
    p01 = inn * (lam * gain0 + (1.0 + lam) * gain1) / decay
    p11 = (
        p01 * (loss * (1.0 + decay) + 2.0 * slope * slope)
        + slope * decay * (1.0 + lam) * p00
        - q01
        + gain0 * gain1 * inn
    ) / (slope * decay * (1.0 - lam))
    return closed, gain0, gain1, inverse, (rho - p00, -p01, rho - p11)


def coefficients_kernel(blocks, noise_ref, *refs):
    arguments, (const_ref, w_ref, merge_ref, basis_ref, obs_ref) = refs[:4], refs[4:9]
    scale_ref, length_ref, sems = refs[9:]
    targets = (scale_ref, length_ref, obs_ref, basis_ref)
    copies = [
        pltpu.make_async_copy(source, target, sems.at[k])
        for k, (source, target) in enumerate(zip(arguments, targets))
    ]
    for copy in copies:
        copy.start()
    for copy in copies[:2]:
        copy.wait()
    steps = w_ref.shape[1]
    width = scale_ref.shape[1]
    tile = (SUB, width)
    scale2 = jnp.broadcast_to(scale_ref[...], tile)
    length = jnp.broadcast_to(length_ref[...], tile)
    noise_var = jnp.full(tile, noise_ref[0], F32)
    closed, gain0, gain1, inverse, excess = steady_state(scale2, length, noise_var)
    zero = jnp.zeros(tile, F32)

    squares, grams = [closed], [(inverse, zero, zero)]
    doublings = (steps * blocks).bit_length() - 1
    for _ in range(doublings):
        base = squares[-1]
        grams.append(mat_add(grams[-1], congruence(grams[-1], base)))
        squares.append(mat_mul(base, base))
    local = steps.bit_length() - 1
    consts = closed + (gain0, gain1, inverse) + squares[3] + squares[4] + squares[5]
    for place, value in enumerate(consts):
        const_ref[place] = value
    const_ref[len(consts)] = -1.0 / noise_var
    rounds = blocks.bit_length() - 1
    groups = squares[local:-1] + [()], grams[local:], [()] * rounds + [excess]
    values = [value for group in zip(*groups) for part in group for value in part]
    for place, value in enumerate(values):
        merge_ref[place : place + 1, :] = value[0:1, :]

    row = lax.broadcasted_iota(jnp.int32, tile, 0)
    small, gram_small = squares[:3], grams[:3]
    behind = power(small, 7 - row, zero)
    gram = gramian(small, gram_small, 7 - row, zero)
    eight, gram_eight = squares[3], grams[3]
    parts = steps // SUB
    for part in range(parts - 1, -1, -1):
        rows = pl.ds(part * SUB, SUB)
        w_ref[0, rows, :] = behind[0] * gain0 + behind[1] * gain1
        w_ref[1, rows, :] = behind[2] * gain0 + behind[3] * gain1
        k0 = gain0 * gram[0] + gain1 * gram[1]
        k1 = gain0 * gram[1] + gain1 * gram[2]
        w_ref[2, rows, :] = inverse - (k0 * closed[0] + k1 * closed[2])
        w_ref[3, rows, :] = -(k0 * closed[1] + k1 * closed[3])
        if part:
            behind = mat_mul(behind, eight)
            gram = mat_add(gram_eight, congruence(gram, eight))
    ahead = power(small, row, zero)
    for part in range(parts):
        rows = pl.ds(part * SUB, SUB)
        u0, u1 = w_ref[2, rows, :], w_ref[3, rows, :]
        w_ref[2, rows, :] = u0 * ahead[0] + u1 * ahead[2]
        w_ref[3, rows, :] = u0 * ahead[1] + u1 * ahead[3]
        if part < parts - 1:
            ahead = mat_mul(ahead, eight)

    for copy in copies[2:]:
        copy.wait()


def rotate_kernel(first, place_ref, *refs):
    pieces, stage = first
    obs_refs, (basis_ref, *refs) = refs[: len(pieces)], refs[len(pieces) :]
    depth = obs_refs[0].shape[1]
    z = refs[0][...] if stage else None
    for piece, obs_ref in zip(pieces, obs_refs):
        begin = pl.multiple_of((place_ref[0] ^ piece) * depth, depth)
        term = jnp.dot(
            obs_ref[...], basis_ref[pl.ds(begin, depth), :], preferred_element_type=F32
        )
        z = term if z is None else z + term
    if stage < 2:
        refs[-1][...] = z
        return
    _, w_ref, z_ref, sum_ref = refs
    z_ref[...] = z
    for line in range(4):
        sum_ref[line : line + 1, :] = jnp.sum(w_ref[line] * z, axis=0, keepdims=True)


def merge(level, me, own, other, merge_ref):
    lower = jnp.full(own.shape, (me >> level) & 1, jnp.int32) == 0
    left, right = jnp.where(lower, own, other), jnp.where(lower, other, own)
    f00, f01, f10, f11, s00, s01, s11 = (
        merge_ref[7 * level + k : 7 * level + k + 1, :] for k in range(7)
    )
    b0, b1 = left[0:1, :], left[1:2, :]
    a0 = right[2:3, :] - s00 * b0 - s01 * b1
    a1 = right[3:4, :] - s01 * b0 - s11 * b1
    return jnp.concatenate(
        (
            right[0:1, :] + f00 * b0 + f01 * b1,
            right[1:2, :] + f10 * b0 + f11 * b1,
            left[2:3, :] + f00 * a0 + f10 * a1,
            left[3:4, :] + f01 * a0 + f11 * a1,
        ),
        axis=0,
    )


def pair_kernel(own_ref, other_ref, out_ref):
    out_ref[0:4, :] = own_ref[...]
    out_ref[4:8, :] = other_ref[...]


def merge_kernel(level, me_ref, merge_ref, *refs):
    *refs, out_ref = refs
    me = me_ref[0]
    if level > 2:
        out_ref[...] = merge(level, me, refs[0][...], refs[1][...], merge_ref)
        return
    parts = {}
    for place, step in enumerate(GROUP):
        parts[step] = refs[place // 2][4 * (place % 2) : 4 * (place % 2) + 4, :]
    for level, stride in enumerate((1, 2, 4)):
        parts = {
            step: merge(level, me ^ step, parts[step], parts[step ^ stride], merge_ref)
            for step in range(0, 8, 2 * stride)
        }
    out_ref[...] = parts[0]


def shift(value, by):
    rows = value.shape[0]
    row = lax.broadcasted_iota(jnp.int32, value.shape, 0)
    keep = row >= by if by > 0 else row < rows + by
    return jnp.where(keep, pltpu.roll(value, by % rows, 0), 0.0)


def reach(blocks, me, merge_ref, g_ref):
    tile = (SUB, merge_ref.shape[1])
    rounds = blocks.bit_length() - 1
    values = [
        jnp.broadcast_to(merge_ref[k : k + 1, :], tile) for k in range(7 * rounds + 6)
    ]
    block_squares = [tuple(values[7 * k : 7 * k + 4]) for k in range(rounds)]
    block_grams = [tuple(values[7 * k + 4 : 7 * k + 7]) for k in range(rounds)]
    s, excess = values[-6:-3], values[-3:]
    zero = jnp.zeros(tile, F32)
    row = lax.broadcasted_iota(jnp.int32, tile, 0)
    left = (
        1.0 + excess[0] * s[0] + excess[1] * s[1],
        excess[0] * s[1] + excess[1] * s[2],
        excess[1] * s[0] + excess[2] * s[1],
        1.0 + excess[1] * s[1] + excess[2] * s[2],
    )
    determ = 1.0 / (left[0] * left[3] - left[1] * left[2])
    start = mat_mul((left[3], -left[1], -left[2], left[0]), full(excess))
    start = tuple(x * determ for x in start)
    mine = jnp.full(tile, me, jnp.int32)
    to_me = power(block_squares, mine, zero)
    rest = full(gramian(block_squares, block_grams, blocks - 1 - mine, zero))
    to_state = mat_mul(to_me, start)
    to_adjoint = mat_mul(mat_mul(rest, mat_mul(to_me, block_squares[0])), start)
    for group in range(g_ref.shape[1] // SUB):
        rows = row + group * SUB
        kind = rows & 3
        line = rows >> 2
        step = jnp.zeros_like(line)
        for place, offset in enumerate(GROUP):
            step = jnp.where(line == place, offset, step)
        span = jnp.where(line < 8, 1, jnp.left_shift(1, jnp.maximum(line - 5, 0)))
        near_me = mine ^ jnp.where(line < 8, step, span)
        front = jnp.minimum((near_me // span) * span, blocks - 1)
        back = jnp.minimum(front + span - 1, blocks - 1)
        before, after = back < me, front > me
        gap = jnp.where(before, me - 1 - back, jnp.where(after, front - 1 - me, 0))
        reach = jnp.where(before, me - back, jnp.where(after, back - me, 0))
        near = power(block_squares, gap, zero)
        far = power(block_squares, reach, zero)
        origin = mat_trans(power(block_squares, front, zero))
        left_over = full(gramian(block_squares, block_grams, blocks - 1 - back, zero))
        end = mat_trans(mat_mul(power(block_squares, back, zero), block_squares[0]))
        first = mat_mul(end, left_over)
        state_b = mat_sub(mat_pick(before, near, (zero,) * 4), mat_mul(to_state, first))
        state_l = mat_mul(to_state, origin)
        cross = mat_pick(after, mat_mul(mat_trans(far), left_over), mat_mul(rest, far))
        adjoint_b = mat_sub(mat_mul(to_adjoint, first), cross)
        adjoint_l = mat_sub(
            mat_pick(after, mat_trans(near), (zero,) * 4), mat_mul(to_adjoint, origin)
        )
        place = pl.ds(group * SUB, SUB)
        for output, (from_b, from_l) in enumerate(
            ((adjoint_b[:2], adjoint_l[:2]), (adjoint_b[2:], adjoint_l[2:]),
             (state_b[:2], state_l[:2]), (state_b[2:], state_l[2:]))
        ):
            g_ref[output, place, :] = jnp.where(
                kind < 2,
                jnp.where(kind == 0, from_b[0], from_b[1]),
                jnp.where(kind == 2, from_l[0], from_l[1]),
            )


def local_kernel(blocks, me_ref, z_ref, const_ref, merge_ref, r_ref, g_ref, scratch):
    reach(blocks, me_ref[0], merge_ref, g_ref)
    steps, width = z_ref.shape
    span = steps // SUB
    lanes = 128
    for chunk in range(width // lanes):
        cols = pl.ds(chunk * lanes, lanes)
        scratch[chunk] = z_ref[:, cols]
    for chunk in range(width // lanes):
        cols = pl.ds(chunk * lanes, lanes)
        const = [const_ref[k, :, cols] for k in range(19)]
        f, (k0, k1, inverse) = const[0:4], const[4:7]
        jumps = (const[7:11], const[11:15], const[15:19])
        zero = jnp.zeros((SUB, lanes), F32)
        x0, x1 = zero, zero
        vs = []
        for t in range(span):
            z = scratch[chunk, pl.ds(t, SUB, stride=span), :]
            vs.append(z - x0)
            x0, x1 = f[0] * x0 + f[1] * x1 + k0 * z, f[2] * x0 + f[3] * x1 + k1 * z
        for level, jump in enumerate(jumps):
            s0, s1 = shift(x0, 1 << level), shift(x1, 1 << level)
            x0, x1 = x0 + jump[0] * s0 + jump[1] * s1, x1 + jump[2] * s0 + jump[3] * s1
        x0, x1 = shift(x0, 1), shift(x1, 1)
        for t in range(span):
            vs[t] = (vs[t] - x0) * inverse
            x0, x1 = f[0] * x0 + f[1] * x1, f[2] * x0 + f[3] * x1
        a0, a1 = zero, zero
        for t in range(span - 1, -1, -1):
            a0, a1 = f[0] * a0 + f[2] * a1 + vs[t], f[1] * a0 + f[3] * a1
        for level, jump in enumerate(jumps):
            s0, s1 = shift(a0, -(1 << level)), shift(a1, -(1 << level))
            a0, a1 = a0 + jump[0] * s0 + jump[2] * s1, a1 + jump[1] * s0 + jump[3] * s1
        a0, a1 = shift(a0, -1), shift(a1, -1)
        for t in range(span - 1, -1, -1):
            r = vs[t] - k0 * a0 - k1 * a1
            a0, a1 = f[0] * a0 + f[2] * a1 + vs[t], f[1] * a0 + f[3] * a1
            scratch[chunk, pl.ds(t, SUB, stride=span), :] = r
        r_ref[:, cols] = scratch[chunk]


def rotate_back(residual, pieces, place_ref, basis_ref, outs):
    depth = outs[0].shape[1]
    for piece, out_ref in zip(pieces, outs):
        begin = pl.multiple_of((place_ref[0] ^ piece) * depth, depth)
        out_ref[...] = lax.dot_general(
            residual,
            basis_ref[pl.ds(begin, depth), :],
            (((1,), (1,)), ((), ())),
            preferred_element_type=F32,
        ).astype(out_ref.dtype)


def finish_kernel(pieces, place_ref, r_ref, w_ref, g_ref, const_ref, basis_ref, *refs):
    *sums, residual_ref = refs[: -len(pieces)]
    value = r_ref[...]
    for line in range(4):
        total, place = 0.0, 0
        for sum_ref in sums:
            count = sum_ref.shape[0]
            term = g_ref[line, pl.ds(place, count), :] * sum_ref[...]
            total = total + jnp.sum(term, axis=0, keepdims=True) if count < SUB else total + term
            place += count
            if place == 4 * len(GROUP):
                total = jnp.sum(total, axis=0, keepdims=True)
        value = value - w_ref[line] * total
    scale = const_ref[19, 0:1, :]
    residual = (value * scale).astype(jnp.bfloat16)
    residual_ref[...] = residual
    rotate_back(residual, pieces, place_ref, basis_ref, refs[-len(pieces) :])


def rest_kernel(pieces, place_ref, residual_ref, basis_ref, *outs):
    rotate_back(residual_ref[...], pieces, place_ref, basis_ref, outs)


def exchange(value, axis, count):
    out = [value]
    for step in range(1, count):
        out.append(lax.ppermute(value, axis, [(a, a ^ step) for a in range(count)]))
    return out


def shards(observations, basis, eigvals, lengths, noise):
    steps, depth = observations.shape
    width = basis.shape[1]
    blocks, pieces = lax.axis_size("tm"), lax.axis_size("mode")
    me = lax.axis_index("tm").astype(jnp.int32).reshape(1)
    place = lax.axis_index("mode").astype(jnp.int32).reshape(1)
    rounds = blocks.bit_length() - 1
    vmem = pl.BlockSpec(memory_space=pltpu.VMEM)
    smem = pl.BlockSpec(memory_space=pltpu.SMEM)
    params = pltpu.CompilerParams(vmem_limit_bytes=VMEM_LIMIT)

    def shape(*dims, dtype=F32):
        return jax.ShapeDtypeStruct(dims, dtype)

    obs = exchange(observations, "mode", pieces)
    const, w, merges, basis, obs[0] = pl.pallas_call(
        functools.partial(coefficients_kernel, blocks),
        out_shape=(
            shape(20, SUB, width),
            shape(4, steps, width),
            shape(-(-(7 * rounds + 6) // SUB) * SUB, width),
            shape(*basis.shape, dtype=basis.dtype),
            shape(steps, depth, dtype=observations.dtype),
        ),
        in_specs=[smem] + [pl.BlockSpec(memory_space=pltpu.HBM)] * 4,
        out_specs=(vmem,) * 5,
        scratch_shapes=[
            pltpu.VMEM((1, width), F32),
            pltpu.VMEM((1, width), F32),
            pltpu.SemaphoreType.DMA((4,)),
        ],
        compiler_params=params,
        cost_estimate=pl.CostEstimate(flops=20000000, bytes_accessed=2000000, transcendentals=0),
        name="coefficients",
    )(
        noise,
        *(
            pltpu.with_memory_space_constraint(x, pltpu.HBM)
            for x in (
                eigvals.reshape(1, width),
                lengths.reshape(1, width),
                observations,
                basis,
            )
        ),
    )
    last = [3, 1]
    z = ()
    for stage, group in enumerate(([0], [2])):
        z = pl.pallas_call(
            functools.partial(rotate_kernel, (group, stage)),
            out_shape=shape(steps, width),
            in_specs=[smem] + [vmem] * (len(group) + 1 + len(z)),
            out_specs=vmem,
            compiler_params=params,
            name="rotate_early",
        )(place, *(obs[piece] for piece in group), basis, *z)
        z = (z,)
    z, summary = pl.pallas_call(
        functools.partial(rotate_kernel, (last, 2)),
        out_shape=(shape(steps, width), shape(4, width)),
        in_specs=[smem] + [vmem] * (3 + len(last)),
        out_specs=(vmem,) * 2,
        compiler_params=params,
        name="rotate_last",
    )(place, *(obs[piece] for piece in last), basis, *z, w)
    pair = pl.pallas_call(
        pair_kernel,
        out_shape=shape(8, width),
        in_specs=[vmem] * 2,
        out_specs=vmem,
        compiler_params=params,
        name="pair",
    )(summary, lax.ppermute(summary, "tm", [(a, a ^ MIRROR) for a in range(blocks)]))
    sums = [pair]
    for step in NEAR:
        sums.append(lax.ppermute(pair, "tm", [(a, a ^ step) for a in range(blocks)]))
    for level in range(3, rounds):
        summary = pl.pallas_call(
            functools.partial(merge_kernel, level - 1),
            out_shape=shape(4, width),
            in_specs=[smem] + [vmem] * (5 if level == 3 else 3),
            out_specs=vmem,
            compiler_params=params,
            name="merge",
        )(me, merges, *(sums if level == 3 else (summary, sums[-1])))
        step = 1 << level
        sums.append(lax.ppermute(summary, "tm", [(a, a ^ step) for a in range(blocks)]))
    local, g = pl.pallas_call(
        functools.partial(local_kernel, blocks),
        out_shape=(shape(steps, width), shape(4, -(-4 * (rounds + 5) // SUB) * SUB, width)),
        in_specs=[smem] + [vmem] * 3,
        out_specs=(vmem,) * 2,
        scratch_shapes=[pltpu.VMEM((width // 128, steps, 128), F32)],
        compiler_params=params,
        cost_estimate=pl.CostEstimate(flops=10000000, bytes_accessed=1000000, transcendentals=0),
        name="local",
    )(me, z, const, merges)
    residual, part_y, part_d = pl.pallas_call(
        functools.partial(finish_kernel, [2, 3]),
        out_shape=(shape(steps, width, dtype=jnp.bfloat16),)
        + (shape(steps, depth, dtype=jnp.bfloat16),) * 2,
        in_specs=[smem] + [vmem] * (5 + len(sums)),
        out_specs=(vmem,) * 3,
        compiler_params=params,
        name="finish",
    )(place, local, w, g, const, basis, *sums)
    from_y, from_d = (
        lax.ppermute(part, "mode", [(a, a ^ piece) for a in range(pieces)])
        for piece, part in ((2, part_y), (3, part_d))
    )
    own, part_m = pl.pallas_call(
        functools.partial(rest_kernel, [0, 1]),
        out_shape=(shape(steps, depth), shape(steps, depth, dtype=jnp.bfloat16)),
        in_specs=[smem] + [vmem] * 2,
        out_specs=(vmem,) * 2,
        compiler_params=params,
        name="rest",
    )(place, residual, basis)
    from_m = lax.ppermute(part_m, "mode", [(a, a ^ 1) for a in range(pieces)])
    own, from_y, from_d, from_m = (v.astype(F32) for v in (own, from_y, from_d, from_m))
    return (own + from_m) + (from_d + from_y)


def solution(mesh):
    placed = (P("tm", "mode"), P(None, "mode"), P("mode"), P("mode"), P())
    return jax.shard_map(
        shards, mesh=mesh, in_specs=placed, out_specs=P("tm", "mode"), check_vma=False
    )
```

```python
import functools
import math

import jax
import jax.numpy as jnp
from jax import lax
from jax.experimental import pallas as pl
from jax.experimental.pallas import tpu as pltpu
from jax.sharding import PartitionSpec as P

F32 = jnp.float32
SUB = 8
MIRROR, NEAR = 6, (3, 1, 2)
GROUP = (0, MIRROR) + tuple(step ^ other for step in NEAR for other in (0, MIRROR))
VMEM_LIMIT = 24 * 1024 * 1024


def mat_mul(p, q):
    return (
        p[0] * q[0] + p[1] * q[2],
        p[0] * q[1] + p[1] * q[3],
        p[2] * q[0] + p[3] * q[2],
        p[2] * q[1] + p[3] * q[3],
    )


def mat_trans(p):
    return (p[0], p[2], p[1], p[3])


def mat_add(p, q):
    return tuple(a + b for a, b in zip(p, q))


def mat_sub(p, q):
    return tuple(a - b for a, b in zip(p, q))


def mat_pick(flag, p, q):
    return tuple(jnp.where(flag, a, b) for a, b in zip(p, q))


def full(s):
    return (s[0], s[1], s[1], s[2])


def congruence(s, f):
    t = (
        s[0] * f[0] + s[1] * f[2],
        s[0] * f[1] + s[1] * f[3],
        s[1] * f[0] + s[2] * f[2],
        s[1] * f[1] + s[2] * f[3],
    )
    return (f[0] * t[0] + f[2] * t[2], f[0] * t[1] + f[2] * t[3], f[1] * t[1] + f[3] * t[3])


def power(squares, exponent, like):
    one, zero = jnp.ones_like(like), jnp.zeros_like(like)
    out = None
    for bit, base in enumerate(squares):
        flag = (exponent & (1 << bit)) != 0
        if out is None:
            out = mat_pick(flag, base, (one, zero, zero, one))
        else:
            out = mat_pick(flag, mat_mul(out, base), out)
    return out


def gramian(squares, grams, count, like):
    zero = jnp.zeros_like(like)
    out = (zero, zero, zero)
    for bit, (base, gram) in enumerate(zip(squares, grams)):
        flag = (count & (1 << bit)) != 0
        out = mat_pick(flag, mat_add(gram, congruence(out, base)), out)
    return out


def steady_state(scale2, length, noise_var):
    lam = math.sqrt(3.0) / length
    decay = jnp.exp(-lam)
    twice = 2.0 * lam
    fall = jnp.exp(-twice)
    rho = scale2 / noise_var
    series = 1.0 / 604800.0
    for factor in (60480.0, 6720.0, 840.0, 120.0, 20.0, 4.0, 1.0):
        series = series * twice + 1.0 / factor
    lower = fall * twice * twice * twice * (1.0 / 6.0) * series
    loss = 1.0
    for order in (8, 7, 6, 5, 4, 3, 2):
        loss = 1.0 - lam * (1.0 / order) * loss
    loss = lam * loss
    q00 = rho * lower
    q01 = 2.0 * rho * lam * lam * fall
    q11 = rho * (lower + twice * fall)
    slope = decay * lam
    tilt = loss + slope
    g0 = q00 * tilt * tilt + 2.0 * slope * q01 * tilt + slope * slope * q11
    g1 = slope * q01 - decay * (1.0 - lam) * q00
    loss2 = loss * loss
    c2 = decay * decay
    u = (2.0 * decay * loss2 - g1) / c2
    v = (loss2 * loss2 + g0) / c2
    root = jnp.sqrt(v * (v + 4.0 * u + 16.0))
    product = 4.0 * v / (v + root + jnp.sqrt(2.0 * v * (v + 2.0 * u + root)))
    total = 0.5 * (jnp.sqrt(u * u + 4.0 * u - 2.0 * v + 2.0 * root) - u)
    gain0 = total - 2.0 * loss
    gain1 = (product - loss2 - gain0 * tilt) / slope
    inverse = (1.0 - total + product) / c2
    inn = c2 / (1.0 - total + product)
    closed = (1.0 + slope - loss - gain0, slope, -slope - gain1, decay * (1.0 - lam))
    p00 = inn * ((1.0 - lam) * gain0 - lam * gain1) / decay
    p01 = inn * (lam * gain0 + (1.0 + lam) * gain1) / decay
    p11 = (
        p01 * (loss * (1.0 + decay) + 2.0 * slope * slope)
        + slope * decay * (1.0 + lam) * p00
        - q01
        + gain0 * gain1 * inn
    ) / (slope * decay * (1.0 - lam))
    return closed, gain0, gain1, inverse, (rho - p00, -p01, rho - p11)


def coefficients_kernel(blocks, noise_ref, *refs):
    arguments, (const_ref, w_ref, merge_ref, basis_ref, obs_ref) = refs[:4], refs[4:9]
    scale_ref, length_ref, sems = refs[9:]
    targets = (scale_ref, length_ref, obs_ref, basis_ref)
    copies = [
        pltpu.make_async_copy(source, target, sems.at[k])
        for k, (source, target) in enumerate(zip(arguments, targets))
    ]
    for copy in copies:
        copy.start()
    for copy in copies[:2]:
        copy.wait()
    steps = w_ref.shape[1]
    width = scale_ref.shape[1]
    tile = (SUB, width)
    scale2 = jnp.broadcast_to(scale_ref[...], tile)
    length = jnp.broadcast_to(length_ref[...], tile)
    noise_var = jnp.full(tile, noise_ref[0], F32)
    closed, gain0, gain1, inverse, excess = steady_state(scale2, length, noise_var)
    zero = jnp.zeros(tile, F32)

    squares, grams = [closed], [(inverse, zero, zero)]
    doublings = (steps * blocks).bit_length() - 1
    for _ in range(doublings):
        base = squares[-1]
        grams.append(mat_add(grams[-1], congruence(grams[-1], base)))
        squares.append(mat_mul(base, base))
    local = steps.bit_length() - 1
    consts = closed + (gain0, gain1, inverse) + squares[3] + squares[4] + squares[5]
    for place, value in enumerate(consts):
        const_ref[place] = value
    const_ref[len(consts)] = -1.0 / noise_var
    rounds = blocks.bit_length() - 1
    groups = squares[local:-1] + [()], grams[local:], [()] * rounds + [excess]
    values = [value for group in zip(*groups) for part in group for value in part]
    for place, value in enumerate(values):
        merge_ref[place : place + 1, :] = value[0:1, :]

    row = lax.broadcasted_iota(jnp.int32, tile, 0)
    small, gram_small = squares[:3], grams[:3]
    behind = power(small, 7 - row, zero)
    gram = gramian(small, gram_small, 7 - row, zero)
    eight, gram_eight = squares[3], grams[3]
    parts = steps // SUB
    for part in range(parts - 1, -1, -1):
        rows = pl.ds(part * SUB, SUB)
        w_ref[0, rows, :] = behind[0] * gain0 + behind[1] * gain1
        w_ref[1, rows, :] = behind[2] * gain0 + behind[3] * gain1
        k0 = gain0 * gram[0] + gain1 * gram[1]
        k1 = gain0 * gram[1] + gain1 * gram[2]
        w_ref[2, rows, :] = inverse - (k0 * closed[0] + k1 * closed[2])
        w_ref[3, rows, :] = -(k0 * closed[1] + k1 * closed[3])
        if part:
            behind = mat_mul(behind, eight)
            gram = mat_add(gram_eight, congruence(gram, eight))
    ahead = power(small, row, zero)
    for part in range(parts):
        rows = pl.ds(part * SUB, SUB)
        u0, u1 = w_ref[2, rows, :], w_ref[3, rows, :]
        w_ref[2, rows, :] = u0 * ahead[0] + u1 * ahead[2]
        w_ref[3, rows, :] = u0 * ahead[1] + u1 * ahead[3]
        if part < parts - 1:
            ahead = mat_mul(ahead, eight)

    for copy in copies[2:]:
        copy.wait()


def rotate_kernel(first, place_ref, *refs):
    pieces, stage = first
    obs_refs, (basis_ref, *refs) = refs[: len(pieces)], refs[len(pieces) :]
    depth = obs_refs[0].shape[1]
    z = refs[0][...] if stage else None
    for piece, obs_ref in zip(pieces, obs_refs):
        begin = pl.multiple_of((place_ref[0] ^ piece) * depth, depth)
        term = jnp.dot(
            obs_ref[...], basis_ref[pl.ds(begin, depth), :], preferred_element_type=F32
        )
        z = term if z is None else z + term
    if stage < 2:
        refs[-1][...] = z
        return
    _, w_ref, z_ref, sum_ref = refs
    z_ref[...] = z
    for line in range(4):
        sum_ref[line : line + 1, :] = jnp.sum(w_ref[line] * z, axis=0, keepdims=True)


def merge(level, me, own, other, merge_ref):
    lower = jnp.full(own.shape, (me >> level) & 1, jnp.int32) == 0
    left, right = jnp.where(lower, own, other), jnp.where(lower, other, own)
    f00, f01, f10, f11, s00, s01, s11 = (
        merge_ref[7 * level + k : 7 * level + k + 1, :] for k in range(7)
    )
    b0, b1 = left[0:1, :], left[1:2, :]
    a0 = right[2:3, :] - s00 * b0 - s01 * b1
    a1 = right[3:4, :] - s01 * b0 - s11 * b1
    return jnp.concatenate(
        (
            right[0:1, :] + f00 * b0 + f01 * b1,
            right[1:2, :] + f10 * b0 + f11 * b1,
            left[2:3, :] + f00 * a0 + f10 * a1,
            left[3:4, :] + f01 * a0 + f11 * a1,
        ),
        axis=0,
    )


def pair_kernel(own_ref, other_ref, out_ref):
    out_ref[0:4, :] = own_ref[...]
    out_ref[4:8, :] = other_ref[...]


def merge_kernel(level, me_ref, merge_ref, *refs):
    *refs, out_ref = refs
    me = me_ref[0]
    if level > 2:
        out_ref[...] = merge(level, me, refs[0][...], refs[1][...], merge_ref)
        return
    parts = {}
    for place, step in enumerate(GROUP):
        parts[step] = refs[place // 2][4 * (place % 2) : 4 * (place % 2) + 4, :]
    for level, stride in enumerate((1, 2, 4)):
        parts = {
            step: merge(level, me ^ step, parts[step], parts[step ^ stride], merge_ref)
            for step in range(0, 8, 2 * stride)
        }
    out_ref[...] = parts[0]


def shift(value, by):
    rows = value.shape[0]
    row = lax.broadcasted_iota(jnp.int32, value.shape, 0)
    keep = row >= by if by > 0 else row < rows + by
    return jnp.where(keep, pltpu.roll(value, by % rows, 0), 0.0)


def reach(blocks, me, merge_ref, g_ref):
    tile = (SUB, merge_ref.shape[1])
    rounds = blocks.bit_length() - 1
    values = [
        jnp.broadcast_to(merge_ref[k : k + 1, :], tile) for k in range(7 * rounds + 6)
    ]
    block_squares = [tuple(values[7 * k : 7 * k + 4]) for k in range(rounds)]
    block_grams = [tuple(values[7 * k + 4 : 7 * k + 7]) for k in range(rounds)]
    s, excess = values[-6:-3], values[-3:]
    zero = jnp.zeros(tile, F32)
    row = lax.broadcasted_iota(jnp.int32, tile, 0)
    left = (
        1.0 + excess[0] * s[0] + excess[1] * s[1],
        excess[0] * s[1] + excess[1] * s[2],
        excess[1] * s[0] + excess[2] * s[1],
        1.0 + excess[1] * s[1] + excess[2] * s[2],
    )
    determ = 1.0 / (left[0] * left[3] - left[1] * left[2])
    start = mat_mul((left[3], -left[1], -left[2], left[0]), full(excess))
    start = tuple(x * determ for x in start)
    mine = jnp.full(tile, me, jnp.int32)
    to_me = power(block_squares, mine, zero)
    rest = full(gramian(block_squares, block_grams, blocks - 1 - mine, zero))
    to_state = mat_mul(to_me, start)
    to_adjoint = mat_mul(mat_mul(rest, mat_mul(to_me, block_squares[0])), start)
    for group in range(g_ref.shape[1] // SUB):
        rows = row + group * SUB
        kind = rows & 3
        line = rows >> 2
        step = jnp.zeros_like(line)
        for place, offset in enumerate(GROUP):
            step = jnp.where(line == place, offset, step)
        span = jnp.where(line < 8, 1, jnp.left_shift(1, jnp.maximum(line - 5, 0)))
        near_me = mine ^ jnp.where(line < 8, step, span)
        front = jnp.minimum((near_me // span) * span, blocks - 1)
        back = jnp.minimum(front + span - 1, blocks - 1)
        before, after = back < me, front > me
        gap = jnp.where(before, me - 1 - back, jnp.where(after, front - 1 - me, 0))
        reach = jnp.where(before, me - back, jnp.where(after, back - me, 0))
        near = power(block_squares, gap, zero)
        far = power(block_squares, reach, zero)
        origin = mat_trans(power(block_squares, front, zero))
        left_over = full(gramian(block_squares, block_grams, blocks - 1 - back, zero))
        end = mat_trans(mat_mul(power(block_squares, back, zero), block_squares[0]))
        first = mat_mul(end, left_over)
        state_b = mat_sub(mat_pick(before, near, (zero,) * 4), mat_mul(to_state, first))
        state_l = mat_mul(to_state, origin)
        cross = mat_pick(after, mat_mul(mat_trans(far), left_over), mat_mul(rest, far))
        adjoint_b = mat_sub(mat_mul(to_adjoint, first), cross)
        adjoint_l = mat_sub(
            mat_pick(after, mat_trans(near), (zero,) * 4), mat_mul(to_adjoint, origin)
        )
        place = pl.ds(group * SUB, SUB)
        for output, (from_b, from_l) in enumerate(
            ((adjoint_b[:2], adjoint_l[:2]), (adjoint_b[2:], adjoint_l[2:]),
             (state_b[:2], state_l[:2]), (state_b[2:], state_l[2:]))
        ):
            g_ref[output, place, :] = jnp.where(
                kind < 2,
                jnp.where(kind == 0, from_b[0], from_b[1]),
                jnp.where(kind == 2, from_l[0], from_l[1]),
            )


def local_kernel(blocks, me_ref, z_ref, const_ref, merge_ref, r_ref, g_ref, scratch):
    reach(blocks, me_ref[0], merge_ref, g_ref)
    steps, width = z_ref.shape
    span = steps // SUB
    lanes = 128
    for chunk in range(width // lanes):
        cols = pl.ds(chunk * lanes, lanes)
        scratch[chunk] = z_ref[:, cols]
    for chunk in range(width // lanes):
        cols = pl.ds(chunk * lanes, lanes)
        const = [const_ref[k, :, cols] for k in range(19)]
        f, (k0, k1, inverse) = const[0:4], const[4:7]
        jumps = (const[7:11], const[11:15], const[15:19])
        zero = jnp.zeros((SUB, lanes), F32)
        x0, x1 = zero, zero
        vs = []
        for t in range(span):
            z = scratch[chunk, pl.ds(t, SUB, stride=span), :]
            vs.append(z - x0)
            x0, x1 = f[0] * x0 + f[1] * x1 + k0 * z, f[2] * x0 + f[3] * x1 + k1 * z
        for level, jump in enumerate(jumps):
            s0, s1 = shift(x0, 1 << level), shift(x1, 1 << level)
            x0, x1 = x0 + jump[0] * s0 + jump[1] * s1, x1 + jump[2] * s0 + jump[3] * s1
        x0, x1 = shift(x0, 1), shift(x1, 1)
        for t in range(span):
            vs[t] = (vs[t] - x0) * inverse
            x0, x1 = f[0] * x0 + f[1] * x1, f[2] * x0 + f[3] * x1
        a0, a1 = zero, zero
        for t in range(span - 1, -1, -1):
            a0, a1 = f[0] * a0 + f[2] * a1 + vs[t], f[1] * a0 + f[3] * a1
        for level, jump in enumerate(jumps):
            s0, s1 = shift(a0, -(1 << level)), shift(a1, -(1 << level))
            a0, a1 = a0 + jump[0] * s0 + jump[2] * s1, a1 + jump[1] * s0 + jump[3] * s1
        a0, a1 = shift(a0, -1), shift(a1, -1)
        for t in range(span - 1, -1, -1):
            r = vs[t] - k0 * a0 - k1 * a1
            a0, a1 = f[0] * a0 + f[2] * a1 + vs[t], f[1] * a0 + f[3] * a1
            scratch[chunk, pl.ds(t, SUB, stride=span), :] = r
        r_ref[:, cols] = scratch[chunk]


def rotate_back(residual, pieces, place_ref, basis_ref, outs):
    depth = outs[0].shape[1]
    for piece, out_ref in zip(pieces, outs):
        begin = pl.multiple_of((place_ref[0] ^ piece) * depth, depth)
        out_ref[...] = lax.dot_general(
            residual,
            basis_ref[pl.ds(begin, depth), :],
            (((1,), (1,)), ((), ())),
            preferred_element_type=F32,
        ).astype(out_ref.dtype)


def finish_kernel(pieces, place_ref, r_ref, w_ref, g_ref, const_ref, basis_ref, *refs):
    *sums, residual_ref = refs[: -len(pieces)]
    value = r_ref[...]
    for line in range(4):
        total, place = 0.0, 0
        for sum_ref in sums:
            count = sum_ref.shape[0]
            term = g_ref[line, pl.ds(place, count), :] * sum_ref[...]
            total = total + jnp.sum(term, axis=0, keepdims=True) if count < SUB else total + term
            place += count
            if place == 4 * len(GROUP):
                total = jnp.sum(total, axis=0, keepdims=True)
        value = value - w_ref[line] * total
    scale = const_ref[19, 0:1, :]
    residual = (value * scale).astype(jnp.bfloat16)
    residual_ref[...] = residual
    rotate_back(residual, pieces, place_ref, basis_ref, refs[-len(pieces) :])


def rest_kernel(pieces, place_ref, residual_ref, basis_ref, *outs):
    rotate_back(residual_ref[...], pieces, place_ref, basis_ref, outs)


def exchange(value, axis, count):
    out = [value]
    for step in range(1, count):
        out.append(lax.ppermute(value, axis, [(a, a ^ step) for a in range(count)]))
    return out


def shards(observations, basis, eigvals, lengths, noise):
    steps, depth = observations.shape
    width = basis.shape[1]
    blocks, pieces = lax.axis_size("tm"), lax.axis_size("mode")
    me = lax.axis_index("tm").astype(jnp.int32).reshape(1)
    place = lax.axis_index("mode").astype(jnp.int32).reshape(1)
    rounds = blocks.bit_length() - 1
    vmem = pl.BlockSpec(memory_space=pltpu.VMEM)
    smem = pl.BlockSpec(memory_space=pltpu.SMEM)
    params = pltpu.CompilerParams(vmem_limit_bytes=VMEM_LIMIT)

    def shape(*dims, dtype=F32):
        return jax.ShapeDtypeStruct(dims, dtype)

    obs = exchange(observations, "mode", pieces)
    const, w, merges, basis, obs[0] = pl.pallas_call(
        functools.partial(coefficients_kernel, blocks),
        out_shape=(
            shape(20, SUB, width),
            shape(4, steps, width),
            shape(-(-(7 * rounds + 6) // SUB) * SUB, width),
            shape(*basis.shape, dtype=basis.dtype),
            shape(steps, depth, dtype=observations.dtype),
        ),
        in_specs=[smem] + [pl.BlockSpec(memory_space=pltpu.HBM)] * 4,
        out_specs=(vmem,) * 5,
        scratch_shapes=[
            pltpu.VMEM((1, width), F32),
            pltpu.VMEM((1, width), F32),
            pltpu.SemaphoreType.DMA((4,)),
        ],
        compiler_params=params,
        cost_estimate=pl.CostEstimate(flops=20000000, bytes_accessed=2000000, transcendentals=0),
        name="coefficients",
    )(
        noise,
        *(
            pltpu.with_memory_space_constraint(x, pltpu.HBM)
            for x in (
                eigvals.reshape(1, width),
                lengths.reshape(1, width),
                observations,
                basis,
            )
        ),
    )
    last = [2, 1]
    z = ()
    for stage, group in enumerate(([0], [3])):
        z = pl.pallas_call(
            functools.partial(rotate_kernel, (group, stage)),
            out_shape=shape(steps, width),
            in_specs=[smem] + [vmem] * (len(group) + 1 + len(z)),
            out_specs=vmem,
            compiler_params=params,
            name="rotate_early",
        )(place, *(obs[piece] for piece in group), basis, *z)
        z = (z,)
    z, summary = pl.pallas_call(
        functools.partial(rotate_kernel, (last, 2)),
        out_shape=(shape(steps, width), shape(4, width)),
        in_specs=[smem] + [vmem] * (3 + len(last)),
        out_specs=(vmem,) * 2,
        compiler_params=params,
        name="rotate_last",
    )(place, *(obs[piece] for piece in last), basis, *z, w)
    pair = pl.pallas_call(
        pair_kernel,
        out_shape=shape(8, width),
        in_specs=[vmem] * 2,
        out_specs=vmem,
        compiler_params=params,
        name="pair",
    )(summary, lax.ppermute(summary, "tm", [(a, a ^ MIRROR) for a in range(blocks)]))
    sums = [pair]
    for step in NEAR:
        sums.append(lax.ppermute(pair, "tm", [(a, a ^ step) for a in range(blocks)]))
    for level in range(3, rounds):
        summary = pl.pallas_call(
            functools.partial(merge_kernel, level - 1),
            out_shape=shape(4, width),
            in_specs=[smem] + [vmem] * (5 if level == 3 else 3),
            out_specs=vmem,
            compiler_params=params,
            name="merge",
        )(me, merges, *(sums if level == 3 else (summary, sums[-1])))
        step = 1 << level
        sums.append(lax.ppermute(summary, "tm", [(a, a ^ step) for a in range(blocks)]))
    local, g = pl.pallas_call(
        functools.partial(local_kernel, blocks),
        out_shape=(shape(steps, width), shape(4, -(-4 * (rounds + 5) // SUB) * SUB, width)),
        in_specs=[smem] + [vmem] * 3,
        out_specs=(vmem,) * 2,
        scratch_shapes=[pltpu.VMEM((width // 128, steps, 128), F32)],
        compiler_params=params,
        cost_estimate=pl.CostEstimate(flops=10000000, bytes_accessed=1000000, transcendentals=0),
        name="local",
    )(me, z, const, merges)
    residual, part_y, part_d = pl.pallas_call(
        functools.partial(finish_kernel, [2, 3]),
        out_shape=(shape(steps, width, dtype=jnp.bfloat16),)
        + (shape(steps, depth, dtype=jnp.bfloat16),) * 2,
        in_specs=[smem] + [vmem] * (5 + len(sums)),
        out_specs=(vmem,) * 3,
        compiler_params=params,
        name="finish",
    )(place, local, w, g, const, basis, *sums)
    from_y, from_d = (
        lax.ppermute(part, "mode", [(a, a ^ piece) for a in range(pieces)])
        for piece, part in ((2, part_y), (3, part_d))
    )
    own, part_m = pl.pallas_call(
        functools.partial(rest_kernel, [0, 1]),
        out_shape=(shape(steps, depth), shape(steps, depth, dtype=jnp.bfloat16)),
        in_specs=[smem] + [vmem] * 2,
        out_specs=(vmem,) * 2,
        compiler_params=params,
        name="rest",
    )(place, residual, basis)
    from_m = lax.ppermute(part_m, "mode", [(a, a ^ 1) for a in range(pieces)])
    own, from_y, from_d, from_m = (v.astype(F32) for v in (own, from_y, from_d, from_m))
    return (own + from_m) + (from_d + from_y)


def solution(mesh):
    placed = (P("tm", "mode"), P(None, "mode"), P("mode"), P("mode"), P())
    return jax.shard_map(
        shards, mesh=mesh, in_specs=placed, out_specs=P("tm", "mode"), check_vma=False
    )
```

```python
import functools
import math

import jax
import jax.numpy as jnp
from jax import lax
from jax.experimental import pallas as pl
from jax.experimental.pallas import tpu as pltpu
from jax.sharding import PartitionSpec as P

F32 = jnp.float32
SUB = 8
MIRROR, NEAR = 6, (2, 1, 3)
GROUP = (0, MIRROR) + tuple(step ^ other for step in NEAR for other in (0, MIRROR))
VMEM_LIMIT = 24 * 1024 * 1024


def mat_mul(p, q):
    return (
        p[0] * q[0] + p[1] * q[2],
        p[0] * q[1] + p[1] * q[3],
        p[2] * q[0] + p[3] * q[2],
        p[2] * q[1] + p[3] * q[3],
    )


def mat_trans(p):
    return (p[0], p[2], p[1], p[3])


def mat_add(p, q):
    return tuple(a + b for a, b in zip(p, q))


def mat_sub(p, q):
    return tuple(a - b for a, b in zip(p, q))


def mat_pick(flag, p, q):
    return tuple(jnp.where(flag, a, b) for a, b in zip(p, q))


def full(s):
    return (s[0], s[1], s[1], s[2])


def congruence(s, f):
    t = (
        s[0] * f[0] + s[1] * f[2],
        s[0] * f[1] + s[1] * f[3],
        s[1] * f[0] + s[2] * f[2],
        s[1] * f[1] + s[2] * f[3],
    )
    return (f[0] * t[0] + f[2] * t[2], f[0] * t[1] + f[2] * t[3], f[1] * t[1] + f[3] * t[3])


def power(squares, exponent, like):
    one, zero = jnp.ones_like(like), jnp.zeros_like(like)
    out = None
    for bit, base in enumerate(squares):
        flag = (exponent & (1 << bit)) != 0
        if out is None:
            out = mat_pick(flag, base, (one, zero, zero, one))
        else:
            out = mat_pick(flag, mat_mul(out, base), out)
    return out


def gramian(squares, grams, count, like):
    zero = jnp.zeros_like(like)
    out = (zero, zero, zero)
    for bit, (base, gram) in enumerate(zip(squares, grams)):
        flag = (count & (1 << bit)) != 0
        out = mat_pick(flag, mat_add(gram, congruence(out, base)), out)
    return out


def steady_state(scale2, length, noise_var):
    lam = math.sqrt(3.0) / length
    decay = jnp.exp(-lam)
    twice = 2.0 * lam
    fall = jnp.exp(-twice)
    rho = scale2 / noise_var
    series = 1.0 / 604800.0
    for factor in (60480.0, 6720.0, 840.0, 120.0, 20.0, 4.0, 1.0):
        series = series * twice + 1.0 / factor
    lower = fall * twice * twice * twice * (1.0 / 6.0) * series
    loss = 1.0
    for order in (8, 7, 6, 5, 4, 3, 2):
        loss = 1.0 - lam * (1.0 / order) * loss
    loss = lam * loss
    q00 = rho * lower
    q01 = 2.0 * rho * lam * lam * fall
    q11 = rho * (lower + twice * fall)
    slope = decay * lam
    tilt = loss + slope
    g0 = q00 * tilt * tilt + 2.0 * slope * q01 * tilt + slope * slope * q11
    g1 = slope * q01 - decay * (1.0 - lam) * q00
    loss2 = loss * loss
    c2 = decay * decay
    u = (2.0 * decay * loss2 - g1) / c2
    v = (loss2 * loss2 + g0) / c2
    root = jnp.sqrt(v * (v + 4.0 * u + 16.0))
    product = 4.0 * v / (v + root + jnp.sqrt(2.0 * v * (v + 2.0 * u + root)))
    total = 0.5 * (jnp.sqrt(u * u + 4.0 * u - 2.0 * v + 2.0 * root) - u)
    gain0 = total - 2.0 * loss
    gain1 = (product - loss2 - gain0 * tilt) / slope
    inverse = (1.0 - total + product) / c2
    inn = c2 / (1.0 - total + product)
    closed = (1.0 + slope - loss - gain0, slope, -slope - gain1, decay * (1.0 - lam))
    p00 = inn * ((1.0 - lam) * gain0 - lam * gain1) / decay
    p01 = inn * (lam * gain0 + (1.0 + lam) * gain1) / decay
    p11 = (
        p01 * (loss * (1.0 + decay) + 2.0 * slope * slope)
        + slope * decay * (1.0 + lam) * p00
        - q01
        + gain0 * gain1 * inn
    ) / (slope * decay * (1.0 - lam))
    return closed, gain0, gain1, inverse, (rho - p00, -p01, rho - p11)


def coefficients_kernel(blocks, noise_ref, *refs):
    arguments, (const_ref, w_ref, merge_ref, basis_ref, obs_ref) = refs[:4], refs[4:9]
    scale_ref, length_ref, sems = refs[9:]
    targets = (scale_ref, length_ref, obs_ref, basis_ref)
    copies = [
        pltpu.make_async_copy(source, target, sems.at[k])
        for k, (source, target) in enumerate(zip(arguments, targets))
    ]
    for copy in copies:
        copy.start()
    for copy in copies[:2]:
        copy.wait()
    steps = w_ref.shape[1]
    width = scale_ref.shape[1]
    tile = (SUB, width)
    scale2 = jnp.broadcast_to(scale_ref[...], tile)
    length = jnp.broadcast_to(length_ref[...], tile)
    noise_var = jnp.full(tile, noise_ref[0], F32)
    closed, gain0, gain1, inverse, excess = steady_state(scale2, length, noise_var)
    zero = jnp.zeros(tile, F32)

    squares, grams = [closed], [(inverse, zero, zero)]
    doublings = (steps * blocks).bit_length() - 1
    for _ in range(doublings):
        base = squares[-1]
        grams.append(mat_add(grams[-1], congruence(grams[-1], base)))
        squares.append(mat_mul(base, base))
    local = steps.bit_length() - 1
    consts = closed + (gain0, gain1, inverse) + squares[3] + squares[4] + squares[5]
    for place, value in enumerate(consts):
        const_ref[place] = value
    const_ref[len(consts)] = -1.0 / noise_var
    rounds = blocks.bit_length() - 1
    groups = squares[local:-1] + [()], grams[local:], [()] * rounds + [excess]
    values = [value for group in zip(*groups) for part in group for value in part]
    for place, value in enumerate(values):
        merge_ref[place : place + 1, :] = value[0:1, :]

    row = lax.broadcasted_iota(jnp.int32, tile, 0)
    small, gram_small = squares[:3], grams[:3]
    behind = power(small, 7 - row, zero)
    gram = gramian(small, gram_small, 7 - row, zero)
    eight, gram_eight = squares[3], grams[3]
    parts = steps // SUB
    for part in range(parts - 1, -1, -1):
        rows = pl.ds(part * SUB, SUB)
        w_ref[0, rows, :] = behind[0] * gain0 + behind[1] * gain1
        w_ref[1, rows, :] = behind[2] * gain0 + behind[3] * gain1
        k0 = gain0 * gram[0] + gain1 * gram[1]
        k1 = gain0 * gram[1] + gain1 * gram[2]
        w_ref[2, rows, :] = inverse - (k0 * closed[0] + k1 * closed[2])
        w_ref[3, rows, :] = -(k0 * closed[1] + k1 * closed[3])
        if part:
            behind = mat_mul(behind, eight)
            gram = mat_add(gram_eight, congruence(gram, eight))
    ahead = power(small, row, zero)
    for part in range(parts):
        rows = pl.ds(part * SUB, SUB)
        u0, u1 = w_ref[2, rows, :], w_ref[3, rows, :]
        w_ref[2, rows, :] = u0 * ahead[0] + u1 * ahead[2]
        w_ref[3, rows, :] = u0 * ahead[1] + u1 * ahead[3]
        if part < parts - 1:
            ahead = mat_mul(ahead, eight)

    for copy in copies[2:]:
        copy.wait()


def rotate_kernel(first, place_ref, *refs):
    pieces, stage = first
    obs_refs, (basis_ref, *refs) = refs[: len(pieces)], refs[len(pieces) :]
    depth = obs_refs[0].shape[1]
    z = refs[0][...] if stage else None
    for piece, obs_ref in zip(pieces, obs_refs):
        begin = pl.multiple_of((place_ref[0] ^ piece) * depth, depth)
        term = jnp.dot(
            obs_ref[...], basis_ref[pl.ds(begin, depth), :], preferred_element_type=F32
        )
        z = term if z is None else z + term
    if stage < 2:
        refs[-1][...] = z
        return
    _, w_ref, z_ref, sum_ref = refs
    z_ref[...] = z
    for line in range(4):
        sum_ref[line : line + 1, :] = jnp.sum(w_ref[line] * z, axis=0, keepdims=True)


def merge(level, me, own, other, merge_ref):
    lower = jnp.full(own.shape, (me >> level) & 1, jnp.int32) == 0
    left, right = jnp.where(lower, own, other), jnp.where(lower, other, own)
    f00, f01, f10, f11, s00, s01, s11 = (
        merge_ref[7 * level + k : 7 * level + k + 1, :] for k in range(7)
    )
    b0, b1 = left[0:1, :], left[1:2, :]
    a0 = right[2:3, :] - s00 * b0 - s01 * b1
    a1 = right[3:4, :] - s01 * b0 - s11 * b1
    return jnp.concatenate(
        (
            right[0:1, :] + f00 * b0 + f01 * b1,
            right[1:2, :] + f10 * b0 + f11 * b1,
            left[2:3, :] + f00 * a0 + f10 * a1,
            left[3:4, :] + f01 * a0 + f11 * a1,
        ),
        axis=0,
    )


def pair_kernel(_, own_ref, other_ref, out_ref):
    out_ref[0:4, :] = own_ref[...]
    out_ref[4:8, :] = other_ref[...]


def merge_kernel(level, me_ref, merge_ref, *refs):
    *refs, out_ref = refs
    me = me_ref[0]
    if level > 2:
        out_ref[...] = merge(level, me, refs[0][...], refs[1][...], merge_ref)
        return
    parts = {}
    for place, step in enumerate(GROUP):
        parts[step] = refs[place // 2][4 * (place % 2) : 4 * (place % 2) + 4, :]
    for level, stride in enumerate((1, 2, 4)):
        parts = {
            step: merge(level, me ^ step, parts[step], parts[step ^ stride], merge_ref)
            for step in range(0, 8, 2 * stride)
        }
    out_ref[...] = parts[0]


def shift(value, by):
    rows = value.shape[0]
    row = lax.broadcasted_iota(jnp.int32, value.shape, 0)
    keep = row >= by if by > 0 else row < rows + by
    return jnp.where(keep, pltpu.roll(value, by % rows, 0), 0.0)


def reach(blocks, me, merge_ref, g_ref):
    tile = (SUB, merge_ref.shape[1])
    rounds = blocks.bit_length() - 1
    values = [
        jnp.broadcast_to(merge_ref[k : k + 1, :], tile) for k in range(7 * rounds + 6)
    ]
    block_squares = [tuple(values[7 * k : 7 * k + 4]) for k in range(rounds)]
    block_grams = [tuple(values[7 * k + 4 : 7 * k + 7]) for k in range(rounds)]
    s, excess = values[-6:-3], values[-3:]
    zero = jnp.zeros(tile, F32)
    row = lax.broadcasted_iota(jnp.int32, tile, 0)
    left = (
        1.0 + excess[0] * s[0] + excess[1] * s[1],
        excess[0] * s[1] + excess[1] * s[2],
        excess[1] * s[0] + excess[2] * s[1],
        1.0 + excess[1] * s[1] + excess[2] * s[2],
    )
    determ = 1.0 / (left[0] * left[3] - left[1] * left[2])
    start = mat_mul((left[3], -left[1], -left[2], left[0]), full(excess))
    start = tuple(x * determ for x in start)
    mine = jnp.full(tile, me, jnp.int32)
    to_me = power(block_squares, mine, zero)
    rest = full(gramian(block_squares, block_grams, blocks - 1 - mine, zero))
    to_state = mat_mul(to_me, start)
    to_adjoint = mat_mul(mat_mul(rest, mat_mul(to_me, block_squares[0])), start)
    for group in range(g_ref.shape[1] // SUB):
        rows = row + group * SUB
        kind = rows & 3
        line = rows >> 2
        step = jnp.zeros_like(line)
        for place, offset in enumerate(GROUP):
            step = jnp.where(line == place, offset, step)
        span = jnp.where(line < 8, 1, jnp.left_shift(1, jnp.maximum(line - 5, 0)))
        near_me = mine ^ jnp.where(line < 8, step, span)
        front = jnp.minimum((near_me // span) * span, blocks - 1)
        back = jnp.minimum(front + span - 1, blocks - 1)
        before, after = back < me, front > me
        gap = jnp.where(before, me - 1 - back, jnp.where(after, front - 1 - me, 0))
        reach = jnp.where(before, me - back, jnp.where(after, back - me, 0))
        near = power(block_squares, gap, zero)
        far = power(block_squares, reach, zero)
        origin = mat_trans(power(block_squares, front, zero))
        left_over = full(gramian(block_squares, block_grams, blocks - 1 - back, zero))
        end = mat_trans(mat_mul(power(block_squares, back, zero), block_squares[0]))
        first = mat_mul(end, left_over)
        state_b = mat_sub(mat_pick(before, near, (zero,) * 4), mat_mul(to_state, first))
        state_l = mat_mul(to_state, origin)
        cross = mat_pick(after, mat_mul(mat_trans(far), left_over), mat_mul(rest, far))
        adjoint_b = mat_sub(mat_mul(to_adjoint, first), cross)
        adjoint_l = mat_sub(
            mat_pick(after, mat_trans(near), (zero,) * 4), mat_mul(to_adjoint, origin)
        )
        place = pl.ds(group * SUB, SUB)
        for output, (from_b, from_l) in enumerate(
            ((adjoint_b[:2], adjoint_l[:2]), (adjoint_b[2:], adjoint_l[2:]),
             (state_b[:2], state_l[:2]), (state_b[2:], state_l[2:]))
        ):
            g_ref[output, place, :] = jnp.where(
                kind < 2,
                jnp.where(kind == 0, from_b[0], from_b[1]),
                jnp.where(kind == 2, from_l[0], from_l[1]),
            )


def local_kernel(blocks, me_ref, z_ref, const_ref, merge_ref, r_ref, g_ref, scratch):
    reach(blocks, me_ref[0], merge_ref, g_ref)
    steps, width = z_ref.shape
    span = steps // SUB
    lanes = 128
    for chunk in range(width // lanes):
        cols = pl.ds(chunk * lanes, lanes)
        scratch[chunk] = z_ref[:, cols]
    for chunk in range(width // lanes):
        cols = pl.ds(chunk * lanes, lanes)
        const = [const_ref[k, :, cols] for k in range(19)]
        f, (k0, k1, inverse) = const[0:4], const[4:7]
        jumps = (const[7:11], const[11:15], const[15:19])
        zero = jnp.zeros((SUB, lanes), F32)
        x0, x1 = zero, zero
        vs = []
        for t in range(span):
            z = scratch[chunk, pl.ds(t, SUB, stride=span), :]
            vs.append(z - x0)
            x0, x1 = f[0] * x0 + f[1] * x1 + k0 * z, f[2] * x0 + f[3] * x1 + k1 * z
        for level, jump in enumerate(jumps):
            s0, s1 = shift(x0, 1 << level), shift(x1, 1 << level)
            x0, x1 = x0 + jump[0] * s0 + jump[1] * s1, x1 + jump[2] * s0 + jump[3] * s1
        x0, x1 = shift(x0, 1), shift(x1, 1)
        for t in range(span):
            vs[t] = (vs[t] - x0) * inverse
            x0, x1 = f[0] * x0 + f[1] * x1, f[2] * x0 + f[3] * x1
        a0, a1 = zero, zero
        for t in range(span - 1, -1, -1):
            a0, a1 = f[0] * a0 + f[2] * a1 + vs[t], f[1] * a0 + f[3] * a1
        for level, jump in enumerate(jumps):
            s0, s1 = shift(a0, -(1 << level)), shift(a1, -(1 << level))
            a0, a1 = a0 + jump[0] * s0 + jump[2] * s1, a1 + jump[1] * s0 + jump[3] * s1
        a0, a1 = shift(a0, -1), shift(a1, -1)
        for t in range(span - 1, -1, -1):
            r = vs[t] - k0 * a0 - k1 * a1
            a0, a1 = f[0] * a0 + f[2] * a1 + vs[t], f[1] * a0 + f[3] * a1
            scratch[chunk, pl.ds(t, SUB, stride=span), :] = r
        r_ref[:, cols] = scratch[chunk]


def rotate_back(residual, pieces, place_ref, basis_ref, outs):
    depth = outs[0].shape[1]
    for piece, out_ref in zip(pieces, outs):
        begin = pl.multiple_of((place_ref[0] ^ piece) * depth, depth)
        out_ref[...] = lax.dot_general(
            residual,
            basis_ref[pl.ds(begin, depth), :],
            (((1,), (1,)), ((), ())),
            preferred_element_type=F32,
        ).astype(out_ref.dtype)


def finish_kernel(pieces, place_ref, r_ref, w_ref, g_ref, const_ref, basis_ref, *refs):
    *sums, residual_ref = refs[: -len(pieces)]
    value = r_ref[...]
    for line in range(4):
        total, place = 0.0, 0
        for sum_ref in sums:
            count = sum_ref.shape[0]
            term = g_ref[line, pl.ds(place, count), :] * sum_ref[...]
            total = total + jnp.sum(term, axis=0, keepdims=True) if count < SUB else total + term
            place += count
            if place == 4 * len(GROUP):
                total = jnp.sum(total, axis=0, keepdims=True)
        value = value - w_ref[line] * total
    scale = const_ref[19, 0:1, :]
    residual = (value * scale).astype(jnp.bfloat16)
    residual_ref[...] = residual
    rotate_back(residual, pieces, place_ref, basis_ref, refs[-len(pieces) :])


def rest_kernel(pieces, place_ref, residual_ref, basis_ref, *outs):
    rotate_back(residual_ref[...], pieces, place_ref, basis_ref, outs)


def exchange(value, axis, count):
    out = [value]
    for step in range(1, count):
        out.append(lax.ppermute(value, axis, [(a, a ^ step) for a in range(count)]))
    return out


def shards(observations, basis, eigvals, lengths, noise):
    steps, depth = observations.shape
    width = basis.shape[1]
    blocks, pieces = lax.axis_size("tm"), lax.axis_size("mode")
    me = lax.axis_index("tm").astype(jnp.int32).reshape(1)
    place = lax.axis_index("mode").astype(jnp.int32).reshape(1)
    rounds = blocks.bit_length() - 1
    vmem = pl.BlockSpec(memory_space=pltpu.VMEM)
    smem = pl.BlockSpec(memory_space=pltpu.SMEM)
    params = pltpu.CompilerParams(vmem_limit_bytes=VMEM_LIMIT)

    def shape(*dims, dtype=F32):
        return jax.ShapeDtypeStruct(dims, dtype)

    obs = exchange(observations, "mode", pieces)
    const, w, merges, basis, obs[0] = pl.pallas_call(
        functools.partial(coefficients_kernel, blocks),
        out_shape=(
            shape(20, SUB, width),
            shape(4, steps, width),
            shape(-(-(7 * rounds + 6) // SUB) * SUB, width),
            shape(*basis.shape, dtype=basis.dtype),
            shape(steps, depth, dtype=observations.dtype),
        ),
        in_specs=[smem] + [pl.BlockSpec(memory_space=pltpu.HBM)] * 4,
        out_specs=(vmem,) * 5,
        scratch_shapes=[
            pltpu.VMEM((1, width), F32),
            pltpu.VMEM((1, width), F32),
            pltpu.SemaphoreType.DMA((4,)),
        ],
        compiler_params=params,
        cost_estimate=pl.CostEstimate(flops=20000000, bytes_accessed=2000000, transcendentals=0),
        name="coefficients",
    )(
        noise,
        *(
            pltpu.with_memory_space_constraint(x, pltpu.HBM)
            for x in (
                eigvals.reshape(1, width),
                lengths.reshape(1, width),
                observations,
                basis,
            )
        ),
    )
    last = pieces - 1
    z = ()
    for stage, group in enumerate(([0], list(range(1, last)))):
        z = pl.pallas_call(
            functools.partial(rotate_kernel, (group, stage)),
            out_shape=shape(steps, width),
            in_specs=[smem] + [vmem] * (len(group) + 1 + len(z)),
            out_specs=vmem,
            compiler_params=params,
            name="rotate_early",
        )(place, *(obs[piece] for piece in group), basis, *z)
        z = (z,)
    z, summary = pl.pallas_call(
        functools.partial(rotate_kernel, ([last], 2)),
        out_shape=(shape(steps, width), shape(4, width)),
        in_specs=[smem] + [vmem] * 4,
        out_specs=(vmem,) * 2,
        compiler_params=params,
        name="rotate_last",
    )(place, obs[last], basis, *z, w)
    local, g = pl.pallas_call(
        functools.partial(local_kernel, blocks),
        out_shape=(shape(steps, width), shape(4, -(-4 * (rounds + 5) // SUB) * SUB, width)),
        in_specs=[smem] + [vmem] * 3,
        out_specs=(vmem,) * 2,
        scratch_shapes=[pltpu.VMEM((width // 128, steps, 128), F32)],
        compiler_params=params,
        cost_estimate=pl.CostEstimate(flops=10000000, bytes_accessed=1000000, transcendentals=0),
        name="local",
    )(me, z, const, merges)
    pair = pl.pallas_call(
        pair_kernel,
        out_shape=shape(8, width),
        in_specs=[vmem] * 3,
        out_specs=vmem,
        compiler_params=params,
        name="pair",
    )(g, summary, lax.ppermute(summary, "tm", [(a, a ^ MIRROR) for a in range(blocks)]))
    sums = [pair]
    for step in NEAR:
        sums.append(lax.ppermute(pair, "tm", [(a, a ^ step) for a in range(blocks)]))
    for level in range(3, rounds):
        summary = pl.pallas_call(
            functools.partial(merge_kernel, level - 1),
            out_shape=shape(4, width),
            in_specs=[smem] + [vmem] * (5 if level == 3 else 3),
            out_specs=vmem,
            compiler_params=params,
            name="merge",
        )(me, merges, *(sums if level == 3 else (summary, sums[-1])))
        step = 1 << level
        sums.append(lax.ppermute(summary, "tm", [(a, a ^ step) for a in range(blocks)]))
    far = list(range(2, pieces)) + [1]
    near = [0]
    residual, *parts = pl.pallas_call(
        functools.partial(finish_kernel, far),
        out_shape=(shape(steps, width, dtype=jnp.bfloat16),)
        + (shape(steps, depth, dtype=jnp.bfloat16),) * len(far),
        in_specs=[smem] + [vmem] * (5 + len(sums)),
        out_specs=(vmem,) * (1 + len(far)),
        compiler_params=params,
        name="finish",
    )(place, local, w, g, const, basis, *sums)
    arrived = [
        lax.ppermute(part, "mode", [(a, a ^ piece) for a in range(pieces)])
        for piece, part in zip(far, parts)
    ]
    grad_obs = pl.pallas_call(
        functools.partial(rest_kernel, near),
        out_shape=shape(steps, depth),
        in_specs=[smem] + [vmem] * 2,
        out_specs=vmem,
        compiler_params=params,
        cost_estimate=pl.CostEstimate(flops=80000000, bytes_accessed=1500000, transcendentals=0),
        name="rest",
    )(place, residual, basis)
    for part in arrived:
        grad_obs = grad_obs + part.astype(F32)
    return grad_obs


def solution(mesh):
    placed = (P("tm", "mode"), P(None, "mode"), P("mode"), P("mode"), P())
    return jax.shard_map(
        shards, mesh=mesh, in_specs=placed, out_specs=P("tm", "mode"), check_vma=False
    )
```

```python
import functools
import math

import jax
import jax.numpy as jnp
from jax import lax
from jax.experimental import pallas as pl
from jax.experimental.pallas import tpu as pltpu
from jax.sharding import PartitionSpec as P

F32 = jnp.float32
SUB = 8
MIRROR, NEAR = 4, (3, 2, 1)
GROUP = (0, MIRROR) + tuple(step ^ other for step in NEAR for other in (0, MIRROR))
VMEM_LIMIT = 24 * 1024 * 1024


def mat_mul(p, q):
    return (
        p[0] * q[0] + p[1] * q[2],
        p[0] * q[1] + p[1] * q[3],
        p[2] * q[0] + p[3] * q[2],
        p[2] * q[1] + p[3] * q[3],
    )


def mat_trans(p):
    return (p[0], p[2], p[1], p[3])


def mat_add(p, q):
    return tuple(a + b for a, b in zip(p, q))


def mat_sub(p, q):
    return tuple(a - b for a, b in zip(p, q))


def mat_pick(flag, p, q):
    return tuple(jnp.where(flag, a, b) for a, b in zip(p, q))


def full(s):
    return (s[0], s[1], s[1], s[2])


def congruence(s, f):
    t = (
        s[0] * f[0] + s[1] * f[2],
        s[0] * f[1] + s[1] * f[3],
        s[1] * f[0] + s[2] * f[2],
        s[1] * f[1] + s[2] * f[3],
    )
    return (f[0] * t[0] + f[2] * t[2], f[0] * t[1] + f[2] * t[3], f[1] * t[1] + f[3] * t[3])


def power(squares, exponent, like):
    one, zero = jnp.ones_like(like), jnp.zeros_like(like)
    out = None
    for bit, base in enumerate(squares):
        flag = (exponent & (1 << bit)) != 0
        if out is None:
            out = mat_pick(flag, base, (one, zero, zero, one))
        else:
            out = mat_pick(flag, mat_mul(out, base), out)
    return out


def gramian(squares, grams, count, like):
    zero = jnp.zeros_like(like)
    out = (zero, zero, zero)
    for bit, (base, gram) in enumerate(zip(squares, grams)):
        flag = (count & (1 << bit)) != 0
        out = mat_pick(flag, mat_add(gram, congruence(out, base)), out)
    return out


def steady_state(scale2, length, noise_var):
    lam = math.sqrt(3.0) / length
    decay = jnp.exp(-lam)
    twice = 2.0 * lam
    fall = jnp.exp(-twice)
    rho = scale2 / noise_var
    series = 1.0 / 604800.0
    for factor in (60480.0, 6720.0, 840.0, 120.0, 20.0, 4.0, 1.0):
        series = series * twice + 1.0 / factor
    lower = fall * twice * twice * twice * (1.0 / 6.0) * series
    loss = 1.0
    for order in (8, 7, 6, 5, 4, 3, 2):
        loss = 1.0 - lam * (1.0 / order) * loss
    loss = lam * loss
    q00 = rho * lower
    q01 = 2.0 * rho * lam * lam * fall
    q11 = rho * (lower + twice * fall)
    slope = decay * lam
    tilt = loss + slope
    g0 = q00 * tilt * tilt + 2.0 * slope * q01 * tilt + slope * slope * q11
    g1 = slope * q01 - decay * (1.0 - lam) * q00
    loss2 = loss * loss
    c2 = decay * decay
    u = (2.0 * decay * loss2 - g1) / c2
    v = (loss2 * loss2 + g0) / c2
    root = jnp.sqrt(v * (v + 4.0 * u + 16.0))
    product = 4.0 * v / (v + root + jnp.sqrt(2.0 * v * (v + 2.0 * u + root)))
    total = 0.5 * (jnp.sqrt(u * u + 4.0 * u - 2.0 * v + 2.0 * root) - u)
    gain0 = total - 2.0 * loss
    gain1 = (product - loss2 - gain0 * tilt) / slope
    inverse = (1.0 - total + product) / c2
    inn = c2 / (1.0 - total + product)
    closed = (1.0 + slope - loss - gain0, slope, -slope - gain1, decay * (1.0 - lam))
    p00 = inn * ((1.0 - lam) * gain0 - lam * gain1) / decay
    p01 = inn * (lam * gain0 + (1.0 + lam) * gain1) / decay
    p11 = (
        p01 * (loss * (1.0 + decay) + 2.0 * slope * slope)
        + slope * decay * (1.0 + lam) * p00
        - q01
        + gain0 * gain1 * inn
    ) / (slope * decay * (1.0 - lam))
    return closed, gain0, gain1, inverse, (rho - p00, -p01, rho - p11)


def coefficients_kernel(blocks, noise_ref, *refs):
    arguments, (const_ref, w_ref, merge_ref, basis_ref, obs_ref) = refs[:4], refs[4:9]
    scale_ref, length_ref, sems = refs[9:]
    targets = (scale_ref, length_ref, obs_ref, basis_ref)
    copies = [
        pltpu.make_async_copy(source, target, sems.at[k])
        for k, (source, target) in enumerate(zip(arguments, targets))
    ]
    for copy in copies:
        copy.start()
    for copy in copies[:2]:
        copy.wait()
    steps = w_ref.shape[1]
    width = scale_ref.shape[1]
    tile = (SUB, width)
    scale2 = jnp.broadcast_to(scale_ref[...], tile)
    length = jnp.broadcast_to(length_ref[...], tile)
    noise_var = jnp.full(tile, noise_ref[0], F32)
    closed, gain0, gain1, inverse, excess = steady_state(scale2, length, noise_var)
    zero = jnp.zeros(tile, F32)

    squares, grams = [closed], [(inverse, zero, zero)]
    doublings = (steps * blocks).bit_length() - 1
    for _ in range(doublings):
        base = squares[-1]
        grams.append(mat_add(grams[-1], congruence(grams[-1], base)))
        squares.append(mat_mul(base, base))
    local = steps.bit_length() - 1
    consts = closed + (gain0, gain1, inverse) + squares[3] + squares[4] + squares[5]
    for place, value in enumerate(consts):
        const_ref[place] = value
    const_ref[len(consts)] = -1.0 / noise_var
    rounds = blocks.bit_length() - 1
    groups = squares[local:-1] + [()], grams[local:], [()] * rounds + [excess]
    values = [value for group in zip(*groups) for part in group for value in part]
    for place, value in enumerate(values):
        merge_ref[place : place + 1, :] = value[0:1, :]

    row = lax.broadcasted_iota(jnp.int32, tile, 0)
    small, gram_small = squares[:3], grams[:3]
    behind = power(small, 7 - row, zero)
    gram = gramian(small, gram_small, 7 - row, zero)
    eight, gram_eight = squares[3], grams[3]
    parts = steps // SUB
    for part in range(parts - 1, -1, -1):
        rows = pl.ds(part * SUB, SUB)
        w_ref[0, rows, :] = behind[0] * gain0 + behind[1] * gain1
        w_ref[1, rows, :] = behind[2] * gain0 + behind[3] * gain1
        k0 = gain0 * gram[0] + gain1 * gram[1]
        k1 = gain0 * gram[1] + gain1 * gram[2]
        w_ref[2, rows, :] = inverse - (k0 * closed[0] + k1 * closed[2])
        w_ref[3, rows, :] = -(k0 * closed[1] + k1 * closed[3])
        if part:
            behind = mat_mul(behind, eight)
            gram = mat_add(gram_eight, congruence(gram, eight))
    ahead = power(small, row, zero)
    for part in range(parts):
        rows = pl.ds(part * SUB, SUB)
        u0, u1 = w_ref[2, rows, :], w_ref[3, rows, :]
        w_ref[2, rows, :] = u0 * ahead[0] + u1 * ahead[2]
        w_ref[3, rows, :] = u0 * ahead[1] + u1 * ahead[3]
        if part < parts - 1:
            ahead = mat_mul(ahead, eight)

    for copy in copies[2:]:
        copy.wait()


def rotate_kernel(first, place_ref, *refs):
    pieces, stage = first
    obs_refs, (basis_ref, *refs) = refs[: len(pieces)], refs[len(pieces) :]
    depth = obs_refs[0].shape[1]
    z = refs[0][...] if stage else None
    for piece, obs_ref in zip(pieces, obs_refs):
        begin = pl.multiple_of((place_ref[0] ^ piece) * depth, depth)
        term = jnp.dot(
            obs_ref[...], basis_ref[pl.ds(begin, depth), :], preferred_element_type=F32
        )
        z = term if z is None else z + term
    if stage < 2:
        refs[-1][...] = z
        return
    _, w_ref, z_ref, sum_ref = refs
    z_ref[...] = z
    for line in range(4):
        sum_ref[line : line + 1, :] = jnp.sum(w_ref[line] * z, axis=0, keepdims=True)


def merge(level, me, own, other, merge_ref):
    lower = jnp.full(own.shape, (me >> level) & 1, jnp.int32) == 0
    left, right = jnp.where(lower, own, other), jnp.where(lower, other, own)
    f00, f01, f10, f11, s00, s01, s11 = (
        merge_ref[7 * level + k : 7 * level + k + 1, :] for k in range(7)
    )
    b0, b1 = left[0:1, :], left[1:2, :]
    a0 = right[2:3, :] - s00 * b0 - s01 * b1
    a1 = right[3:4, :] - s01 * b0 - s11 * b1
    return jnp.concatenate(
        (
            right[0:1, :] + f00 * b0 + f01 * b1,
            right[1:2, :] + f10 * b0 + f11 * b1,
            left[2:3, :] + f00 * a0 + f10 * a1,
            left[3:4, :] + f01 * a0 + f11 * a1,
        ),
        axis=0,
    )


def pair_kernel(own_ref, other_ref, out_ref):
    out_ref[0:4, :] = own_ref[...]
    out_ref[4:8, :] = other_ref[...]


def merge_kernel(level, me_ref, merge_ref, *refs):
    *refs, out_ref = refs
    me = me_ref[0]
    if level > 2:
        out_ref[...] = merge(level, me, refs[0][...], refs[1][...], merge_ref)
        return
    parts = {}
    for place, step in enumerate(GROUP):
        parts[step] = refs[place // 2][4 * (place % 2) : 4 * (place % 2) + 4, :]
    for level, stride in enumerate((1, 2, 4)):
        parts = {
            step: merge(level, me ^ step, parts[step], parts[step ^ stride], merge_ref)
            for step in range(0, 8, 2 * stride)
        }
    out_ref[...] = parts[0]


def shift(value, by):
    rows = value.shape[0]
    row = lax.broadcasted_iota(jnp.int32, value.shape, 0)
    keep = row >= by if by > 0 else row < rows + by
    return jnp.where(keep, pltpu.roll(value, by % rows, 0), 0.0)


def reach(blocks, me, merge_ref, g_ref):
    tile = (SUB, merge_ref.shape[1])
    rounds = blocks.bit_length() - 1
    values = [
        jnp.broadcast_to(merge_ref[k : k + 1, :], tile) for k in range(7 * rounds + 6)
    ]
    block_squares = [tuple(values[7 * k : 7 * k + 4]) for k in range(rounds)]
    block_grams = [tuple(values[7 * k + 4 : 7 * k + 7]) for k in range(rounds)]
    s, excess = values[-6:-3], values[-3:]
    zero = jnp.zeros(tile, F32)
    row = lax.broadcasted_iota(jnp.int32, tile, 0)
    left = (
        1.0 + excess[0] * s[0] + excess[1] * s[1],
        excess[0] * s[1] + excess[1] * s[2],
        excess[1] * s[0] + excess[2] * s[1],
        1.0 + excess[1] * s[1] + excess[2] * s[2],
    )
    determ = 1.0 / (left[0] * left[3] - left[1] * left[2])
    start = mat_mul((left[3], -left[1], -left[2], left[0]), full(excess))
    start = tuple(x * determ for x in start)
    mine = jnp.full(tile, me, jnp.int32)
    to_me = power(block_squares, mine, zero)
    rest = full(gramian(block_squares, block_grams, blocks - 1 - mine, zero))
    to_state = mat_mul(to_me, start)
    to_adjoint = mat_mul(mat_mul(rest, mat_mul(to_me, block_squares[0])), start)
    for group in range(g_ref.shape[1] // SUB):
        rows = row + group * SUB
        kind = rows & 3
        line = rows >> 2
        step = jnp.zeros_like(line)
        for place, offset in enumerate(GROUP):
            step = jnp.where(line == place, offset, step)
        span = jnp.where(line < 8, 1, jnp.left_shift(1, jnp.maximum(line - 5, 0)))
        near_me = mine ^ jnp.where(line < 8, step, span)
        front = jnp.minimum((near_me // span) * span, blocks - 1)
        back = jnp.minimum(front + span - 1, blocks - 1)
        before, after = back < me, front > me
        gap = jnp.where(before, me - 1 - back, jnp.where(after, front - 1 - me, 0))
        reach = jnp.where(before, me - back, jnp.where(after, back - me, 0))
        near = power(block_squares, gap, zero)
        far = power(block_squares, reach, zero)
        origin = mat_trans(power(block_squares, front, zero))
        left_over = full(gramian(block_squares, block_grams, blocks - 1 - back, zero))
        end = mat_trans(mat_mul(power(block_squares, back, zero), block_squares[0]))
        first = mat_mul(end, left_over)
        state_b = mat_sub(mat_pick(before, near, (zero,) * 4), mat_mul(to_state, first))
        state_l = mat_mul(to_state, origin)
        cross = mat_pick(after, mat_mul(mat_trans(far), left_over), mat_mul(rest, far))
        adjoint_b = mat_sub(mat_mul(to_adjoint, first), cross)
        adjoint_l = mat_sub(
            mat_pick(after, mat_trans(near), (zero,) * 4), mat_mul(to_adjoint, origin)
        )
        place = pl.ds(group * SUB, SUB)
        for output, (from_b, from_l) in enumerate(
            ((adjoint_b[:2], adjoint_l[:2]), (adjoint_b[2:], adjoint_l[2:]),
             (state_b[:2], state_l[:2]), (state_b[2:], state_l[2:]))
        ):
            g_ref[output, place, :] = jnp.where(
                kind < 2,
                jnp.where(kind == 0, from_b[0], from_b[1]),
                jnp.where(kind == 2, from_l[0], from_l[1]),
            )


def local_kernel(blocks, me_ref, z_ref, const_ref, merge_ref, r_ref, g_ref, scratch):
    reach(blocks, me_ref[0], merge_ref, g_ref)
    steps, width = z_ref.shape
    span = steps // SUB
    lanes = 128
    for chunk in range(width // lanes):
        cols = pl.ds(chunk * lanes, lanes)
        scratch[chunk] = z_ref[:, cols]
    for chunk in range(width // lanes):
        cols = pl.ds(chunk * lanes, lanes)
        const = [const_ref[k, :, cols] for k in range(19)]
        f, (k0, k1, inverse) = const[0:4], const[4:7]
        jumps = (const[7:11], const[11:15], const[15:19])
        zero = jnp.zeros((SUB, lanes), F32)
        x0, x1 = zero, zero
        vs = []
        for t in range(span):
            z = scratch[chunk, pl.ds(t, SUB, stride=span), :]
            vs.append(z - x0)
            x0, x1 = f[0] * x0 + f[1] * x1 + k0 * z, f[2] * x0 + f[3] * x1 + k1 * z
        for level, jump in enumerate(jumps):
            s0, s1 = shift(x0, 1 << level), shift(x1, 1 << level)
            x0, x1 = x0 + jump[0] * s0 + jump[1] * s1, x1 + jump[2] * s0 + jump[3] * s1
        x0, x1 = shift(x0, 1), shift(x1, 1)
        for t in range(span):
            vs[t] = (vs[t] - x0) * inverse
            x0, x1 = f[0] * x0 + f[1] * x1, f[2] * x0 + f[3] * x1
        a0, a1 = zero, zero
        for t in range(span - 1, -1, -1):
            a0, a1 = f[0] * a0 + f[2] * a1 + vs[t], f[1] * a0 + f[3] * a1
        for level, jump in enumerate(jumps):
            s0, s1 = shift(a0, -(1 << level)), shift(a1, -(1 << level))
            a0, a1 = a0 + jump[0] * s0 + jump[2] * s1, a1 + jump[1] * s0 + jump[3] * s1
        a0, a1 = shift(a0, -1), shift(a1, -1)
        for t in range(span - 1, -1, -1):
            r = vs[t] - k0 * a0 - k1 * a1
            a0, a1 = f[0] * a0 + f[2] * a1 + vs[t], f[1] * a0 + f[3] * a1
            scratch[chunk, pl.ds(t, SUB, stride=span), :] = r
        r_ref[:, cols] = scratch[chunk]


def rotate_back(residual, pieces, place_ref, basis_ref, outs):
    depth = outs[0].shape[1]
    for piece, out_ref in zip(pieces, outs):
        begin = pl.multiple_of((place_ref[0] ^ piece) * depth, depth)
        out_ref[...] = lax.dot_general(
            residual,
            basis_ref[pl.ds(begin, depth), :],
            (((1,), (1,)), ((), ())),
            preferred_element_type=F32,
        ).astype(out_ref.dtype)


def finish_kernel(pieces, place_ref, r_ref, w_ref, g_ref, const_ref, basis_ref, *refs):
    *sums, residual_ref = refs[: -len(pieces)]
    value = r_ref[...]
    for line in range(4):
        total, place = 0.0, 0
        for sum_ref in sums:
            count = sum_ref.shape[0]
            term = g_ref[line, pl.ds(place, count), :] * sum_ref[...]
            total = total + jnp.sum(term, axis=0, keepdims=True) if count < SUB else total + term
            place += count
            if place == 4 * len(GROUP):
                total = jnp.sum(total, axis=0, keepdims=True)
        value = value - w_ref[line] * total
    scale = const_ref[19, 0:1, :]
    residual = (value * scale).astype(jnp.bfloat16)
    residual_ref[...] = residual
    rotate_back(residual, pieces, place_ref, basis_ref, refs[-len(pieces) :])


def rest_kernel(pieces, place_ref, residual_ref, basis_ref, *outs):
    rotate_back(residual_ref[...], pieces, place_ref, basis_ref, outs)


def exchange(value, axis, count):
    out = [value]
    for step in range(1, count):
        out.append(lax.ppermute(value, axis, [(a, a ^ step) for a in range(count)]))
    return out


def shards(observations, basis, eigvals, lengths, noise):
    steps, depth = observations.shape
    width = basis.shape[1]
    blocks, pieces = lax.axis_size("tm"), lax.axis_size("mode")
    me = lax.axis_index("tm").astype(jnp.int32).reshape(1)
    place = lax.axis_index("mode").astype(jnp.int32).reshape(1)
    rounds = blocks.bit_length() - 1
    vmem = pl.BlockSpec(memory_space=pltpu.VMEM)
    smem = pl.BlockSpec(memory_space=pltpu.SMEM)
    params = pltpu.CompilerParams(vmem_limit_bytes=VMEM_LIMIT)

    def shape(*dims, dtype=F32):
        return jax.ShapeDtypeStruct(dims, dtype)

    obs = exchange(observations, "mode", pieces)
    const, w, merges, basis, obs[0] = pl.pallas_call(
        functools.partial(coefficients_kernel, blocks),
        out_shape=(
            shape(20, SUB, width),
            shape(4, steps, width),
            shape(-(-(7 * rounds + 6) // SUB) * SUB, width),
            shape(*basis.shape, dtype=basis.dtype),
            shape(steps, depth, dtype=observations.dtype),
        ),
        in_specs=[smem] + [pl.BlockSpec(memory_space=pltpu.HBM)] * 4,
        out_specs=(vmem,) * 5,
        scratch_shapes=[
            pltpu.VMEM((1, width), F32),
            pltpu.VMEM((1, width), F32),
            pltpu.SemaphoreType.DMA((4,)),
        ],
        compiler_params=params,
        cost_estimate=pl.CostEstimate(flops=20000000, bytes_accessed=2000000, transcendentals=0),
        name="coefficients",
    )(
        noise,
        *(
            pltpu.with_memory_space_constraint(x, pltpu.HBM)
            for x in (
                eigvals.reshape(1, width),
                lengths.reshape(1, width),
                observations,
                basis,
            )
        ),
    )
    last = pieces - 1
    z = ()
    for stage, group in enumerate(([0], list(range(last - 1, 0, -1)))):
        z = pl.pallas_call(
            functools.partial(rotate_kernel, (group, stage)),
            out_shape=shape(steps, width),
            in_specs=[smem] + [vmem] * (len(group) + 1 + len(z)),
            out_specs=vmem,
            compiler_params=params,
            name="rotate_early",
        )(place, *(obs[piece] for piece in group), basis, *z)
        z = (z,)
    z, summary = pl.pallas_call(
        functools.partial(rotate_kernel, ([last], 2)),
        out_shape=(shape(steps, width), shape(4, width)),
        in_specs=[smem] + [vmem] * 4,
        out_specs=(vmem,) * 2,
        compiler_params=params,
        name="rotate_last",
    )(place, obs[last], basis, *z, w)
    pair = pl.pallas_call(
        pair_kernel,
        out_shape=shape(8, width),
        in_specs=[vmem] * 2,
        out_specs=vmem,
        compiler_params=params,
        name="pair",
    )(summary, lax.ppermute(summary, "tm", [(a, a ^ MIRROR) for a in range(blocks)]))
    sums = [pair]
    for step in NEAR:
        sums.append(lax.ppermute(pair, "tm", [(a, a ^ step) for a in range(blocks)]))
    for level in range(3, rounds):
        summary = pl.pallas_call(
            functools.partial(merge_kernel, level - 1),
            out_shape=shape(4, width),
            in_specs=[smem] + [vmem] * (5 if level == 3 else 3),
            out_specs=vmem,
            compiler_params=params,
            name="merge",
        )(me, merges, *(sums if level == 3 else (summary, sums[-1])))
        step = 1 << level
        sums.append(lax.ppermute(summary, "tm", [(a, a ^ step) for a in range(blocks)]))
    local, g = pl.pallas_call(
        functools.partial(local_kernel, blocks),
        out_shape=(shape(steps, width), shape(4, -(-4 * (rounds + 5) // SUB) * SUB, width)),
        in_specs=[smem] + [vmem] * 3,
        out_specs=(vmem,) * 2,
        scratch_shapes=[pltpu.VMEM((width // 128, steps, 128), F32)],
        compiler_params=params,
        cost_estimate=pl.CostEstimate(flops=10000000, bytes_accessed=1000000, transcendentals=0),
        name="local",
    )(me, z, const, merges)
    residual, part_y, part_d = pl.pallas_call(
        functools.partial(finish_kernel, [2, 3]),
        out_shape=(shape(steps, width, dtype=jnp.bfloat16),)
        + (shape(steps, depth, dtype=jnp.bfloat16),) * 2,
        in_specs=[smem] + [vmem] * (5 + len(sums)),
        out_specs=(vmem,) * 3,
        compiler_params=params,
        name="finish",
    )(place, local, w, g, const, basis, *sums)
    from_y, from_d = (
        lax.ppermute(part, "mode", [(a, a ^ piece) for a in range(pieces)])
        for piece, part in ((2, part_y), (3, part_d))
    )
    own, part_m = pl.pallas_call(
        functools.partial(rest_kernel, [0, 1]),
        out_shape=(shape(steps, depth), shape(steps, depth, dtype=jnp.bfloat16)),
        in_specs=[smem] + [vmem] * 2,
        out_specs=(vmem,) * 2,
        compiler_params=params,
        name="rest",
    )(place, residual, basis)
    from_m = lax.ppermute(part_m, "mode", [(a, a ^ 1) for a in range(pieces)])
    own, from_y, from_d, from_m = (v.astype(F32) for v in (own, from_y, from_d, from_m))
    return (own + from_m) + (from_d + from_y)


def solution(mesh):
    placed = (P("tm", "mode"), P(None, "mode"), P("mode"), P("mode"), P())
    return jax.shard_map(
        shards, mesh=mesh, in_specs=placed, out_specs=P("tm", "mode"), check_vma=False
    )
```
